32 devices in a mesh: row: 8 (over y, x, core), col: 4 (over z).
Axes of the slice: x: 2, y: 2, z: 4, core: 2. Of those that a mesh axis runs over, the one named last changes fastest.
Arguments:
- token_ids: int32 [8192], P('row'), may hold values from 0 to 31999
- target_ids: int32 [1024], P('row'), may hold values from 0 to 31999
- loss_slots: int32 [1024], P('row'), may hold values from 0 to 1023
- valid_mask: int32 [1024], replicated, may hold values 0 or 1
- prefix_lens: int32 [8], replicated, may hold values from 0 to 1023
- embed_table: float32 [32000, 1152], P('col', 'row'), may hold values from -0.375 to 0.375
- norm_gains: float32 [3, 1152], replicated, may hold values from 0.5 to 1.5
- qkv_weight: float32 [1152, 1920], P('row', 'col'), may hold values from -0.1875 to 0.1875
- output_weight: float32 [1152, 1152], P('row', 'col'), may hold values from -3 to 3
- mlp_weight: float32 [3, 1152, 3072], P(None, 'row', 'col'), may hold values from -0.1875 to 0.1875
- embed_mean: float32 [32000, 1152], P('col', 'row'), may hold values from -0.05 to 0.05
- embed_square: float32 [32000, 1152], P('col', 'row'), may hold values from 2e-05 to 0.0002
- gain_mean: float32 [3, 1152], replicated, may hold values from -0.05 to 0.05
- gain_square: float32 [3, 1152], replicated, may hold values from 2e-05 to 0.0002
- qkv_mean: float32 [1152, 1920], P('row', 'col'), may hold values from -0.05 to 0.05
- qkv_square: float32 [1152, 1920], P('row', 'col'), may hold values from 2e-05 to 0.0002
- out_mean: float32 [1152, 1152], P('row', 'col'), may hold values from -0.00390625 to 0.00390625
- out_square: float32 [1152, 1152], P('row', 'col'), may hold values from 9.765625e-08 to 9.765625e-07
- mlp_mean: float32 [3, 1152, 3072], P(None, 'row', 'col'), may hold values from -0.01953125 to 0.01953125
- mlp_square: float32 [3, 1152, 3072], P(None, 'row', 'col'), may hold values from 1.953125e-06 to 1.953125e-05
- left_bases: float32 [5, 1152, 1152], P(None, 'row'), may hold values from -0.1875 to 0.1875
- qkv_bases: float32 [1920, 1920], P('col'), may hold values from -0.125 to 0.125
- out_bases: float32 [1152, 1152], P('col'), may hold values from -0.1875 to 0.1875
- feedforward_bases: float32 [3, 3072, 3072], P(None, 'col'), may hold values from -0.109375 to 0.109375
Outputs:
- loss_value: float32 [], replicated
- embed_next: float32 [32000, 1152], P('col', 'row')
- embed_moment: float32 [32000, 1152], P('col', 'row')
- embed_scale: float32 [32000, 1152], P('col', 'row')
- gain_update: float32 [3, 1152], replicated
- gain_moment: float32 [3, 1152], replicated
- gain_scale: float32 [3, 1152], replicated
- qkv_next: float32 [1152, 1920], P('row', 'col')
- qkv_moment: float32 [1152, 1920], P('row', 'col')
- qkv_scale: float32 [1152, 1920], P('row', 'col')
- out_update: float32 [1152, 1152], P('row', 'col')
- out_moment: float32 [1152, 1152], P('row', 'col')
- out_scale: float32 [1152, 1152], P('row', 'col')
- mlp_next: float32 [3, 1152, 3072], P(None, 'row', 'col')
- mlp_moment: float32 [3, 1152, 3072], P(None, 'row', 'col')
- mlp_scale: float32 [3, 1152, 3072], P(None, 'row', 'col')
The draws below stay inside these ranges and needn't reach their ends.
All inputs are finite; a program needn't handle non-finite values.
Results may differ from the reference program's by a relative error of at most 0.018.
Values may be sent and summed in bfloat16 or wider, within the bound.
A program may use at most 320 MiB of HBM per device.

```python
import math
import jax
import jax.numpy as jnp
import numpy as np
from jax import lax

D = 1152
Q_HEADS = 18
KV_HEADS = 6
HEAD = 64
FF = 3072
VOCAB = 32000
LEN = 1024
PICK = 128
SEQS = 8
TOKENS = 8192
PICKS = 1024
QKV = 1920
QH = 1152


def with_ends(array, own_key, smallest, top_value):
    longest = array.shape.index(max(array.shape))
    spots = []
    for shift in (0, 1):
        where = [jax.random.randint(jax.random.fold_in(own_key, axis), (), 0, length) for axis, length in enumerate(array.shape)]
        where[longest] = (where[longest] + shift) % array.shape[longest]
        spots.append(tuple(where))
    return array.at[spots[0]].set(smallest).at[spots[1]].set(top_value)


def block_levels(key, dims, pieces, smallest, top_value):
    level = 1.0
    for position, parts in pieces:
        steps = jax.random.uniform(jax.random.fold_in(jax.random.fold_in(key, 6), position), (parts,), jnp.float32, smallest / len(pieces), top_value / len(pieces))
        level = level * jnp.repeat(jnp.exp(steps), dims[position] // parts).reshape((-1,) + (1,) * (len(dims) - 1 - position))
    return level


def rank_bounds(number_of, slope):
    portions = [(1 << 20) // math.isqrt(grade ** slope) + 1 for grade in range(1, number_of + 1)]
    width = 1 + sum(portions) // (1 << 30)
    return np.cumsum(np.array([max(1, weight // width) for weight in portions]))


def skewed_ids(own_key, shape, amount, slope):
    listing = rank_bounds(amount, slope)
    pick = jax.random.randint(jax.random.fold_in(own_key, 1), shape, 0, int(listing[amount - 1]))
    grade = jnp.searchsorted(jnp.asarray(listing, jnp.int32), pick, side="right")
    return jax.random.permutation(jax.random.fold_in(own_key, 2), amount)[grade].astype(jnp.int32)


def noise(stream_key, extent, deviation, most, cuts=(), kind=jnp.bfloat16):
    values = jax.random.normal(stream_key, extent, jnp.float32) * deviation
    if len(cuts) > 0:
        values = block_levels(stream_key, extent, cuts, -0.22, 0.18) * values
    return jnp.clip(values, min=-most, max=most).astype(kind)


def setup_inputs(seed: int = 0) -> dict:
    splits = jax.random.split(jax.random.key(seed), 25)
    token_ids = with_ends(skewed_ids(splits[0], (TOKENS,), VOCAB, 2), jax.random.fold_in(splits[0], 3), 0, VOCAB - 1).astype(jnp.int32)
    target_ids = with_ends(skewed_ids(splits[1], (PICKS,), VOCAB, 2), jax.random.fold_in(splits[1], 3), 0, VOCAB - 1).astype(jnp.int32)
    loss_slots = with_ends(jax.random.randint(splits[2], (PICKS,), 0, LEN), jax.random.fold_in(splits[2], 1), 0, LEN - 1).astype(jnp.int32)
    valid_mask = with_ends((jax.random.randint(splits[3], (PICKS,), 0, 4) < 3).astype(jnp.int32), jax.random.fold_in(splits[3], 1), 0, 1)
    prefix_lens = with_ends(jax.random.randint(splits[4], (SEQS,), 0, LEN), jax.random.fold_in(splits[4], 1), 0, LEN - 1).astype(jnp.int32)
    embed_table = noise(splits[5], (VOCAB, D), (D // 4) ** -0.5, 0.375, ((0, 4), (1, 8)), jnp.float32)
    norm_gains = jnp.clip(1.0 + 0.1 * jax.random.normal(splits[6], (3, D), jnp.float32), 0.5, 1.5)
    qkv_weight = noise(splits[7], (D, QKV), D ** -0.5, 0.1875, ((0, 8), (1, 4)), jnp.float32)
    output_weight = noise(splits[8], (D, QH), (max(QH // 256, 1)) ** -0.5, 3.0, ((0, 8), (1, 4)), jnp.float32)
    mlp_weight = noise(splits[9], (3, D, FF), D ** -0.5, 0.1875, ((1, 8), (2, 4)), jnp.float32)
    embed_mean = noise(splits[10], (VOCAB, D), 0.008, 0.05, ((0, 4), (1, 8)), jnp.float32)
    embed_square = jnp.clip(jnp.exp(math.log(0.0002) - 2.3025851 * jax.random.uniform(splits[11], (VOCAB, D), jnp.float32) ** block_levels(splits[11], (VOCAB, D), ((0, 4), (1, 8)), -0.2, 0.2)), 1.9999999494757503e-05, 0.0002)
    gain_mean = noise(splits[12], (3, D), 0.008, 0.05, (), jnp.float32)
    gain_square = jnp.clip(jnp.exp(jax.random.uniform(splits[13], (3, D), jnp.float32, math.log(1.9999999494757503e-05), math.log(0.0002))), 1.9999999494757503e-05, 0.0002)
    qkv_mean = noise(splits[14], (D, QKV), 0.008, 0.05, ((0, 8), (1, 4)), jnp.float32)
    qkv_square = jnp.clip(jnp.exp(math.log(0.0002) - 2.3025851 * jax.random.uniform(splits[15], (D, QKV), jnp.float32) ** block_levels(splits[15], (D, QKV), ((0, 8), (1, 4)), -0.2, 0.2)), 1.9999999494757503e-05, 0.0002)
    out_mean = noise(splits[16], (D, QH), (0.02 * (SEQS * PICK) ** -0.5), 0.00390625, ((0, 8), (1, 4)), jnp.float32)
    out_square = jnp.clip(jnp.exp(math.log(9.765625463842298e-07) - 2.3025852 * jax.random.uniform(splits[17], (D, QH), jnp.float32) ** block_levels(splits[17], (D, QH), ((0, 8), (1, 4)), -0.2, 0.2)), 9.765624753299562e-08, 9.765625463842298e-07)
    mlp_mean = noise(splits[18], (3, D, FF), (0.1 * (SEQS * PICK) ** -0.5), 0.01953125, ((1, 8), (2, 4)), jnp.float32)
    mlp_square = jnp.clip(jnp.exp(math.log(1.9531249563442543e-05) - 2.30258502 * jax.random.uniform(splits[19], (3, D, FF), jnp.float32) ** block_levels(splits[19], (3, D, FF), ((1, 8), (2, 4)), -0.2, 0.2)), 1.9531250927684596e-06, 1.9531249563442543e-05)
    left_bases = noise(splits[20], (5, D, D), D ** -0.5, 0.1875, ((1, 8),), jnp.float32)
    qkv_bases = noise(splits[21], (QKV, QKV), QKV ** -0.5, 0.125, ((0, 4),), jnp.float32)
    out_bases = noise(splits[22], (QH, QH), QH ** -0.5, 0.1875, ((0, 4),), jnp.float32)
    feedforward_bases = noise(splits[23], (3, FF, FF), FF ** -0.5, 0.109375, ((1, 4),), jnp.float32)
    return {"token_ids": token_ids, "target_ids": target_ids, "loss_slots": loss_slots, "valid_mask": valid_mask, "prefix_lens": prefix_lens, "embed_table": embed_table, "norm_gains": norm_gains, "qkv_weight": qkv_weight, "output_weight": output_weight, "mlp_weight": mlp_weight, "embed_mean": embed_mean, "embed_square": embed_square, "gain_mean": gain_mean, "gain_square": gain_square, "qkv_mean": qkv_mean, "qkv_square": qkv_square, "out_mean": out_mean, "out_square": out_square, "mlp_mean": mlp_mean, "mlp_square": mlp_square, "left_bases": left_bases, "qkv_bases": qkv_bases, "out_bases": out_bases, "feedforward_bases": feedforward_bases}


NORM_EPSILON = 1e-05
ADAM_EPSILON = 1e-08
MOMENT_BETA = 0.5
SOAP_RATE = 0.05
ADAM_RATE = 0.01
WEIGHT_DECAY = 0.1
MASK_VALUE = -1e+30
FULL_PRECISION = lax.Precision.HIGHEST

@jax.custom_vjp
def low(v):
    return lax.optimization_barrier(v.astype(jnp.bfloat16)).astype(jnp.float32)

@jax.custom_vjp
def low_back(v):
    return v

def low_keep(v):
    return (low(v), None)

def low_pass(kept, grad):
    return (grad,)

def back_keep(v):
    return (v, None)

def back_low(kept, grad):
    return (low(grad),)
low.defvjp(low_keep, low_pass)
low_back.defvjp(back_keep, back_low)

def matmul(left_op, right_op):
    return jnp.dot(left_op, right_op, precision=FULL_PRECISION, preferred_element_type=jnp.float32)

def matmul_last(left_op, right_op):
    return lax.dot_general(left_op, right_op, (((1,), (1,)), ((), ())), precision=FULL_PRECISION, preferred_element_type=jnp.float32)

def rms_norm(values, gain_vec):
    return values * lax.rsqrt(lax.optimization_barrier(jnp.mean(values * values, axis=-1, keepdims=True)) + NORM_EPSILON) * gain_vec

def rotary(values, positions):
    half_width = values.shape[-1] // 2
    frequency = jnp.power(10000.0, -jnp.arange(half_width, dtype=jnp.float32) / half_width)
    angles = positions[:, None].astype(jnp.float32) * frequency[None, :]
    cosine = jnp.cos(angles)[:, None, :]
    sine_part = jnp.sin(angles)[:, None, :]
    first_half = values[..., :half_width]
    second_half = values[..., half_width:]
    return jnp.concatenate([first_half * cosine - second_half * sine_part, second_half * cosine + first_half * sine_part], axis=-1)

def layer_loss(embed_table, norm_gains, qkv_weight, output_weight, mlp_weight, token_ids, target_ids, loss_slots, valid_mask, prefix_lens):
    table_low = low(embed_table)
    qkv_low = low(qkv_weight)
    out_low = low(output_weight)
    mlp_low = low(mlp_weight)
    valid_count = jnp.maximum(jnp.sum(valid_mask).astype(jnp.float32), 1.0)
    positions = jnp.arange(LEN, dtype=jnp.int32)
    causal = positions[None, :] <= positions[:, None]
    group_size = Q_HEADS // KV_HEADS
    query_width = Q_HEADS * HEAD
    kv_width = KV_HEADS * HEAD
    scaling = HEAD ** (-0.5)

    def sequence_loss(carried, inputs):
        seq_ids, seq_targets, seq_slots, seq_valid, seq_prefix = inputs
        embedded = low_back(jnp.take(table_low, seq_ids, axis=0))
        normed = low(rms_norm(embedded, norm_gains[0]))
        project = low(low_back(matmul(normed, qkv_low)))
        queries_raw = project[:, :query_width].reshape(LEN, Q_HEADS, HEAD)
        keys_raw = project[:, query_width:query_width + kv_width].reshape(LEN, KV_HEADS, HEAD)
        attn_values = project[:, query_width + kv_width:].reshape(LEN, KV_HEADS, HEAD)
        queries = low(rotary(queries_raw, positions)).reshape(LEN, KV_HEADS, group_size, HEAD)
        attn_keys = low(rotary(keys_raw, positions))
        raw_scores = jnp.einsum('qhgd,khd->hgqk', queries, attn_keys, precision=FULL_PRECISION) * scaling
        allowed = causal | (positions[None, :] < seq_prefix)
        scores = low_back(jnp.where(allowed, raw_scores, MASK_VALUE))
        attn_probs = jax.nn.softmax(scores, axis=-1)
        attended = jnp.einsum('hgqk,khd->qhgd', low(attn_probs), attn_values, precision=FULL_PRECISION).reshape(LEN, query_width)
        attended = low(low_back(attended))
        hidden_one = embedded + low_back(matmul_last(attended, out_low))
        middle = low(rms_norm(hidden_one, norm_gains[1]))
        gate_part = low_back(matmul(middle, mlp_low[0]))
        upward = low_back(matmul(middle, mlp_low[1]))
        inner_act = low(jax.nn.silu(gate_part) * upward)
        hidden_two = hidden_one + low_back(matmul_last(inner_act, mlp_low[2]))
        final = low(rms_norm(hidden_two, norm_gains[2]))
        final_pick = jnp.take(final, seq_slots.astype(jnp.int32), axis=0)
        logits = low_back(matmul_last(final_pick, table_low))
        log_total = jax.nn.logsumexp(logits, axis=-1)
        picked = jnp.take_along_axis(logits, seq_targets[:, None].astype(jnp.int32), axis=1)[:, 0]
        return (carried + jnp.sum(seq_valid.astype(jnp.float32) * (log_total - picked)), None)
    inputs = (token_ids.reshape(SEQS, LEN), target_ids.reshape(SEQS, PICK), loss_slots.reshape(SEQS, PICK), valid_mask.reshape(SEQS, PICK), prefix_lens)
    summed, unused = lax.scan(jax.checkpoint(sequence_loss), jnp.zeros((), jnp.float32), inputs)
    return summed / valid_count

def soap_update(weight, gradient_value, moment, square_avg, left_basis, right_basis):
    rotated = matmul(matmul(left_basis.T, gradient_value), right_basis)
    moment_new = MOMENT_BETA * moment + (1.0 - MOMENT_BETA) * rotated
    square_new = MOMENT_BETA * square_avg + (1.0 - MOMENT_BETA) * rotated * rotated
    normalized = moment_new / (jnp.sqrt(square_new) + ADAM_EPSILON)
    update = matmul(matmul(left_basis, normalized), right_basis.T)
    return (-(SOAP_RATE * (update + WEIGHT_DECAY * weight)), moment_new, square_new)

def adam_update(weight, gradient_value, moment, square_avg, decay_rate):
    moment_new = MOMENT_BETA * moment + (1.0 - MOMENT_BETA) * gradient_value
    square_new = MOMENT_BETA * square_avg + (1.0 - MOMENT_BETA) * gradient_value * gradient_value
    change = -(ADAM_RATE * (moment_new / (jnp.sqrt(square_new) + ADAM_EPSILON) + decay_rate * weight))
    return (change, moment_new, square_new)

def reference(token_ids, target_ids, loss_slots, valid_mask, prefix_lens, embed_table, norm_gains, qkv_weight, output_weight, mlp_weight, embed_mean, embed_square, gain_mean, gain_square, qkv_mean, qkv_square, out_mean, out_square, mlp_mean, mlp_square, left_bases, qkv_bases, out_bases, feedforward_bases):

    def objective(table_arg, gains_arg, qkv_matrix, out_matrix, mlp_matrix):
        return layer_loss(table_arg, gains_arg, qkv_matrix, out_matrix, mlp_matrix, token_ids, target_ids, loss_slots, valid_mask, prefix_lens)
    loss_value, pull_back = jax.vjp(objective, embed_table, norm_gains, qkv_weight, output_weight, mlp_weight)
    grad_table, grad_gains, grad_qkv, grad_out, grad_mlp = pull_back(jnp.ones((), jnp.float32))
    embed_change, embed_moment, embed_scale = adam_update(embed_table, grad_table, embed_mean, embed_square, WEIGHT_DECAY)
    embed_next = embed_table + embed_change
    gain_update, gain_moment, gain_scale = adam_update(norm_gains, grad_gains, gain_mean, gain_square, 0.0)
    qkv_change, qkv_moment, qkv_scale = soap_update(qkv_weight, grad_qkv, qkv_mean, qkv_square, left_bases[0], qkv_bases)
    qkv_next = qkv_weight + qkv_change
    out_update, out_moment, out_scale = soap_update(output_weight, grad_out, out_mean, out_square, left_bases[1], out_bases)
    results = [soap_update(mlp_weight[matrix_index], grad_mlp[matrix_index], mlp_mean[matrix_index], mlp_square[matrix_index], left_bases[2 + matrix_index], feedforward_bases[matrix_index]) for matrix_index in range(3)]
    mlp_next = mlp_weight + jnp.stack([entry[0] for entry in results])
    mlp_moment = jnp.stack([entry[1] for entry in results])
    mlp_scale = jnp.stack([entry[2] for entry in results])
    return (loss_value, embed_next, embed_moment, embed_scale, gain_update, gain_moment, gain_scale, qkv_next, qkv_moment, qkv_scale, out_update, out_moment, out_scale, mlp_next, mlp_moment, mlp_scale)
```

```python
import jax
import jax.numpy as jnp
from jax import lax
from jax.sharding import PartitionSpec as P

Q_HEADS = 18
KV_HEADS = 6
HEAD = 64
LEN = 1024
PICK = 128


NORM_EPSILON = 1e-05
ADAM_EPSILON = 1e-08
MOMENT_BETA = 0.5
SOAP_RATE = 0.05
ADAM_RATE = 0.01
WEIGHT_DECAY = 0.1
MASK_VALUE = -1e30


def send(value, axis, shift):
    count = lax.axis_size(axis)
    return lax.ppermute(value, axis, [(k, (k + shift) % count) for k in range(count)])


def collect(value, axis):
    return [value] + [send(value, axis, k) for k in range(1, lax.axis_size(axis))]


def deliver(pieces, axis, sign):
    return [pieces[0]] + [send(pieces[k], axis, sign * k) for k in range(1, len(pieces))]


def summed(pieces):
    total = pieces[0].astype(jnp.float32)
    for piece in pieces[1:]:
        total = total + piece.astype(jnp.float32)
    return total


def to_absolute(pieces, index):
    count = len(pieces)
    order = [pieces[0]] + [pieces[count - k] for k in range(1, count)]
    return jnp.roll(jnp.stack(order), index, axis=0)


def pick_block(values, index, axis):
    return lax.dynamic_index_in_dim(values, index, axis, keepdims=False)


def rms_norm(values, gain_vec):
    return (
        values
        * lax.rsqrt(jnp.mean(values * values, axis=-1, keepdims=True) + NORM_EPSILON)
        * gain_vec
    )


def rotary(values, positions):
    half_width = values.shape[-1] // 2
    frequency = jnp.power(10000.0, -jnp.arange(half_width, dtype=jnp.float32) / half_width)
    angles = positions[:, None].astype(jnp.float32) * frequency[None, :]
    cosine = jnp.cos(angles)[:, None, :]
    sine_part = jnp.sin(angles)[:, None, :]
    first_half = values[..., :half_width]
    second_half = values[..., half_width:]
    return jnp.concatenate(
        [
            first_half * cosine - second_half * sine_part,
            second_half * cosine + first_half * sine_part,
        ],
        axis=-1,
    )


def swiglu(gate_part, upward):
    return jax.nn.silu(gate_part) * upward


def matmul(left_op, right_op):
    return jnp.dot(left_op, right_op, preferred_element_type=jnp.float32)


def matmul_last(left_op, right_op):
    return lax.dot_general(
        left_op, right_op, (((1,), (1,)), ((), ())), preferred_element_type=jnp.float32
    )


def matmul_first(left_op, right_op):
    return lax.dot_general(
        left_op, right_op, (((0,), (0,)), ((), ())), preferred_element_type=jnp.float32
    )


def norm_back(values, gain_vec, grad_output):
    unused, pull_back = jax.vjp(rms_norm, values, gain_vec)
    return pull_back(grad_output)


def moments(rotated, moment, square_avg):
    moment_new = MOMENT_BETA * moment + (1.0 - MOMENT_BETA) * rotated
    square_new = MOMENT_BETA * square_avg + (1.0 - MOMENT_BETA) * rotated * rotated
    return (moment_new, square_new, moment_new / (jnp.sqrt(square_new) + ADAM_EPSILON))


def adam_update(weight, gradient_value, moment, square_avg, decay_rate):
    moment_new = MOMENT_BETA * moment + (1.0 - MOMENT_BETA) * gradient_value
    square_new = MOMENT_BETA * square_avg + (1.0 - MOMENT_BETA) * gradient_value * gradient_value
    change = -(
        ADAM_RATE * (moment_new / (jnp.sqrt(square_new) + ADAM_EPSILON) + decay_rate * weight)
    )
    return (change, moment_new, square_new)


def per_device(
    token_ids,
    target_ids,
    loss_slots,
    valid_mask,
    prefix_lens,
    embed_table,
    norm_gains,
    qkv_weight,
    output_weight,
    mlp_weight,
    embed_mean,
    embed_square,
    gain_mean,
    gain_square,
    qkv_mean,
    qkv_square,
    out_mean,
    out_square,
    mlp_mean,
    mlp_square,
    left_bases,
    qkv_bases,
    out_bases,
    feedforward_bases,
):
    row_index = lax.axis_index("row")
    col_index = lax.axis_index("col")
    row_count = lax.axis_size("row")
    col_count = lax.axis_size("col")
    low = jnp.bfloat16
    group_tokens = token_ids.shape[0]
    pick_count = loss_slots.shape[0]
    device_tokens = group_tokens // col_count
    vocab_shard, features = embed_table.shape
    width = features * row_count
    query_width = Q_HEADS * HEAD
    kv_width = KV_HEADS * HEAD
    group_size = Q_HEADS // KV_HEADS
    scaling = HEAD ** (-0.5)
    qkv_cols, out_cols, ff_cols = qkv_weight.shape[1], output_weight.shape[1], mlp_weight.shape[2]
    vocab_part = vocab_shard // row_count

    ids_all = lax.all_gather(jnp.concatenate([token_ids, target_ids]), "row", axis=0)
    tokens_all = ids_all[:, :group_tokens].reshape(row_count, col_count, device_tokens)
    targets_all = ids_all[:, group_tokens:].reshape(row_count * pick_count)
    local_tokens = tokens_all - col_index * vocab_shard
    vocab_line = jnp.arange(vocab_shard, dtype=jnp.int32)

    table_low_t = embed_table.astype(low).T
    attn_block = jnp.concatenate(
        collect(qkv_weight.astype(low), "col") + collect(output_weight.astype(low), "col"), axis=1
    )
    attn_full = lax.all_gather(attn_block, "row", axis=0, tiled=True)
    mlp_low = mlp_weight.astype(low)
    mlp_block = jnp.concatenate(
        collect(mlp_low[0], "col") + collect(mlp_low[1], "col") + collect(mlp_low[2], "col"), axis=1
    )
    mlp_full = lax.all_gather(mlp_block, "row", axis=0, tiled=True)
    bases_low = left_bases.astype(low)
    left_full = lax.all_gather(
        jnp.concatenate([bases_low[k] for k in range(5)], axis=1), "row", axis=0, tiled=True
    )
    qkv_width, out_width, ff_width = (
        qkv_cols * col_count,
        out_cols * col_count,
        ff_cols * col_count,
    )
    qkv_full, out_full = attn_full[:, :qkv_width], attn_full[:, qkv_width:]
    gate_full, up_full, down_full = (
        mlp_full[:, k * ff_width : (k + 1) * ff_width] for k in range(3)
    )

    def rotate_left(values, k):
        return matmul(values, left_full[:, k * width : (k + 1) * width]).astype(low)

    def absolute_columns(values):
        count = values.shape[1] // col_count
        parts = [values[:, k * count : (k + 1) * count] for k in range(col_count)]
        stacked = to_absolute(parts, col_index)
        return jnp.moveaxis(stacked, 0, 1).reshape(values.shape)

    def relative_columns(values):
        count = values.shape[1] // col_count
        stacked = jnp.moveaxis(values.reshape(values.shape[0], col_count, count), 1, 0)
        turned = jnp.roll(stacked, -col_index, axis=0)
        order = [turned[0]] + [turned[col_count - k] for k in range(1, col_count)]
        return jnp.concatenate(order, axis=1)

    table_parts = jnp.moveaxis(table_low_t.reshape(features, row_count, vocab_part), 1, 0)
    part_pieces = [
        pick_block(table_parts, (row_index + k) % row_count, 0) for k in range(row_count)
    ]
    table_part = to_absolute(deliver(part_pieces, "row", 1), row_index).reshape(width, vocab_part)

    def chosen(k):
        return pick_block(local_tokens, (col_index + k) % col_count, 1).reshape(-1)

    def one_hot(ids):
        return (ids[:, None] == vocab_line[None, :]).astype(low)

    looked = [
        matmul_last(one_hot(chosen(k)), table_low_t).astype(low) for k in range(col_count)
    ]
    found = summed(deliver(looked, "col", 1)).astype(low)
    embedded = lax.all_to_all(found, "row", split_axis=0, concat_axis=1, tiled=True).astype(
        jnp.float32
    )

    normed = rms_norm(embedded, norm_gains[0]).astype(low)
    project = absolute_columns(matmul(normed, qkv_full).astype(low))
    first_token = col_index * device_tokens
    positions = first_token + jnp.arange(device_tokens, dtype=jnp.int32)
    seq_prefix = jnp.sum(
        jnp.where(jnp.arange(prefix_lens.shape[0], dtype=jnp.int32) == row_index, prefix_lens, 0)
    )

    def rotate_here(values):
        return rotary(values, positions)

    queries_raw = project[:, :query_width].astype(jnp.float32).reshape(device_tokens, Q_HEADS, HEAD)
    keys_raw = (
        project[:, query_width : query_width + kv_width]
        .astype(jnp.float32)
        .reshape(device_tokens, KV_HEADS, HEAD)
    )
    queries = rotate_here(queries_raw).astype(low).reshape(device_tokens, KV_HEADS, group_size, HEAD)
    keys_local = rotate_here(keys_raw).astype(low).reshape(device_tokens, kv_width)
    keys_values = jnp.concatenate(
        collect(
            jnp.concatenate([keys_local, project[:, query_width + kv_width :]], axis=1), "col"
        ),
        axis=0,
    )
    attn_keys = keys_values[:, :kv_width].reshape(LEN, KV_HEADS, HEAD)
    attn_values = keys_values[:, kv_width:].reshape(LEN, KV_HEADS, HEAD)
    key_blocks = (col_index - jnp.arange(col_count, dtype=jnp.int32)) % col_count
    key_positions = (
        key_blocks[:, None] * device_tokens + jnp.arange(device_tokens, dtype=jnp.int32)[None, :]
    ).reshape(LEN)
    allowed = (key_positions[None, :] <= positions[:, None]) | (key_positions[None, :] < seq_prefix)

    raw_scores = (
        jnp.einsum("qhgd,khd->hgqk", queries, attn_keys, preferred_element_type=jnp.float32)
        * scaling
    )
    scores = jnp.where(allowed, raw_scores, MASK_VALUE)
    largest = jnp.max(scores, axis=-1, keepdims=True)
    weights = jnp.exp(scores - largest)
    attn_probs = weights / jnp.sum(weights, axis=-1, keepdims=True)
    attended = (
        jnp.einsum(
            "hgqk,khd->qhgd",
            attn_probs.astype(low),
            attn_values,
            preferred_element_type=jnp.float32,
        )
        .astype(low)
        .reshape(device_tokens, query_width)
    )
    attended = relative_columns(attended)
    hidden_one = embedded + matmul_last(attended, out_full)
    middle = rms_norm(hidden_one, norm_gains[1]).astype(low)
    gate_part = matmul(middle, gate_full)
    upward = matmul(middle, up_full)
    inner_act = swiglu(gate_part, upward).astype(low)
    hidden_two = hidden_one + matmul_last(inner_act, down_full)
    final = rms_norm(hidden_two, norm_gains[2]).astype(low)

    pick_hit = (loss_slots[:, None] == positions[None, :]).astype(low)
    final_here = matmul(pick_hit, final).astype(low)
    final_seq = lax.psum(final_here, "col")
    final_pick = lax.all_gather(final_seq, "row", axis=0, tiled=True)
    logits = matmul(final_pick, table_part)
    local_max = jnp.max(logits, axis=-1)
    local_sum = jnp.sum(jnp.exp(logits - local_max[:, None]), axis=-1)
    part_first = col_index * vocab_shard + row_index * vocab_part
    target_hit = (
        jnp.arange(vocab_part, dtype=jnp.int32)[None, :] == (targets_all - part_first)[:, None]
    )
    local_target = jnp.sum(jnp.where(target_hit, logits, 0.0), axis=-1)
    everyone = lax.all_gather(
        jnp.stack([local_max, local_sum, local_target]), ("row", "col"), axis=0
    )
    top = jnp.max(everyone[:, 0], axis=0)
    log_total = top + jnp.log(jnp.sum(everyone[:, 1] * jnp.exp(everyone[:, 0] - top), axis=0))
    target_logit = jnp.sum(everyone[:, 2], axis=0)
    valid_count = jnp.maximum(jnp.sum(valid_mask).astype(jnp.float32), 1.0)
    row_weights = valid_mask.astype(jnp.float32) / valid_count
    loss_value = jnp.sum(row_weights * (log_total - target_logit))
    grad_logits = (
        (jnp.exp(logits - log_total[:, None]) - target_hit.astype(jnp.float32))
        * row_weights[:, None]
    ).astype(low)
    grad_pick = matmul_last(grad_logits, table_part).astype(low)
    grad_seq = lax.psum_scatter(grad_pick, "row", scatter_dimension=0, tiled=True)
    grad_seq = lax.psum(grad_seq, "col")
    grad_final = matmul_first(pick_hit, grad_seq)

    table_grad_part = matmul_first(final_pick, grad_logits).astype(low)
    grad_parts = table_grad_part.reshape(row_count, features, vocab_part)
    grad_pieces = [pick_block(grad_parts, (row_index + k) % row_count, 0) for k in range(row_count)]
    table_grad = to_absolute(deliver(grad_pieces, "row", 1), row_index)
    table_grad = jnp.moveaxis(table_grad, 0, 1).reshape(features, vocab_shard).astype(jnp.float32)

    grad_two, gain_two = norm_back(hidden_two, norm_gains[2], grad_final)
    grad_two_low = grad_two.astype(low)
    down_grad = matmul_first(rotate_left(grad_two_low, 4), inner_act).astype(low)
    grad_inner = matmul(grad_two_low, down_full)
    unused, pull_swiglu = jax.vjp(swiglu, gate_part, upward)
    grad_gate, grad_up = pull_swiglu(grad_inner)
    grad_gate = grad_gate.astype(low)
    grad_up = grad_up.astype(low)
    gate_grad = matmul_first(rotate_left(middle, 2), grad_gate).astype(low)
    up_grad = matmul_first(rotate_left(middle, 3), grad_up).astype(low)
    grad_middle = matmul_last(grad_gate, gate_full) + matmul_last(grad_up, up_full)
    grad_middle_in, gain_one = norm_back(hidden_one, norm_gains[1], grad_middle)
    grad_one = grad_two + grad_middle_in
    grad_one_low = grad_one.astype(low)
    out_grad = matmul_first(rotate_left(grad_one_low, 1), attended).astype(low)
    grad_attended = absolute_columns(matmul(grad_one_low, out_full).astype(low)).reshape(
        device_tokens, KV_HEADS, group_size, HEAD
    )
    grad_probs = jnp.einsum(
        "qhgd,khd->hgqk", grad_attended, attn_values, preferred_element_type=jnp.float32
    )
    inner_sum = jnp.sum(attn_probs * grad_probs, axis=-1, keepdims=True)
    grad_scores = (attn_probs * (grad_probs - inner_sum)).astype(low)
    grad_queries = (
        jnp.einsum("hgqk,khd->qhgd", grad_scores, attn_keys, preferred_element_type=jnp.float32)
        * scaling
    )
    grad_keys = (
        jnp.einsum("hgqk,qhgd->khd", grad_scores, queries, preferred_element_type=jnp.float32)
        * scaling
    )
    grad_values = jnp.einsum(
        "hgqk,qhgd->khd",
        attn_probs.astype(low),
        grad_attended,
        preferred_element_type=jnp.float32,
    )
    grad_pairs = (
        jnp.concatenate([grad_keys.reshape(LEN, kv_width), grad_values.reshape(LEN, kv_width)], axis=1)
        .astype(low)
        .reshape(col_count, device_tokens, 2 * kv_width)
    )
    grad_pairs = summed(deliver([grad_pairs[k] for k in range(col_count)], "col", -1))
    unused, pull_query = jax.vjp(rotate_here, queries_raw)
    grad_query_raw = pull_query(grad_queries.reshape(device_tokens, Q_HEADS, HEAD))[0]
    unused, pull_key = jax.vjp(rotate_here, keys_raw)
    grad_key_raw = pull_key(grad_pairs[:, :kv_width].reshape(device_tokens, KV_HEADS, HEAD))[0]
    grad_project = relative_columns(
        jnp.concatenate(
            [
                grad_query_raw.reshape(device_tokens, query_width),
                grad_key_raw.reshape(device_tokens, kv_width),
                grad_pairs[:, kv_width:],
            ],
            axis=1,
        ).astype(low)
    )
    qkv_grad = matmul_first(rotate_left(normed, 0), grad_project).astype(low)
    grad_normed = matmul_last(grad_project, qkv_full)
    grad_embed_in, gain_zero = norm_back(embedded, norm_gains[0], grad_normed)
    grad_embedded = (grad_one + grad_embed_in).astype(low)
    by_feature = lax.all_to_all(grad_embedded, "row", split_axis=1, concat_axis=0, tiled=True)
    for k, piece in enumerate(collect(by_feature, "col")):
        table_grad = table_grad + matmul_first(piece, one_hot(chosen(-k)))
    gain_grads = lax.psum(jnp.stack([gain_zero, gain_one, gain_two]), ("row", "col"))

    def reduce_rows(*parts):
        together = parts[0] if len(parts) == 1 else jnp.concatenate(parts, axis=1)
        return lax.psum_scatter(together, "row", scatter_dimension=0, tiled=True)

    def reduce_cols(values):
        count = values.shape[1] // col_count
        return summed(
            deliver([values[:, k * count : (k + 1) * count] for k in range(col_count)], "col", -1)
        )

    def soap(left_rows, right_basis, weight, moment, square_avg):
        count = weight.shape[1]
        right_low = right_basis.astype(low)
        right = matmul(reduce_cols(left_rows).astype(low), right_low).astype(low)
        pieces = [
            lax.dynamic_slice_in_dim(right, (col_index + k) % col_count * count, count, 1)
            for k in range(col_count)
        ]
        rotated = summed(deliver(pieces, "col", 1))
        moment_new, square_new, step = moments(rotated, moment, square_avg)
        whole = absolute_columns(jnp.concatenate(collect(step.astype(low), "col"), axis=1))
        back = matmul_last(whole, right_low).astype(low)
        return moment_new, square_new, back

    mlp_down_rows = reduce_rows(down_grad)
    mlp_gate_up_rows = reduce_rows(gate_grad, up_grad)
    attn_rows = reduce_rows(out_grad, qkv_grad)
    down_moment, down_scale, down_back = soap(
        mlp_down_rows, feedforward_bases[2], mlp_weight[2], mlp_mean[2], mlp_square[2]
    )
    gate_moment, gate_scale, gate_back = soap(
        mlp_gate_up_rows[:, :ff_width], feedforward_bases[0], mlp_weight[0], mlp_mean[0], mlp_square[0]
    )
    up_moment, up_scale, up_back = soap(
        mlp_gate_up_rows[:, ff_width:], feedforward_bases[1], mlp_weight[1], mlp_mean[1], mlp_square[1]
    )
    out_moment, out_scale, out_back = soap(
        attn_rows[:, :out_width], out_bases, output_weight, out_mean, out_square
    )
    qkv_moment, qkv_scale, qkv_back = soap(
        attn_rows[:, out_width:], qkv_bases, qkv_weight, qkv_mean, qkv_square
    )
    back_mlp = lax.all_gather(
        jnp.concatenate([down_back, gate_back, up_back], axis=1), "row", axis=0, tiled=True
    )
    back_attn = lax.all_gather(
        jnp.concatenate([out_back, qkv_back], axis=1), "row", axis=0, tiled=True
    )
    update_down = matmul(bases_low[4], back_mlp[:, :ff_cols])
    update_gate = matmul(bases_low[2], back_mlp[:, ff_cols : 2 * ff_cols])
    update_up = matmul(bases_low[3], back_mlp[:, 2 * ff_cols :])
    update_out = matmul(bases_low[1], back_attn[:, :out_cols])
    update_qkv = matmul(bases_low[0], back_attn[:, out_cols:])
    update_mlp = jnp.stack([update_gate, update_up, update_down])
    mlp_moment = jnp.stack([gate_moment, up_moment, down_moment])
    mlp_scale = jnp.stack([gate_scale, up_scale, down_scale])
    qkv_next = qkv_weight + -(SOAP_RATE * (update_qkv + WEIGHT_DECAY * qkv_weight))
    out_update = -(SOAP_RATE * (update_out + WEIGHT_DECAY * output_weight))
    mlp_next = mlp_weight + -(SOAP_RATE * (update_mlp + WEIGHT_DECAY * mlp_weight))
    embed_change, embed_moment, embed_scale = adam_update(
        embed_table, table_grad.T, embed_mean, embed_square, WEIGHT_DECAY
    )
    embed_next = embed_table + embed_change
    gain_update, gain_moment, gain_scale = adam_update(
        norm_gains, gain_grads, gain_mean, gain_square, 0.0
    )
    return (
        loss_value,
        embed_next,
        embed_moment,
        embed_scale,
        gain_update,
        gain_moment,
        gain_scale,
        qkv_next,
        qkv_moment,
        qkv_scale,
        out_update,
        out_moment,
        out_scale,
        mlp_next,
        mlp_moment,
        mlp_scale,
    )


def solution(mesh):
    placed = (
        P("row"),
        P("row"),
        P("row"),
        P(),
        P(),
        P("col", "row"),
        P(),
        P("row", "col"),
        P("row", "col"),
        P(None, "row", "col"),
        P("col", "row"),
        P("col", "row"),
        P(),
        P(),
        P("row", "col"),
        P("row", "col"),
        P("row", "col"),
        P("row", "col"),
        P(None, "row", "col"),
        P(None, "row", "col"),
        P(None, "row", None),
        P("col", None),
        P("col", None),
        P(None, "col", None),
    )
    return jax.shard_map(
        per_device,
        mesh=mesh,
        in_specs=placed,
        out_specs=(
            P(),
            P("col", "row"),
            P("col", "row"),
            P("col", "row"),
            P(),
            P(),
            P(),
            P("row", "col"),
            P("row", "col"),
            P("row", "col"),
            P("row", "col"),
            P("row", "col"),
            P("row", "col"),
            P(None, "row", "col"),
            P(None, "row", "col"),
            P(None, "row", "col"),
        ),
        check_vma=False,
    )
```

```python
import functools

import jax
import jax.numpy as jnp
from jax import lax
from jax.experimental import pallas as pl
from jax.experimental.pallas import tpu as pltpu
from jax.sharding import PartitionSpec as P

Q_HEADS = 18
KV_HEADS = 6
HEAD = 64
LEN = 1024
PICK = 128


NORM_EPSILON = 1e-05
ADAM_EPSILON = 1e-08
MOMENT_BETA = 0.5
SOAP_RATE = 0.05
ADAM_RATE = 0.01
WEIGHT_DECAY = 0.1
MASK_VALUE = -1e30
MESH = pl.DeviceIdType.MESH
VMEM_LIMIT = 58 * 2**20
VOCAB_TILE = 1024
LOOK_STEP = 32
SMALL_BLOCK = 384


def greet(peers):
    barrier = pltpu.get_barrier_semaphore()
    for peer in peers:
        pl.semaphore_signal(barrier, inc=1, device_id=peer, device_id_type=MESH)
    pl.semaphore_wait(barrier, len(peers))


def push(source, target, sems, slot, peer):
    copy = pltpu.make_async_remote_copy(
        src_ref=source,
        dst_ref=target,
        send_sem=sems[0].at[slot],
        recv_sem=sems[1].at[slot],
        device_id=peer,
        device_id_type=MESH,
    )
    copy.start()
    return copy


def row_peer(row, col, rows, k):
    half = rows // 2
    if k < half:
        return ((row + 2 * k) % rows, col)
    return ((row // 2 * 2 + 2 * (k - half)) % rows + 1 - row % 2, col)


def share_kernel(rows, cols, x_ref, out_ref, col_send, col_recv, row_send, row_recv):
    row, col = lax.axis_index("row"), lax.axis_index("col")
    col_peers = [(row, (col + k) % cols) for k in range(1, cols)]
    row_peers = [((row + k) % rows, col) for k in range(1, rows)]
    greet(col_peers + row_peers)
    out_ref[row, col] = x_ref[...]
    copies = [
        push(out_ref.at[row, col], out_ref.at[row, col], (col_send, col_recv), k, peer)
        for k, peer in enumerate(col_peers)
    ]
    for copy in copies:
        copy.wait()
    copies = [
        push(out_ref.at[row], out_ref.at[row], (row_send, row_recv), k, peer)
        for k, peer in enumerate(row_peers)
    ]
    for copy in copies:
        copy.wait()


def share(value, collective_id):
    rows, cols = lax.axis_size("row"), lax.axis_size("col")
    return pl.pallas_call(
        functools.partial(share_kernel, rows, cols),
        out_shape=jax.ShapeDtypeStruct((rows, cols, *value.shape), value.dtype),
        in_specs=[pl.BlockSpec(memory_space=pltpu.VMEM)],
        out_specs=pl.BlockSpec(memory_space=pltpu.VMEM),
        scratch_shapes=[
            pltpu.SemaphoreType.DMA((cols - 1,)),
            pltpu.SemaphoreType.DMA((cols - 1,)),
            pltpu.SemaphoreType.DMA((rows - 1,)),
            pltpu.SemaphoreType.DMA((rows - 1,)),
        ],
        compiler_params=pltpu.CompilerParams(
            collective_id=collective_id, has_side_effects=True, vmem_limit_bytes=VMEM_LIMIT
        ),
    )(value)


def spread_kernel(
    rows, cols, x_ref, out_ref, landed, part_send, part_recv, col_send, col_recv,
    row_send, row_recv, core_send, core_recv,
):
    row, col = lax.axis_index("row"), lax.axis_index("col")
    half = rows // 2
    other = row // 2 * 2 + 1 - row % 2
    col_peers = [(row, (col + k) % cols) for k in range(1, cols)]
    row_peers = [((row + 2 * k) % rows, col) for k in range(1, half)]
    greet(col_peers + row_peers + [(other, col)])
    copies = [
        push(x_ref.at[(col + k + 1) % cols], landed.at[k], (part_send, part_recv), k, peer)
        for k, peer in enumerate(col_peers)
    ]
    for copy in copies:
        copy.wait()
    total = x_ref[col].astype(jnp.float32)
    for k in range(cols - 1):
        total = total + landed[k].astype(jnp.float32)
    out_ref[row, col] = total.astype(out_ref.dtype)
    copies = [
        push(out_ref.at[row, col], out_ref.at[row, col], (col_send, col_recv), k, peer)
        for k, peer in enumerate(col_peers)
    ]
    for copy in copies:
        copy.wait()
    across = [
        push(out_ref.at[row], out_ref.at[row], (row_send, row_recv), k, peer)
        for k, peer in enumerate(row_peers)
    ]
    between = [push(out_ref.at[row], out_ref.at[row], (core_send, core_recv), 0, (other, col))]
    for k in range(1, half):
        across[k - 1].wait_recv()
        source = (row + rows - 2 * k) % rows
        between.append(
            push(out_ref.at[source], out_ref.at[source], (core_send, core_recv), k, (other, col))
        )
    for copy in across:
        copy.wait_send()
    for copy in between:
        copy.wait()


def spread(value, collective_id):
    rows, cols = lax.axis_size("row"), lax.axis_size("col")
    count, width = value.shape
    part = count // cols
    dma = pltpu.SemaphoreType.DMA
    out = pl.pallas_call(
        functools.partial(spread_kernel, rows, cols),
        out_shape=jax.ShapeDtypeStruct((rows, cols, part, width), value.dtype),
        in_specs=[pl.BlockSpec(memory_space=pltpu.VMEM)],
        out_specs=pl.BlockSpec(memory_space=pltpu.VMEM),
        scratch_shapes=[pltpu.VMEM((cols - 1, part, width), value.dtype)]
        + [dma((cols - 1,))] * 4
        + [dma((rows // 2 - 1,))] * 2
        + [dma((rows // 2,))] * 2,
        compiler_params=pltpu.CompilerParams(
            collective_id=collective_id, has_side_effects=True, vmem_limit_bytes=VMEM_LIMIT
        ),
    )(value.reshape(cols, part, width))
    return out.reshape(rows * count, width)


def fold_kernel(
    rows, cols, x_ref, out_ref, from_core, to_row, from_row, mine, landed, core_send, core_recv,
    row_send, row_recv, part_send, part_recv, col_send, col_recv,
):
    row, col = lax.axis_index("row"), lax.axis_index("col")
    half = rows // 2
    core = row % 2
    other = row // 2 * 2 + 1 - core
    col_peers = [(row, (col + k) % cols) for k in range(1, cols)]
    row_peers = [((row + 2 * k) % rows, col) for k in range(1, half)]
    greet(col_peers + row_peers + [(other, col)])
    between = [
        push(
            x_ref.at[(row + 2 * k) % rows // 2 * 2 + 1 - core],
            from_core.at[k],
            (core_send, core_recv),
            k,
            (other, col),
        )
        for k in [*range(1, half), 0]
    ]
    across = []
    for k in range(1, half):
        between[k - 1].wait_recv()
        to_row[k - 1] = (
            x_ref[(row + 2 * k) % rows].astype(jnp.float32) + from_core[k].astype(jnp.float32)
        ).astype(to_row.dtype)
        across.append(
            push(to_row.at[k - 1], from_row.at[k - 1], (row_send, row_recv), k - 1, row_peers[k - 1])
        )
    between[half - 1].wait_recv()
    total = x_ref[row].astype(jnp.float32) + from_core[0].astype(jnp.float32)
    for k in range(half - 1):
        across[k].wait_recv()
        total = total + from_row[k].astype(jnp.float32)
    mine[...] = total.astype(mine.dtype)
    copies = [
        push(mine.at[(col + k + 1) % cols], landed.at[k], (part_send, part_recv), k, peer)
        for k, peer in enumerate(col_peers)
    ]
    for copy in copies:
        copy.wait()
    part = mine[col].astype(jnp.float32)
    for k in range(cols - 1):
        part = part + landed[k].astype(jnp.float32)
    out_ref[col] = part.astype(out_ref.dtype)
    copies = [
        push(out_ref.at[col], out_ref.at[col], (col_send, col_recv), k, peer)
        for k, peer in enumerate(col_peers)
    ]
    for copy in copies:
        copy.wait()
    for copy in between + across:
        copy.wait_send()


def fold(value, collective_id):
    rows, cols = lax.axis_size("row"), lax.axis_size("col")
    count, width = value.shape[0] // rows, value.shape[1]
    part = count // cols
    half = rows // 2
    dma = pltpu.SemaphoreType.DMA
    block = (cols, part, width)
    out = pl.pallas_call(
        functools.partial(fold_kernel, rows, cols),
        out_shape=jax.ShapeDtypeStruct(block, value.dtype),
        in_specs=[pl.BlockSpec(memory_space=pltpu.VMEM)],
        out_specs=pl.BlockSpec(memory_space=pltpu.VMEM),
        scratch_shapes=[
            pltpu.VMEM((half, *block), value.dtype),
            pltpu.VMEM((half - 1, *block), value.dtype),
            pltpu.VMEM((half - 1, *block), value.dtype),
            pltpu.VMEM(block, value.dtype),
            pltpu.VMEM((cols - 1, part, width), value.dtype),
        ]
        + [dma((half,))] * 2
        + [dma((half - 1,))] * 2
        + [dma((cols - 1,))] * 4,
        compiler_params=pltpu.CompilerParams(
            collective_id=collective_id, has_side_effects=True, vmem_limit_bytes=VMEM_LIMIT
        ),
    )(value.reshape(rows, *block))
    return out.reshape(count, width)


def flipped(index, entry):
    bit = 1
    while bit <= entry:
        if entry & bit:
            index = index + bit * (1 - 2 * (index // bit % 2))
        bit *= 2
    return index


class Matrix:
    def __init__(self, place, grad, basis, refs, adds_weight):
        self.row, self.col, self.rows, self.cols = place
        self.grad, self.basis = grad, basis
        (
            self.mean, self.square, self.weight, self.left,
            self.next, self.moment, self.scale,
            self.sums, self.work, self.inbox, self.steps, self.whole, self.sems, self.row_sems, self.core_sems,
        ) = refs
        self.adds_weight = adds_weight
        self.levels = [1 << k for k in range(self.cols.bit_length() - 1)]
        self.slot = 0
        self.started = []
        self.pending = []

    def send(self, source, target, bit):
        peer = (self.row, flipped(self.col, bit))
        slot = self.slot
        self.slot += 1
        copy = push(source, target, (self.sems.at[0], self.sems.at[1]), slot, peer)
        self.started.append(copy)
        return copy

    def arrive(self):
        for copy in self.pending:
            copy.wait_recv()
        self.pending = []

    def halving(self, phase):
        entries = list(range(self.cols))
        place = phase * (self.cols - 1)
        first = True
        for bit in self.levels:
            gone = [e for e in entries if e & bit]
            entries = [e for e in entries if not e & bit]
            for k, e in enumerate(gone):
                if first and phase == 0:
                    source = self.grad(e)
                elif first:
                    self.multiply(e)
                    source = self.work.at[e]
                else:
                    source = self.sums.at[e // 2] if phase == 0 else self.work.at[e]
                self.pending.append(self.send(source, self.inbox.at[place + k], bit))
            if first and phase == 1:
                for e in entries:
                    self.multiply(e)
            yield
            self.arrive()
            for k, e in enumerate(gone):
                mine = e - bit
                if first and phase == 0:
                    held = self.grad(mine)[...]
                else:
                    held = self.sums[mine // 2] if phase == 0 else self.work[mine]
                self.total = held.astype(jnp.float32) + self.inbox[place + k].astype(jnp.float32)
                if phase == 0:
                    self.sums[mine // 2] = self.total.astype(self.sums.dtype)
                elif bit != self.levels[-1]:
                    self.work[mine] = self.total.astype(self.work.dtype)
            place += len(gone)
            first = False

    def multiply(self, e):
        self.work[e] = jnp.dot(
            self.sums[0],
            self.basis(e),
            preferred_element_type=jnp.float32,
        ).astype(self.work.dtype)

    def go(self):
        yield from self.halving(0)
        yield from self.halving(1)
        rotated = self.total
        moment = MOMENT_BETA * self.mean[...] + (1.0 - MOMENT_BETA) * rotated
        scale = MOMENT_BETA * self.square[...] + (1.0 - MOMENT_BETA) * rotated * rotated
        self.moment[...] = moment
        self.scale[...] = scale
        self.steps[0] = (moment / (jnp.sqrt(scale) + ADAM_EPSILON)).astype(self.steps.dtype)
        arriving = [(0, None)]
        back = None
        while arriving:
            e, arrived = arriving.pop(0)
            if arrived is not None:
                arrived.wait_recv()
            for bit in reversed(self.levels):
                if e % (2 * bit) == 0:
                    copy = self.send(self.steps.at[e], self.steps.at[e + bit], bit)
                    arriving.append((e + bit, copy))
            term = lax.dot_general(
                self.steps[e],
                self.basis(e),
                (((1,), (1,)), ((), ())),
                preferred_element_type=jnp.float32,
            )
            back = term if back is None else back + term
            yield
        self.whole[self.row] = back.astype(self.whole.dtype)
        half = self.rows // 2
        other = (self.row // 2 * 2 + 1 - self.row % 2, self.col)
        own = self.whole.at[self.row]
        across = [
            push(own, own, (self.row_sems.at[0], self.row_sems.at[1]), k - 1, peer)
            for k, peer in enumerate(same_core(self.row, self.col, self.rows), 1)
        ]
        core_sems = (self.core_sems.at[0], self.core_sems.at[1])
        between = [push(own, own, core_sems, 0, other)]
        self.started += across + between
        yield
        for k in range(1, half):
            across[k - 1].wait_recv()
            block = self.whole.at[(self.row + self.rows - 2 * k) % self.rows]
            copy = push(block, block, core_sems, k, other)
            between.append(copy)
            self.started.append(copy)
        yield
        for copy in between:
            copy.wait_recv()
        depth, count = self.weight.shape
        everything = self.whole[...].reshape(self.rows * depth, count)
        update = jnp.dot(self.left[...], everything, preferred_element_type=jnp.float32)
        weight = self.weight[...]
        change = -(SOAP_RATE * (update + WEIGHT_DECAY * weight))
        self.next[...] = weight + change if self.adds_weight else change
        for copy in self.started:
            copy.wait_send()


def same_core(row, col, rows):
    return [((row + 2 * k) % rows, col) for k in range(1, rows // 2)]


def soap_kernel(rows, cols, adds, streamed, *refs):
    row, col = lax.axis_index("row"), lax.axis_index("col")
    peers = [(row, flipped(col, 1 << k)) for k in range(cols.bit_length() - 1)]
    greet(peers + same_core(row, col, rows) + [(row // 2 * 2 + 1 - row % 2, col)])
    count = len(adds)
    shared = 1 if streamed else count
    grads, bases, refs = refs[:shared], refs[shared : 2 * shared], refs[2 * shared :]
    inputs, refs = refs[: 4 * count], refs[4 * count :]
    outputs, refs = refs[: 3 * count], refs[3 * count :]
    scratch, refs = refs[: 8 * count], refs[8 * count :]
    running = []
    loads = []
    for m, add in enumerate(adds):
        grad, basis = grads[m % shared], bases[m % shared]
        others = inputs[4 * m : 4 * m + 4]
        width = others[0].shape[1]
        if streamed:
            held, stage, load_sems = refs

            def grad_of(e, grad=grad, m=m, width=width):
                at = pl.multiple_of((streamed.index(m) * cols + flipped(col, e)) * width, width)
                return grad.at[:, pl.ds(at, width)]

            def basis_of(e, held=held, m=m):
                return held[m, e]

            for e in [*range(1, cols, 2), *range(2, cols, 2), 0]:
                at = pl.multiple_of(flipped(col, e) * width, width)
                for part in range(2):
                    lines = pl.ds(part * (width // 2), width // 2)
                    copy = pltpu.make_async_copy(
                        basis.at[m, lines, pl.ds(at, width)], stage.at[part], load_sems.at[part]
                    )
                    loads.append((copy, part, m, e))
        else:

            def grad_of(e, grad=grad):
                return grad.at[flipped(col, e)]

            def basis_of(e, basis=basis):
                return basis[flipped(col, e)]

        refs_of = (*others, *outputs[3 * m : 3 * m + 3], *scratch[8 * m : 8 * m + 8])
        running.append(Matrix((row, col, rows, cols), grad_of, basis_of, refs_of, add).go())
    if streamed:
        running = [running[m] for m in streamed]
        loads = [load for m in streamed for load in loads if load[2] == m]
        for copy, *unused in loads[:2]:
            copy.start()
    for m in running:
        next(m)
    for k, (copy, slot, m, e) in enumerate(loads):
        copy.wait()
        lines = pl.ds(slot * stage.shape[1], stage.shape[1])
        held[m, e, lines] = stage[slot].astype(held.dtype)
        if k + 2 < len(loads):
            loads[k + 2][0].start()
    while running:
        running = [m for m in running if next(m, "done") != "done"]


def soap(grads, bases, matrices, adds, streamed, collective_id):
    rows, cols = lax.axis_size("row"), lax.axis_size("col")
    dma = pltpu.SemaphoreType.DMA
    vmem = pl.BlockSpec(memory_space=pltpu.VMEM)
    outs, scratch = [], []
    for mean, square, weight, left in matrices:
        outs += [jax.ShapeDtypeStruct(weight.shape, jnp.float32)] * 3
        block = weight.shape
        scratch += [
            pltpu.VMEM((cols // 2, *block), left.dtype),
            pltpu.VMEM((cols, *block), left.dtype),
            pltpu.VMEM((2 * (cols - 1), *block), left.dtype),
            pltpu.VMEM((cols, *block), left.dtype),
            pltpu.VMEM((rows, *block), left.dtype),
            dma((2, 3 * (cols - 1))),
            dma((2, rows // 2 - 1)),
            dma((2, rows // 2)),
        ]
    if streamed:
        width = matrices[0][2].shape[1]
        scratch += [
            pltpu.VMEM((len(matrices), cols, width, width), jnp.bfloat16),
            pltpu.VMEM((2, width // 2, width), jnp.float32),
            dma((2,)),
        ]
    got = pl.pallas_call(
        functools.partial(soap_kernel, rows, cols, adds, streamed),
        out_shape=outs,
        in_specs=[vmem] * len(grads)
        + [pl.BlockSpec(memory_space=pl.ANY) if streamed else vmem] * len(bases)
        + [vmem] * (4 * len(matrices)),
        out_specs=[vmem] * len(outs),
        scratch_shapes=scratch,
        compiler_params=pltpu.CompilerParams(
            collective_id=collective_id, has_side_effects=True, vmem_limit_bytes=VMEM_LIMIT
        ),
    )(*grads, *bases, *[part for matrix in matrices for part in matrix])
    return [got[k * 3 : k * 3 + 3] for k in range(len(matrices))]


def outer_kernel(values_ref, left_ref, other_ref, *refs):
    out_ref, turned = refs[-2:]

    @pl.when(pl.program_id(0) == 0)
    def _():
        turned[...] = jnp.dot(
            values_ref[...], left_ref[...], preferred_element_type=jnp.float32
        ).astype(turned.dtype)

    out_ref[...] = lax.dot_general(
        turned[...], other_ref[...], (((0,), (0,)), ((), ())), preferred_element_type=jnp.float32
    ).astype(out_ref.dtype)


def outer(values, left_full, basis, other, block, total, at, buffer):
    tokens, width = values.shape
    specs = [
        pl.BlockSpec((tokens, width), lambda j: (0, 0)),
        pl.BlockSpec((width, width), lambda j: (0, basis)),
        pl.BlockSpec((tokens, block), lambda j: (0, j)),
    ]
    operands = [values, left_full, other]
    aliases = {}
    if buffer is not None:
        specs.append(pl.BlockSpec(memory_space=pl.ANY))
        operands.append(buffer)
        aliases = {3: 0}
    return pl.pallas_call(
        outer_kernel,
        grid=(other.shape[1] // block,),
        out_shape=jax.ShapeDtypeStruct((width, total), values.dtype),
        in_specs=specs,
        out_specs=pl.BlockSpec((width, block), lambda j: (0, at + j)),
        scratch_shapes=[pltpu.VMEM((tokens, width), values.dtype)],
        input_output_aliases=aliases,
        compiler_params=pltpu.CompilerParams(vmem_limit_bytes=VMEM_LIMIT),
        cost_estimate=pl.CostEstimate(
            flops=2 * tokens * width * (width + other.shape[1]),
            bytes_accessed=2 * width * (width + other.shape[1] + tokens),
            transcendentals=0,
        ),
    )(*operands)


def one_hot_tile(ids, first, count):
    columns = lax.broadcasted_iota(jnp.int32, (ids.shape[0], count), 1)
    return jnp.where(ids - first == columns, 1.0, 0.0).astype(jnp.bfloat16)


def lookup_kernel(rows, cols, ids_ref, table_ref, out_ref, table, taken, found, inbox, sems, row_sems):
    row, col = lax.axis_index("row"), lax.axis_index("col")
    levels = [1 << k for k in range(cols.bit_length() - 1)]
    row_peers = [((row + k) % rows, col) for k in range(1, rows)]
    greet([(row, flipped(col, bit)) for bit in levels] + row_peers)
    features, tokens = out_ref.shape[1:]
    planes = [(k, min(128, features - 128 * k)) for k in range(table.shape[1])]

    def turn(v, carry):
        first = pl.multiple_of(v * 128, 128)
        entries = table_ref[:, pl.ds(first, 128)].astype(jnp.float32).T
        for k, lanes in planes:
            table[pl.ds(first, 128), k, pl.ds(0, lanes)] = entries[:, 128 * k : 128 * k + lanes]
        return carry

    lax.fori_loop(0, table_ref.shape[1] // 128, turn, 0)

    def look(e):
        source = flipped(col, e) * rows

        def block(k, carry):
            start = (source + k) * tokens

            def some(j, carry):
                for u in range(LOOK_STEP):
                    at = j * LOOK_STEP + u
                    taken[at] = table[ids_ref[start + at]]
                return carry

            lax.fori_loop(0, tokens // LOOK_STEP, some, 0)
            for p, lanes in planes:
                found[e, k, pl.ds(128 * p, lanes), :] = taken[:, p, :].T[:lanes].astype(found.dtype)
            return carry

        lax.fori_loop(0, rows, block, 0)

    entries = list(range(cols))
    started, slot = [], 0
    for bit in levels:
        gone = [e for e in entries if e & bit]
        entries = [e for e in entries if not e & bit]
        copies = []
        for e in gone:
            if bit == 1:
                look(e)
            peer = (row, flipped(col, bit))
            copies.append(push(found.at[e], inbox.at[slot], (sems.at[0], sems.at[1]), slot, peer))
            slot += 1
        if bit == 1:
            for e in reversed(entries):
                look(e)
        for k, e in enumerate(gone):
            copies[k].wait_recv()
            at = slot - len(gone) + k
            found[e - bit] = found[e - bit] + inbox[at]
        started += copies
    out_ref[row] = found[0, row]
    copies = [
        push(found.at[0, peer[0]], out_ref.at[row], (row_sems.at[0], row_sems.at[1]), k, peer)
        for k, peer in enumerate(row_peers)
    ]
    for copy in copies:
        copy.wait_recv()
    for copy in copies + started:
        copy.wait_send()


def lookup(ids, table, tokens, collective_id):
    rows, cols = lax.axis_size("row"), lax.axis_size("col")
    features, count = table.shape
    planes = -(-features // 128)
    dma = pltpu.SemaphoreType.DMA
    vmem = pl.BlockSpec(memory_space=pltpu.VMEM)
    block = (rows, features, tokens)
    return pl.pallas_call(
        functools.partial(lookup_kernel, rows, cols),
        out_shape=jax.ShapeDtypeStruct(block, table.dtype),
        in_specs=[pl.BlockSpec(memory_space=pltpu.SMEM), vmem],
        out_specs=vmem,
        scratch_shapes=[
            pltpu.VMEM((count, planes, 128), jnp.float32),
            pltpu.VMEM((tokens, planes, 128), jnp.float32),
            pltpu.VMEM((cols, *block), table.dtype),
            pltpu.VMEM((cols - 1, *block), table.dtype),
            dma((2, cols - 1)),
            dma((2, rows - 1)),
        ],
        compiler_params=pltpu.CompilerParams(
            collective_id=collective_id, has_side_effects=True, vmem_limit_bytes=VMEM_LIMIT
        ),
    )(ids, table)


def scatter_kernel(
    rows, cols, ids_ref, grad_ref, base_ref, out_ref, held, sems, row_sems
):
    row, col = lax.axis_index("row"), lax.axis_index("col")
    levels = [1 << k for k in range(cols.bit_length() - 1)]
    row_peers = [((row + k) % rows, col) for k in range(1, rows)]
    greet([(row, flipped(col, bit)) for bit in levels] + row_peers)
    held[0, row] = grad_ref[row]
    copies = [
        push(grad_ref.at[peer[0]], held.at[0, row], (row_sems.at[0], row_sems.at[1]), k, peer)
        for k, peer in enumerate(row_peers)
    ]
    count = out_ref.shape[1]

    def place(e, first_time):
        source = flipped(col, e)

        def block(v, carry):
            first = pl.multiple_of(v * VOCAB_TILE, VOCAB_TILE)
            total = base_ref[:, pl.ds(first, VOCAB_TILE)] if first_time else out_ref[:, pl.ds(first, VOCAB_TILE)]
            for k in range(rows):
                total = total + lax.dot_general(
                    held[e, k],
                    one_hot_tile(ids_ref[source, k], first, VOCAB_TILE),
                    (((1,), (0,)), ((), ())),
                    preferred_element_type=jnp.float32,
                )
            out_ref[:, pl.ds(first, VOCAB_TILE)] = total
            return carry

        lax.fori_loop(0, count // VOCAB_TILE, block, 0)

    for copy in copies:
        copy.wait_recv()
    started = list(copies)
    arriving, slot = [(0, None)], 0
    while arriving:
        e, arrived = arriving.pop(0)
        if arrived is not None:
            arrived.wait_recv()
        for bit in reversed(levels):
            if e % (2 * bit) == 0:
                copy = push(
                    held.at[e], held.at[e + bit], (sems.at[0], sems.at[1]), slot,
                    (row, flipped(col, bit)),
                )
                slot += 1
                started.append(copy)
                arriving.append((e + bit, copy))
        place(e, e == 0)
    for copy in started:
        copy.wait_send()


def scatter(ids, grad, base, collective_id):
    rows, cols = lax.axis_size("row"), lax.axis_size("col")
    dma = pltpu.SemaphoreType.DMA
    vmem = pl.BlockSpec(memory_space=pltpu.VMEM)
    return pl.pallas_call(
        functools.partial(scatter_kernel, rows, cols),
        out_shape=jax.ShapeDtypeStruct(base.shape, jnp.float32),
        in_specs=[vmem] * 3,
        out_specs=vmem,
        scratch_shapes=[
            pltpu.VMEM((cols, *grad.shape), grad.dtype),
            dma((2, cols - 1)),
            dma((2, rows - 1)),
        ],
        compiler_params=pltpu.CompilerParams(
            collective_id=collective_id, has_side_effects=True, vmem_limit_bytes=VMEM_LIMIT
        ),
    )(ids, grad, base)


def send(value, axis, shift):
    count = lax.axis_size(axis)
    return lax.ppermute(value, axis, [(k, (k + shift) % count) for k in range(count)])


def collect(value, axis):
    return [value] + [send(value, axis, k) for k in range(1, lax.axis_size(axis))]


def deliver(pieces, axis, sign):
    return [pieces[0]] + [send(pieces[k], axis, sign * k) for k in range(1, len(pieces))]


def summed(pieces):
    total = pieces[0].astype(jnp.float32)
    for piece in pieces[1:]:
        total = total + piece.astype(jnp.float32)
    return total


def to_absolute(pieces, index):
    count = len(pieces)
    order = [pieces[0]] + [pieces[count - k] for k in range(1, count)]
    return jnp.roll(jnp.stack(order), index, axis=0)


def pick_block(values, index, axis):
    return lax.dynamic_index_in_dim(values, index, axis, keepdims=False)


def rms_norm(values, gain_vec):
    return (
        values
        * lax.rsqrt(jnp.mean(values * values, axis=-1, keepdims=True) + NORM_EPSILON)
        * gain_vec
    )


def rotary(values, positions):
    half_width = values.shape[-1] // 2
    frequency = jnp.power(10000.0, -jnp.arange(half_width, dtype=jnp.float32) / half_width)
    angles = positions[:, None].astype(jnp.float32) * frequency[None, :]
    cosine = jnp.cos(angles)[:, None, :]
    sine_part = jnp.sin(angles)[:, None, :]
    first_half = values[..., :half_width]
    second_half = values[..., half_width:]
    return jnp.concatenate(
        [
            first_half * cosine - second_half * sine_part,
            second_half * cosine + first_half * sine_part,
        ],
        axis=-1,
    )


def swiglu(gate_part, upward):
    return jax.nn.silu(gate_part) * upward


def matmul(left_op, right_op):
    return jnp.dot(left_op, right_op, preferred_element_type=jnp.float32)


def matmul_last(left_op, right_op):
    return lax.dot_general(
        left_op, right_op, (((1,), (1,)), ((), ())), preferred_element_type=jnp.float32
    )


def matmul_first(left_op, right_op):
    return lax.dot_general(
        left_op, right_op, (((0,), (0,)), ((), ())), preferred_element_type=jnp.float32
    )


def norm_back(values, gain_vec, grad_output):
    unused, pull_back = jax.vjp(rms_norm, values, gain_vec)
    return pull_back(grad_output)


def adam_update(weight, gradient_value, moment, square_avg, decay_rate):
    moment_new = MOMENT_BETA * moment + (1.0 - MOMENT_BETA) * gradient_value
    square_new = MOMENT_BETA * square_avg + (1.0 - MOMENT_BETA) * gradient_value * gradient_value
    change = -(
        ADAM_RATE * (moment_new / (jnp.sqrt(square_new) + ADAM_EPSILON) + decay_rate * weight)
    )
    return (change, moment_new, square_new)


def per_device(
    token_ids,
    target_ids,
    loss_slots,
    valid_mask,
    prefix_lens,
    embed_table,
    norm_gains,
    qkv_weight,
    output_weight,
    mlp_weight,
    embed_mean,
    embed_square,
    gain_mean,
    gain_square,
    qkv_mean,
    qkv_square,
    out_mean,
    out_square,
    mlp_mean,
    mlp_square,
    left_bases,
    qkv_bases,
    out_bases,
    feedforward_bases,
):
    row_index = lax.axis_index("row")
    col_index = lax.axis_index("col")
    row_count = lax.axis_size("row")
    col_count = lax.axis_size("col")
    low = jnp.bfloat16
    group_tokens = token_ids.shape[0]
    pick_count = loss_slots.shape[0]
    device_tokens = group_tokens // col_count
    vocab_shard, features = embed_table.shape
    width = features * row_count
    query_width = Q_HEADS * HEAD
    kv_width = KV_HEADS * HEAD
    group_size = Q_HEADS // KV_HEADS
    scaling = HEAD ** (-0.5)
    qkv_cols, out_cols, ff_cols = qkv_weight.shape[1], output_weight.shape[1], mlp_weight.shape[2]
    vocab_part = vocab_shard // row_count

    ids_all = lax.all_gather(jnp.concatenate([token_ids, target_ids]), "row", axis=0)
    table_first, left_first, ids_all = lax.optimization_barrier((embed_table, left_bases, ids_all))

    qkv_width, ff_width = qkv_cols * col_count, ff_cols * col_count
    attn_full = lax.all_gather(
        jnp.concatenate([qkv_weight.astype(low), output_weight.astype(low)], axis=1),
        ("col", "row"),
        axis=0,
        tiled=True,
    ).reshape(col_count, width, qkv_cols + out_cols)
    mlp_low = mlp_weight.astype(low)
    mlp_full = lax.all_gather(
        jnp.concatenate([mlp_low[0], mlp_low[1], mlp_low[2]], axis=1),
        ("col", "row"),
        axis=0,
        tiled=True,
    ).reshape(col_count, width, 3 * ff_cols)
    bases_low = left_first.astype(low)
    left_block = jnp.concatenate([bases_low[k] for k in range(5)], axis=1)
    left_full = lax.all_gather(left_block, "row", axis=0, tiled=True)
    columns = range(col_count)
    qkv_full = [attn_full[c, :, :qkv_cols] for c in columns]
    out_full = [attn_full[c, :, qkv_cols:] for c in columns]
    gate_full, up_full, down_full = (
        [mlp_full[c, :, k * ff_cols : (k + 1) * ff_cols] for c in columns] for k in range(3)
    )

    def by_columns(values, weights, multiply):
        return jnp.concatenate([multiply(values, weight) for weight in weights], axis=1)

    def over_columns(values, weights):
        count = values.shape[1] // col_count
        terms = [
            matmul_last(values[:, c * count : (c + 1) * count], weight)
            for c, weight in enumerate(weights)
        ]
        return functools.reduce(jnp.add, terms)

    tokens_all = ids_all[:, :group_tokens].reshape(row_count, col_count, device_tokens)
    targets_all = ids_all[:, group_tokens:].reshape(row_count * pick_count)
    local_tokens = jnp.moveaxis(tokens_all, 1, 0) - col_index * vocab_shard
    inside = (local_tokens >= 0) & (local_tokens < vocab_shard)
    local_tokens = jnp.where(inside, local_tokens, vocab_shard)
    table_low_t = table_first.astype(low).T

    def reduce_rows(values):
        return lax.psum_scatter(values, "row", scatter_dimension=0, tiled=True)

    padded = jnp.pad(table_low_t, ((0, 0), (0, 128 - vocab_shard % 128)))
    found = lookup(local_tokens.reshape(-1), padded, device_tokens, 6)
    table_later, found = lax.optimization_barrier((table_low_t, found))
    embedded = found.reshape(width, device_tokens).T.astype(jnp.float32)

    table_parts = jnp.moveaxis(table_later.reshape(features, row_count, vocab_part), 1, 0)
    part_pieces = [
        pick_block(table_parts, (row_index + k) % row_count, 0) for k in range(row_count)
    ]
    table_part = to_absolute(deliver(part_pieces, "row", 1), row_index).reshape(width, vocab_part)

    normed = rms_norm(embedded, norm_gains[0]).astype(low)
    project = by_columns(normed, qkv_full, matmul).astype(low)
    first_token = col_index * device_tokens
    positions = first_token + jnp.arange(device_tokens, dtype=jnp.int32)
    seq_prefix = jnp.sum(
        jnp.where(jnp.arange(prefix_lens.shape[0], dtype=jnp.int32) == row_index, prefix_lens, 0)
    )

    def rotate_here(values):
        return rotary(values, positions)

    queries_raw = project[:, :query_width].astype(jnp.float32).reshape(device_tokens, Q_HEADS, HEAD)
    keys_raw = (
        project[:, query_width : query_width + kv_width]
        .astype(jnp.float32)
        .reshape(device_tokens, KV_HEADS, HEAD)
    )
    queries = rotate_here(queries_raw).astype(low).reshape(device_tokens, KV_HEADS, group_size, HEAD)
    keys_local = rotate_here(keys_raw).astype(low).reshape(device_tokens, kv_width)
    keys_values = jnp.concatenate(
        collect(
            jnp.concatenate([keys_local, project[:, query_width + kv_width :]], axis=1), "col"
        ),
        axis=0,
    )
    attn_keys = keys_values[:, :kv_width].reshape(LEN, KV_HEADS, HEAD)
    attn_values = keys_values[:, kv_width:].reshape(LEN, KV_HEADS, HEAD)
    key_blocks = (col_index - jnp.arange(col_count, dtype=jnp.int32)) % col_count
    key_positions = (
        key_blocks[:, None] * device_tokens + jnp.arange(device_tokens, dtype=jnp.int32)[None, :]
    ).reshape(LEN)
    allowed = (key_positions[None, :] <= positions[:, None]) | (key_positions[None, :] < seq_prefix)

    raw_scores = (
        jnp.einsum("qhgd,khd->hgqk", queries, attn_keys, preferred_element_type=jnp.float32)
        * scaling
    )
    scores = jnp.where(allowed, raw_scores, MASK_VALUE)
    largest = jnp.max(scores, axis=-1, keepdims=True)
    weights = jnp.exp(scores - largest)
    attn_probs = weights / jnp.sum(weights, axis=-1, keepdims=True)
    attended = (
        jnp.einsum(
            "hgqk,khd->qhgd",
            attn_probs.astype(low),
            attn_values,
            preferred_element_type=jnp.float32,
        )
        .astype(low)
        .reshape(device_tokens, query_width)
    )
    hidden_one = embedded + over_columns(attended, out_full)
    middle = rms_norm(hidden_one, norm_gains[1]).astype(low)
    gate_part = by_columns(middle, gate_full, matmul)
    upward = by_columns(middle, up_full, matmul)
    inner_act = swiglu(gate_part, upward).astype(low)
    hidden_two = hidden_one + over_columns(inner_act, down_full)
    final = rms_norm(hidden_two, norm_gains[2]).astype(low)

    pick_hit = (loss_slots[:, None] == positions[None, :]).astype(low)
    final_here = matmul(pick_hit, final).astype(low)
    final_pick = spread(final_here, 0)
    logits = matmul(final_pick, table_part)
    local_max = jnp.max(logits, axis=-1)
    local_sum = jnp.sum(jnp.exp(logits - local_max[:, None]), axis=-1)
    part_first = col_index * vocab_shard + row_index * vocab_part
    target_hit = (
        jnp.arange(vocab_part, dtype=jnp.int32)[None, :] == (targets_all - part_first)[:, None]
    )
    local_target = jnp.sum(jnp.where(target_hit, logits, 0.0), axis=-1)
    own_stats = jnp.stack([local_max, local_sum, local_target]).reshape(-1, 128)
    everyone = share(own_stats, 1).reshape(row_count * col_count, 3, row_count * pick_count)
    top = jnp.max(everyone[:, 0], axis=0)
    log_total = top + jnp.log(jnp.sum(everyone[:, 1] * jnp.exp(everyone[:, 0] - top), axis=0))
    target_logit = jnp.sum(everyone[:, 2], axis=0)
    valid_count = jnp.maximum(jnp.sum(valid_mask).astype(jnp.float32), 1.0)
    row_weights = valid_mask.astype(jnp.float32) / valid_count
    loss_value = jnp.sum(row_weights * (log_total - target_logit))
    grad_logits = (
        (jnp.exp(logits - log_total[:, None]) - target_hit.astype(jnp.float32))
        * row_weights[:, None]
    ).astype(low)
    grad_pick = matmul_last(grad_logits, table_part).astype(low)
    grad_seq = fold(grad_pick, 2)
    grad_final = matmul_first(pick_hit, grad_seq)

    table_grad_part = matmul_first(final_pick, grad_logits).astype(low)
    grad_parts = table_grad_part.reshape(row_count, features, vocab_part)
    grad_pieces = [pick_block(grad_parts, (row_index + k) % row_count, 0) for k in range(row_count)]
    table_grad = to_absolute(deliver(grad_pieces, "row", 1), row_index)
    table_grad = jnp.moveaxis(table_grad, 0, 1).reshape(features, vocab_shard).astype(jnp.float32)

    grad_two, gain_two = norm_back(hidden_two, norm_gains[2], grad_final)
    grad_two_low = grad_two.astype(low)
    ff_blocks = ff_width // ff_cols
    mlp_grad = outer(grad_two_low, left_full, 4, inner_act, ff_cols, 3 * ff_width, 0, None)
    grad_inner = by_columns(grad_two_low, down_full, matmul)
    unused, pull_swiglu = jax.vjp(swiglu, gate_part, upward)
    grad_gate, grad_up = pull_swiglu(grad_inner)
    grad_gate = grad_gate.astype(low)
    grad_up = grad_up.astype(low)
    mlp_grad = outer(middle, left_full, 2, grad_gate, ff_cols, 3 * ff_width, ff_blocks, mlp_grad)
    mlp_grad = outer(middle, left_full, 3, grad_up, ff_cols, 3 * ff_width, 2 * ff_blocks, mlp_grad)
    grad_gate, grad_up, mlp_grad = lax.optimization_barrier((grad_gate, grad_up, mlp_grad))
    mlp_rows = reduce_rows(mlp_grad)
    grad_middle = over_columns(grad_gate, gate_full) + over_columns(grad_up, up_full)
    grad_middle_in, gain_one = norm_back(hidden_one, norm_gains[1], grad_middle)
    grad_one = grad_two + grad_middle_in
    grad_one_low = grad_one.astype(low)
    attn_width = query_width + qkv_width
    attn_grad = outer(
        grad_one_low, left_full, 1, attended, SMALL_BLOCK, attn_width, 0, None
    )
    grad_attended = by_columns(grad_one_low, out_full, matmul).astype(low).reshape(
        device_tokens, KV_HEADS, group_size, HEAD
    )
    grad_probs = jnp.einsum(
        "qhgd,khd->hgqk", grad_attended, attn_values, preferred_element_type=jnp.float32
    )
    inner_sum = jnp.sum(attn_probs * grad_probs, axis=-1, keepdims=True)
    grad_scores = (attn_probs * (grad_probs - inner_sum)).astype(low)
    grad_queries = (
        jnp.einsum("hgqk,khd->qhgd", grad_scores, attn_keys, preferred_element_type=jnp.float32)
        * scaling
    )
    grad_keys = (
        jnp.einsum("hgqk,qhgd->khd", grad_scores, queries, preferred_element_type=jnp.float32)
        * scaling
    )
    grad_values = jnp.einsum(
        "hgqk,qhgd->khd",
        attn_probs.astype(low),
        grad_attended,
        preferred_element_type=jnp.float32,
    )
    grad_pairs = (
        jnp.concatenate([grad_keys.reshape(LEN, kv_width), grad_values.reshape(LEN, kv_width)], axis=1)
        .astype(low)
        .reshape(col_count, device_tokens, 2 * kv_width)
    )
    grad_pairs = summed(deliver([grad_pairs[k] for k in range(col_count)], "col", -1))
    unused, pull_query = jax.vjp(rotate_here, queries_raw)
    grad_query_raw = pull_query(grad_queries.reshape(device_tokens, Q_HEADS, HEAD))[0]
    unused, pull_key = jax.vjp(rotate_here, keys_raw)
    grad_key_raw = pull_key(grad_pairs[:, :kv_width].reshape(device_tokens, KV_HEADS, HEAD))[0]
    grad_project = jnp.concatenate(
        [
            grad_query_raw.reshape(device_tokens, query_width),
            grad_key_raw.reshape(device_tokens, kv_width),
            grad_pairs[:, kv_width:],
        ],
        axis=1,
    ).astype(low)
    attn_grad = outer(
        normed, left_full, 0, grad_project, SMALL_BLOCK, attn_width,
        query_width // SMALL_BLOCK, attn_grad,
    )
    attn_rows = reduce_rows(attn_grad)
    grad_normed = over_columns(grad_project, qkv_full)
    grad_embed_in, gain_zero = norm_back(embedded, norm_gains[0], grad_normed)
    grad_embedded = (grad_one + grad_embed_in).astype(low)
    own_gains = jnp.stack([gain_zero, gain_one, gain_two]).reshape(-1, 128)
    gain_grads = jnp.sum(
        share(own_gains, 3).reshape(row_count * col_count, 3, width), axis=0
    )
    by_feature = grad_embedded.T.reshape(row_count, features, device_tokens)
    vocab_room = -(-(vocab_shard + 1) // VOCAB_TILE) * VOCAB_TILE
    table_grad = scatter(
        local_tokens[:, :, :, None],
        by_feature,
        jnp.pad(table_grad, ((0, 0), (0, vocab_room - vocab_shard))),
        7,
    )[:, :vocab_shard]

    mlp_rows, table_grad = lax.optimization_barrier((mlp_rows, table_grad))
    mlp_new = soap(
        [mlp_rows],
        [feedforward_bases],
        [(mlp_mean[j], mlp_square[j], mlp_weight[j], bases_low[2 + j]) for j in range(3)],
        (True, True, True),
        (2, 0, 1),
        4,
    )
    mlp_next, mlp_moment, mlp_scale = (
        jnp.stack([entry[k] for entry in mlp_new]) for k in range(3)
    )

    attn_rows, mlp_next = lax.optimization_barrier((attn_rows, mlp_next))

    def blocks(values):
        return jnp.moveaxis(values.reshape(values.shape[0], col_count, -1), 1, 0)

    (out_update, out_moment, out_scale), (qkv_next, qkv_moment, qkv_scale) = soap(
        [blocks(attn_rows[:, :query_width]), blocks(attn_rows[:, query_width:])],
        [blocks(out_bases.astype(low)), blocks(qkv_bases.astype(low))],
        [
            (out_mean, out_square, output_weight, bases_low[1]),
            (qkv_mean, qkv_square, qkv_weight, bases_low[0]),
        ],
        (False, True),
        (),
        5,
    )
    embed_change, embed_moment, embed_scale = adam_update(
        embed_table, table_grad.T, embed_mean, embed_square, WEIGHT_DECAY
    )
    embed_next = embed_table + embed_change
    gain_update, gain_moment, gain_scale = adam_update(
        norm_gains, gain_grads, gain_mean, gain_square, 0.0
    )
    return (
        loss_value,
        embed_next,
        embed_moment,
        embed_scale,
        gain_update,
        gain_moment,
        gain_scale,
        qkv_next,
        qkv_moment,
        qkv_scale,
        out_update,
        out_moment,
        out_scale,
        mlp_next,
        mlp_moment,
        mlp_scale,
    )


def solution(mesh):
    placed = (
        P("row"),
        P("row"),
        P("row"),
        P(),
        P(),
        P("col", "row"),
        P(),
        P("row", "col"),
        P("row", "col"),
        P(None, "row", "col"),
        P("col", "row"),
        P("col", "row"),
        P(),
        P(),
        P("row", "col"),
        P("row", "col"),
        P("row", "col"),
        P("row", "col"),
        P(None, "row", "col"),
        P(None, "row", "col"),
        P(None, "row", None),
        P("col", None),
        P("col", None),
        P(None, "col", None),
    )
    return jax.shard_map(
        per_device,
        mesh=mesh,
        in_specs=placed,
        out_specs=(
            P(),
            P("col", "row"),
            P("col", "row"),
            P("col", "row"),
            P(),
            P(),
            P(),
            P("row", "col"),
            P("row", "col"),
            P("row", "col"),
            P("row", "col"),
            P("row", "col"),
            P("row", "col"),
            P(None, "row", "col"),
            P(None, "row", "col"),
            P(None, "row", "col"),
        ),
        check_vma=False,
    )
```

```python
import functools

import jax
import jax.numpy as jnp
from jax import lax
from jax.experimental import pallas as pl
from jax.experimental.pallas import tpu as pltpu
from jax.sharding import PartitionSpec as P

Q_HEADS = 18
KV_HEADS = 6
HEAD = 64
LEN = 1024
PICK = 128


NORM_EPSILON = 1e-05
ADAM_EPSILON = 1e-08
MOMENT_BETA = 0.5
SOAP_RATE = 0.05
ADAM_RATE = 0.01
WEIGHT_DECAY = 0.1
MASK_VALUE = -1e30
MESH = pl.DeviceIdType.MESH
VMEM_LIMIT = 58 * 2**20
VOCAB_TILE = 1024
LOOK_STEP = 32
TILES_AT_ONCE = 3
SMALL_BLOCK = 384


def greet(peers):
    barrier = pltpu.get_barrier_semaphore()
    for peer in peers:
        pl.semaphore_signal(barrier, inc=1, device_id=peer, device_id_type=MESH)
    pl.semaphore_wait(barrier, len(peers))


def push(source, target, sems, slot, peer):
    copy = pltpu.make_async_remote_copy(
        src_ref=source,
        dst_ref=target,
        send_sem=sems[0].at[slot],
        recv_sem=sems[1].at[slot],
        device_id=peer,
        device_id_type=MESH,
    )
    copy.start()
    return copy


def row_peer(row, col, rows, k):
    half = rows // 2
    if k < half:
        return ((row + 2 * k) % rows, col)
    return ((row // 2 * 2 + 2 * (k - half)) % rows + 1 - row % 2, col)


def share_kernel(rows, cols, x_ref, out_ref, col_send, col_recv, row_send, row_recv):
    row, col = lax.axis_index("row"), lax.axis_index("col")
    col_peers = [(row, (col + k) % cols) for k in range(1, cols)]
    row_peers = [((row + k) % rows, col) for k in range(1, rows)]
    greet(col_peers + row_peers)
    out_ref[row, col] = x_ref[...]
    copies = [
        push(out_ref.at[row, col], out_ref.at[row, col], (col_send, col_recv), k, peer)
        for k, peer in enumerate(col_peers)
    ]
    for copy in copies:
        copy.wait()
    copies = [
        push(out_ref.at[row], out_ref.at[row], (row_send, row_recv), k, peer)
        for k, peer in enumerate(row_peers)
    ]
    for copy in copies:
        copy.wait()


def share(value, collective_id):
    rows, cols = lax.axis_size("row"), lax.axis_size("col")
    return pl.pallas_call(
        functools.partial(share_kernel, rows, cols),
        out_shape=jax.ShapeDtypeStruct((rows, cols, *value.shape), value.dtype),
        in_specs=[pl.BlockSpec(memory_space=pltpu.VMEM)],
        out_specs=pl.BlockSpec(memory_space=pltpu.VMEM),
        scratch_shapes=[
            pltpu.SemaphoreType.DMA((cols - 1,)),
            pltpu.SemaphoreType.DMA((cols - 1,)),
            pltpu.SemaphoreType.DMA((rows - 1,)),
            pltpu.SemaphoreType.DMA((rows - 1,)),
        ],
        compiler_params=pltpu.CompilerParams(
            collective_id=collective_id, has_side_effects=True, vmem_limit_bytes=VMEM_LIMIT
        ),
    )(value)


def spread_kernel(
    rows, cols, x_ref, out_ref, landed, part_send, part_recv, col_send, col_recv,
    row_send, row_recv, core_send, core_recv,
):
    row, col = lax.axis_index("row"), lax.axis_index("col")
    half = rows // 2
    other = row // 2 * 2 + 1 - row % 2
    col_peers = [(row, (col + k) % cols) for k in range(1, cols)]
    row_peers = [((row + 2 * k) % rows, col) for k in range(1, half)]
    greet(col_peers + row_peers + [(other, col)])
    copies = [
        push(x_ref.at[(col + k + 1) % cols], landed.at[k], (part_send, part_recv), k, peer)
        for k, peer in enumerate(col_peers)
    ]
    for copy in copies:
        copy.wait()
    total = x_ref[col].astype(jnp.float32)
    for k in range(cols - 1):
        total = total + landed[k].astype(jnp.float32)
    out_ref[row, col] = total.astype(out_ref.dtype)
    copies = [
        push(out_ref.at[row, col], out_ref.at[row, col], (col_send, col_recv), k, peer)
        for k, peer in enumerate(col_peers)
    ]
    for copy in copies:
        copy.wait()
    across = [
        push(out_ref.at[row], out_ref.at[row], (row_send, row_recv), k, peer)
        for k, peer in enumerate(row_peers)
    ]
    between = [push(out_ref.at[row], out_ref.at[row], (core_send, core_recv), 0, (other, col))]
    for k in range(1, half):
        across[k - 1].wait_recv()
        source = (row + rows - 2 * k) % rows
        between.append(
            push(out_ref.at[source], out_ref.at[source], (core_send, core_recv), k, (other, col))
        )
    for copy in across:
        copy.wait_send()
    for copy in between:
        copy.wait()


def spread(value, collective_id):
    rows, cols = lax.axis_size("row"), lax.axis_size("col")
    count, width = value.shape
    part = count // cols
    dma = pltpu.SemaphoreType.DMA
    out = pl.pallas_call(
        functools.partial(spread_kernel, rows, cols),
        out_shape=jax.ShapeDtypeStruct((rows, cols, part, width), value.dtype),
        in_specs=[pl.BlockSpec(memory_space=pltpu.VMEM)],
        out_specs=pl.BlockSpec(memory_space=pltpu.VMEM),
        scratch_shapes=[pltpu.VMEM((cols - 1, part, width), value.dtype)]
        + [dma((cols - 1,))] * 4
        + [dma((rows // 2 - 1,))] * 2
        + [dma((rows // 2,))] * 2,
        compiler_params=pltpu.CompilerParams(
            collective_id=collective_id, has_side_effects=True, vmem_limit_bytes=VMEM_LIMIT
        ),
    )(value.reshape(cols, part, width))
    return out.reshape(rows * count, width)


def fold_kernel(
    rows, cols, x_ref, out_ref, from_core, to_row, from_row, mine, landed, core_send, core_recv,
    row_send, row_recv, part_send, part_recv, col_send, col_recv,
):
    row, col = lax.axis_index("row"), lax.axis_index("col")
    half = rows // 2
    core = row % 2
    other = row // 2 * 2 + 1 - core
    col_peers = [(row, (col + k) % cols) for k in range(1, cols)]
    row_peers = [((row + 2 * k) % rows, col) for k in range(1, half)]
    greet(col_peers + row_peers + [(other, col)])
    between = [
        push(
            x_ref.at[(row + 2 * k) % rows // 2 * 2 + 1 - core],
            from_core.at[k],
            (core_send, core_recv),
            k,
            (other, col),
        )
        for k in [*range(1, half), 0]
    ]
    across = []
    for k in range(1, half):
        between[k - 1].wait_recv()
        to_row[k - 1] = (
            x_ref[(row + 2 * k) % rows].astype(jnp.float32) + from_core[k].astype(jnp.float32)
        ).astype(to_row.dtype)
        across.append(
            push(to_row.at[k - 1], from_row.at[k - 1], (row_send, row_recv), k - 1, row_peers[k - 1])
        )
    between[half - 1].wait_recv()
    total = x_ref[row].astype(jnp.float32) + from_core[0].astype(jnp.float32)
    for k in range(half - 1):
        across[k].wait_recv()
        total = total + from_row[k].astype(jnp.float32)
    mine[...] = total.astype(mine.dtype)
    copies = [
        push(mine.at[(col + k + 1) % cols], landed.at[k], (part_send, part_recv), k, peer)
        for k, peer in enumerate(col_peers)
    ]
    for copy in copies:
        copy.wait()
    part = mine[col].astype(jnp.float32)
    for k in range(cols - 1):
        part = part + landed[k].astype(jnp.float32)
    out_ref[col] = part.astype(out_ref.dtype)
    copies = [
        push(out_ref.at[col], out_ref.at[col], (col_send, col_recv), k, peer)
        for k, peer in enumerate(col_peers)
    ]
    for copy in copies:
        copy.wait()
    for copy in between + across:
        copy.wait_send()


def fold(value, collective_id):
    rows, cols = lax.axis_size("row"), lax.axis_size("col")
    count, width = value.shape[0] // rows, value.shape[1]
    part = count // cols
    half = rows // 2
    dma = pltpu.SemaphoreType.DMA
    block = (cols, part, width)
    out = pl.pallas_call(
        functools.partial(fold_kernel, rows, cols),
        out_shape=jax.ShapeDtypeStruct(block, value.dtype),
        in_specs=[pl.BlockSpec(memory_space=pltpu.VMEM)],
        out_specs=pl.BlockSpec(memory_space=pltpu.VMEM),
        scratch_shapes=[
            pltpu.VMEM((half, *block), value.dtype),
            pltpu.VMEM((half - 1, *block), value.dtype),
            pltpu.VMEM((half - 1, *block), value.dtype),
            pltpu.VMEM(block, value.dtype),
            pltpu.VMEM((cols - 1, part, width), value.dtype),
        ]
        + [dma((half,))] * 2
        + [dma((half - 1,))] * 2
        + [dma((cols - 1,))] * 4,
        compiler_params=pltpu.CompilerParams(
            collective_id=collective_id, has_side_effects=True, vmem_limit_bytes=VMEM_LIMIT
        ),
    )(value.reshape(rows, *block))
    return out.reshape(count, width)


def line_peers(row, col, cols):
    return [(row, (col + 1) % cols), (row, (col + cols - 1) % cols)]


def line_ways(place):
    row, col, cols = place
    return ((0, col), (1, cols - 1 - col))


def line_copy(place, down, source, target, sems, at, step):
    row, col, cols = place
    slot = at + down * (cols - 1) + step
    return pltpu.make_async_remote_copy(
        src_ref=source,
        dst_ref=target,
        send_sem=sems.at[0, slot],
        recv_sem=sems.at[1, slot],
        device_id=(row, (col + (cols - 1 if down else 1)) % cols),
        device_id_type=MESH,
    )


def line_sum(place, term, work, inbox, at, sems, sem_at, result):
    row, col, cols = place

    def block_of(down, step):
        return jnp.clip(step - (cols - 1 - col) if down else cols - 1 - step + col, 0, cols - 1)

    def copy_of(down, step):
        landing = inbox.at[at + down * (cols - 1) + step]
        return line_copy(place, down, work.at[block_of(down, step)], landing, sems, sem_at, step)

    for step in range(cols - 1):
        for down, index in line_ways(place):
            d = block_of(down, step)

            @pl.when(index == 0)
            def _(d=d, down=down, step=step):
                if term is not None:
                    work[d] = term(d)
                copy_of(down, step).start()

            if step > 0:
                @pl.when((index > 0) & (index <= step))
                def _(d=d, down=down, step=step):
                    copy_of(down, step - 1).wait_recv()
                    arrived = inbox[at + down * (cols - 1) + step - 1]
                    own = work[d] if term is None else term(d)
                    work[d] = (own.astype(jnp.float32) + arrived.astype(jnp.float32)).astype(work.dtype)
                    copy_of(down, step).start()

        yield
    own = work[col] if term is None else term(col)
    result[...] = own.astype(result.dtype)
    for down, index in line_ways(place):
        @pl.when(index > 0)
        def _(down=down):
            copy_of(down, cols - 2).wait_recv()
            arrived = inbox[at + down * (cols - 1) + cols - 2]
            result[...] = (result[...].astype(jnp.float32) + arrived.astype(jnp.float32)).astype(result.dtype)

    for step in range(cols - 1):
        for down, index in line_ways(place):
            @pl.when(index <= step)
            def _(down=down, step=step):
                copy_of(down, step).wait_send()


def line_spread(place, block, sems, sem_at):
    row, col, cols = place

    def copy_of(down, step):
        lies = block(jnp.clip(col + step if down else col - step, 0, cols - 1))
        return line_copy(place, down, lies, lies, sems, sem_at, step)

    for step in range(cols):
        if step > 0:
            for down, index in line_ways(place):
                @pl.when(index >= step)
                def _(down=down, step=step):
                    copy_of(down, step - 1).wait_recv()

        if step < cols - 1:
            for down, index in line_ways(place):
                @pl.when((index >= step) & (index < cols - 1))
                def _(down=down, step=step):
                    copy_of(down, step).start()

            yield
    for step in range(cols - 1):
        for down, index in line_ways(place):
            @pl.when((index >= step) & (index < cols - 1))
            def _(down=down, step=step):
                copy_of(down, step).wait_send()


def swap_go(place, part_of, lies_at, sems, local_sem):
    row, col, rows, cols = place
    own = pltpu.make_async_copy(part_of(row), lies_at(row), local_sem)
    own.start()
    copies = [
        push(part_of((row + k) % rows), lies_at(row), (sems.at[0], sems.at[1]), k - 1, ((row + k) % rows, col))
        for k in range(1, rows)
    ]
    for _ in range(2 * cols):
        yield
    own.wait()
    for copy in copies:
        copy.wait()


class Matrix:
    def __init__(self, place, grad, basis, refs, adds_weight):
        self.row, self.col, self.rows, self.cols = place
        self.grad, self.basis = grad, basis
        (
            self.mean, self.square, self.weight, self.left,
            self.next, self.moment, self.scale,
            self.work, self.inbox, self.sum, self.total, self.whole, self.sems, self.row_sems, self.core_sems,
        ) = refs
        self.adds_weight = adds_weight

    def go(self):
        line = (self.row, self.col, self.cols)
        links = 2 * (self.cols - 1)
        yield from line_sum(
            line, lambda d: self.grad(d)[...], self.work, self.inbox, 0, self.sems, 0, self.sum
        )
        for d in range(self.cols):
            self.work[d] = jnp.dot(
                self.sum[...], self.basis(d), preferred_element_type=jnp.float32
            ).astype(self.work.dtype)
        yield from line_sum(line, None, self.work, self.inbox, links, self.sems, links, self.total)
        rotated = self.total[...]
        moment = MOMENT_BETA * self.mean[...] + (1.0 - MOMENT_BETA) * rotated
        scale = MOMENT_BETA * self.square[...] + (1.0 - MOMENT_BETA) * rotated * rotated
        self.moment[...] = moment
        self.scale[...] = scale
        steps = self.inbox
        steps[self.col] = (moment / (jnp.sqrt(scale) + ADAM_EPSILON)).astype(steps.dtype)
        yield from line_spread(line, lambda d: steps.at[d], self.sems, 2 * links)
        back = None
        for d in range(self.cols):
            term = lax.dot_general(
                steps[d], self.basis(d), (((1,), (1,)), ((), ())), preferred_element_type=jnp.float32
            )
            back = term if back is None else back + term
        self.whole[self.row] = back.astype(self.whole.dtype)
        half = self.rows // 2
        other = (self.row // 2 * 2 + 1 - self.row % 2, self.col)
        own = self.whole.at[self.row]
        across = [
            push(own, own, (self.row_sems.at[0], self.row_sems.at[1]), k - 1, peer)
            for k, peer in enumerate(same_core(self.row, self.col, self.rows), 1)
        ]
        core_sems = (self.core_sems.at[0], self.core_sems.at[1])
        between = [push(own, own, core_sems, 0, other)]
        yield
        for k in range(1, half):
            across[k - 1].wait_recv()
            block = self.whole.at[(self.row + self.rows - 2 * k) % self.rows]
            between.append(push(block, block, core_sems, k, other))
        yield
        for copy in between:
            copy.wait_recv()
        depth, count = self.weight.shape
        everything = self.whole[...].reshape(self.rows * depth, count)
        update = jnp.dot(self.left[...], everything, preferred_element_type=jnp.float32)
        weight = self.weight[...]
        change = -(SOAP_RATE * (update + WEIGHT_DECAY * weight))
        self.next[...] = weight + change if self.adds_weight else change
        for copy in across + between:
            copy.wait_send()


def same_core(row, col, rows):
    return [((row + 2 * k) % rows, col) for k in range(1, rows // 2)]


def soap_kernel(rows, cols, adds, streamed, *refs):
    row, col = lax.axis_index("row"), lax.axis_index("col")
    place = (row, col, rows, cols)
    greet(line_peers(row, col, cols) + [((row + k) % rows, col) for k in range(1, rows)])
    count = len(adds)
    shared = 1 if streamed else count
    grads, bases, refs = refs[:shared], refs[shared : 2 * shared], refs[2 * shared :]
    inputs, refs = refs[: 4 * count], refs[4 * count :]
    extra = 1 if streamed else 4
    others_in, refs = refs[:extra], refs[extra:]
    outputs, refs = refs[: 3 * count], refs[3 * count :]
    extra = 1 if streamed else 2
    others_out, refs = refs[:extra], refs[extra:]
    scratch, refs = refs[: 8 * count], refs[8 * count :]
    running = []
    loads = []
    for m, add in enumerate(adds):
        grad, basis = grads[m % shared], bases[m % shared]
        others = inputs[4 * m : 4 * m + 4]
        width = others[0].shape[1]
        if streamed:
            held, stage, load_sems = refs[:3]

            def grad_of(d, grad=grad, m=m, width=width):
                at = pl.multiple_of((streamed.index(m) * cols + d) * width, width)
                return grad.at[:, pl.ds(at, width)]

            def basis_of(d, held=held, m=m):
                return held[m, d]

            for e in range(cols):
                at = e * width
                for part in range(2):
                    lines = pl.ds(part * (width // 2), width // 2)
                    copy = pltpu.make_async_copy(
                        basis.at[m, lines, pl.ds(at, width)], stage.at[part], load_sems.at[part]
                    )
                    loads.append((copy, part, m, e))
        else:

            def grad_of(d, grad=grad):
                return grad.at[d]

            def basis_of(d, basis=basis):
                return basis[d]

        refs_of = (*others, *outputs[3 * m : 3 * m + 3], *scratch[8 * m : 8 * m + 8])
        running.append(Matrix(place, grad_of, basis_of, refs_of, add).go())
    if streamed:
        running = [running[m] for m in streamed]
        loads = [load for m in streamed for load in loads if load[2] == m]
        for copy, *unused in loads[:2]:
            copy.start()
    if streamed:
        count = others_in[0].shape[2]

        def lies_at(k):
            return others_out[0].at[:, pl.ds(pl.multiple_of(k * count, count), count)]

        running.append(swap_go(place, lambda k: others_in[0].at[k], lies_at, *refs[3:]))
    else:
        running = [
            scatter_go(place, *others_in[:3], others_out[0], *refs[:3]),
            share_go(place, others_in[3], others_out[1], *refs[3:]),
        ] + running
    for m in running:
        next(m)
    for k, (copy, slot, m, e) in enumerate(loads):
        copy.wait()
        lines = pl.ds(slot * stage.shape[1], stage.shape[1])
        held[m, e, lines] = stage[slot].astype(held.dtype)
        if k + 2 < len(loads):
            loads[k + 2][0].start()
    while running:
        running = [m for m in running if next(m, "done") != "done"]


def soap(grads, bases, matrices, adds, streamed, others, collective_id):
    rows, cols = lax.axis_size("row"), lax.axis_size("col")
    dma = pltpu.SemaphoreType.DMA
    vmem = pl.BlockSpec(memory_space=pltpu.VMEM)
    outs, scratch = [], []
    for mean, square, weight, left in matrices:
        outs += [jax.ShapeDtypeStruct(weight.shape, jnp.float32)] * 3
        block = weight.shape
        scratch += [
            pltpu.VMEM((cols, *block), left.dtype),
            pltpu.VMEM((4 * (cols - 1), *block), left.dtype),
            pltpu.VMEM(block, left.dtype),
            pltpu.VMEM(block, jnp.float32),
            pltpu.VMEM((rows, *block), left.dtype),
            dma((2, 6 * (cols - 1))),
            dma((2, rows // 2 - 1)),
            dma((2, rows // 2)),
        ]
    if streamed:
        width = matrices[0][2].shape[1]
        scratch += [
            pltpu.VMEM((len(matrices), cols, width, width), jnp.bfloat16),
            pltpu.VMEM((2, width // 2, width), jnp.float32),
            dma((2,)),
        ]
    anywhere = pl.BlockSpec(memory_space=pl.ANY)
    other_spec = anywhere if streamed else vmem
    out_specs = [vmem] * len(outs) + [other_spec] * (1 if streamed else 2)
    if streamed:
        parts, depth, count = others[0].shape
        outs += [jax.ShapeDtypeStruct((depth, parts * count), others[0].dtype)]
        scratch += [dma((2, rows - 1)), dma]
    else:
        ids, grad, base, own = others
        outs += [
            jax.ShapeDtypeStruct(base.shape, jnp.float32),
            jax.ShapeDtypeStruct((rows, cols, *own.shape), own.dtype),
        ]
        scratch += [pltpu.VMEM((cols, *grad.shape), grad.dtype)]
        scratch += [dma((2, 2 * (cols - 1))), dma((2, rows - 1))] * 2
    got = pl.pallas_call(
        functools.partial(soap_kernel, rows, cols, adds, streamed),
        out_shape=outs,
        in_specs=[vmem] * len(grads)
        + [anywhere if streamed else vmem] * len(bases)
        + [vmem] * (4 * len(matrices))
        + [other_spec] * len(others),
        out_specs=out_specs,
        scratch_shapes=scratch,
        compiler_params=pltpu.CompilerParams(
            collective_id=collective_id, has_side_effects=True, vmem_limit_bytes=VMEM_LIMIT
        ),
    )(*grads, *bases, *[part for matrix in matrices for part in matrix], *others)
    return [got[k * 3 : k * 3 + 3] for k in range(len(matrices))] + list(got[3 * len(matrices) :])


def outer_kernel(values_ref, left_ref, other_ref, *refs):
    out_ref, turned = refs[-2:]

    @pl.when(pl.program_id(0) == 0)
    def _():
        turned[...] = jnp.dot(
            values_ref[...], left_ref[...], preferred_element_type=jnp.float32
        ).astype(turned.dtype)

    out_ref[...] = lax.dot_general(
        turned[...], other_ref[...], (((0,), (0,)), ((), ())), preferred_element_type=jnp.float32
    ).astype(out_ref.dtype)


def outer(values, left_full, basis, other, block, total, at, buffer):
    tokens, width = values.shape
    specs = [
        pl.BlockSpec((tokens, width), lambda j: (0, 0)),
        pl.BlockSpec((width, width), lambda j: (0, basis)),
        pl.BlockSpec((tokens, block), lambda j: (0, j)),
    ]
    operands = [values, left_full, other]
    aliases = {}
    if buffer is not None:
        specs.append(pl.BlockSpec(memory_space=pl.ANY))
        operands.append(buffer)
        aliases = {3: 0}
    return pl.pallas_call(
        outer_kernel,
        grid=(other.shape[1] // block,),
        out_shape=jax.ShapeDtypeStruct((width, total), values.dtype),
        in_specs=specs,
        out_specs=pl.BlockSpec((width, block), lambda j: (0, at + j)),
        scratch_shapes=[pltpu.VMEM((tokens, width), values.dtype)],
        input_output_aliases=aliases,
        compiler_params=pltpu.CompilerParams(vmem_limit_bytes=VMEM_LIMIT),
        cost_estimate=pl.CostEstimate(
            flops=2 * tokens * width * (width + other.shape[1]),
            bytes_accessed=2 * width * (width + other.shape[1] + tokens),
            transcendentals=0,
        ),
    )(*operands)


def one_hot_tile(ids, first, count):
    columns = lax.broadcasted_iota(jnp.int32, (ids.shape[0], count), 1)
    return jnp.where(ids - first == columns, 1.0, 0.0).astype(jnp.bfloat16)


def lookup_kernel(
    rows, cols, ids_ref, table_ref, weight_ref, out_ref, whole_ref,
    table, taken, found, inbox, summed_ref, sems, row_sems, local_sem, col_sems, chip_sems, core_sems,
):
    row, col = lax.axis_index("row"), lax.axis_index("col")
    row_peers = [((row + k) % rows, col) for k in range(1, rows)]
    other = (row // 2 * 2 + 1 - row % 2, col)
    line = (row, col, cols)
    greet(line_peers(row, col, cols) + row_peers)
    own = pltpu.make_async_copy(weight_ref, whole_ref.at[col, row], local_sem)
    own.start()
    own.wait()
    spreading = line_spread(line, lambda d: whole_ref.at[d, row], col_sems, 0)
    next(spreading)
    features, tokens = out_ref.shape[1:]
    planes = [(k, min(128, features - 128 * k)) for k in range(table.shape[1])]

    def turn(v, carry):
        first = pl.multiple_of(v * 128, 128)
        entries = table_ref[:, pl.ds(first, 128)].astype(jnp.float32).T
        for k, lanes in planes:
            table[pl.ds(first, 128), k, pl.ds(0, lanes)] = entries[:, 128 * k : 128 * k + lanes]
        return carry

    lax.fori_loop(0, table_ref.shape[1] // 128, turn, 0)

    def look(e):
        source = e * rows

        def block(k, carry):
            start = (source + k) * tokens

            def some(j, carry):
                for u in range(LOOK_STEP):
                    at = j * LOOK_STEP + u
                    taken[at] = table[ids_ref[start + at]]
                return carry

            lax.fori_loop(0, tokens // LOOK_STEP, some, 0)
            for p, lanes in planes:
                found[e, k, pl.ds(128 * p, lanes), :] = taken[:, p, :].T[:lanes].astype(found.dtype)
            return carry

        lax.fori_loop(0, rows, block, 0)

    orders = [sorted(range(cols), key=lambda d, i=i: -abs(d - i)) for i in range(cols)]
    summing = line_sum(line, None, found, inbox, 0, sems, 0, summed_ref)
    for k in range(cols - 1):
        e = jnp.int32(orders[0][k])
        for i in range(1, cols):
            e = jnp.where(col == i, orders[i][k], e)
        look(e)
        next(summing)
        next(spreading, None)
    for unused in spreading:
        pass
    mine = whole_ref.at[:, row]
    chips = [
        push(mine, mine, (chip_sems.at[0], chip_sems.at[1]), k - 1, peer)
        for k, peer in enumerate(same_core(row, col, rows), 1)
    ]
    core = [push(mine, mine, (core_sems.at[0], core_sems.at[1]), 0, other)]
    look(col)
    for unused in summing:
        pass
    out_ref[row] = summed_ref[row]
    copies = [
        push(summed_ref.at[peer[0]], out_ref.at[row], (row_sems.at[0], row_sems.at[1]), k, peer)
        for k, peer in enumerate(row_peers)
    ]
    for k, arrived in enumerate(chips, 1):
        arrived.wait_recv()
        block = whole_ref.at[:, (row + rows - 2 * k) % rows]
        core.append(push(block, block, (core_sems.at[0], core_sems.at[1]), k, other))
    for copy in copies + core:
        copy.wait_recv()
    for copy in copies + core + chips:
        copy.wait_send()


def lookup(ids, table, weight, tokens, collective_id):
    rows, cols = lax.axis_size("row"), lax.axis_size("col")
    features, count = table.shape
    planes = -(-features // 128)
    dma = pltpu.SemaphoreType.DMA
    vmem = pl.BlockSpec(memory_space=pltpu.VMEM)
    block = (rows, features, tokens)
    return pl.pallas_call(
        functools.partial(lookup_kernel, rows, cols),
        out_shape=[
            jax.ShapeDtypeStruct(block, table.dtype),
            jax.ShapeDtypeStruct((cols, rows, *weight.shape), weight.dtype),
        ],
        in_specs=[pl.BlockSpec(memory_space=pltpu.SMEM), vmem, pl.BlockSpec(memory_space=pl.ANY)],
        out_specs=[vmem, pl.BlockSpec(memory_space=pl.ANY)],
        scratch_shapes=[
            pltpu.VMEM((count, planes, 128), jnp.float32),
            pltpu.VMEM((tokens, planes, 128), jnp.float32),
            pltpu.VMEM((cols, *block), table.dtype),
            pltpu.VMEM((2 * (cols - 1), *block), table.dtype),
            pltpu.VMEM(block, table.dtype),
            dma((2, 2 * (cols - 1))),
            dma((2, rows - 1)),
            dma,
            dma((2, 2 * (cols - 1))),
            dma((2, rows // 2 - 1)),
            dma((2, rows // 2)),
        ],
        compiler_params=pltpu.CompilerParams(
            collective_id=collective_id, has_side_effects=True, vmem_limit_bytes=VMEM_LIMIT
        ),
    )(ids, table, weight)


def scatter_go(place, ids_ref, grad_ref, base_ref, out_ref, held, sems, row_sems):
    row, col, rows, cols = place
    row_peers = [((row + k) % rows, col) for k in range(1, rows)]
    held[col, row] = grad_ref[row]
    started = [
        push(grad_ref.at[peer[0]], held.at[col, row], (row_sems.at[0], row_sems.at[1]), k, peer)
        for k, peer in enumerate(row_peers)
    ]
    tiles = out_ref.shape[1] // VOCAB_TILE

    def tile_of(d, source_ref):
        def tile(v, carry):
            first = pl.multiple_of(v * VOCAB_TILE, VOCAB_TILE)
            total = source_ref[:, pl.ds(first, VOCAB_TILE)].astype(jnp.float32)
            for k in range(rows):
                total = total + lax.dot_general(
                    held[d, k],
                    one_hot_tile(ids_ref[d, k], first, VOCAB_TILE),
                    (((1,), (0,)), ((), ())),
                    preferred_element_type=jnp.float32,
                )
            out_ref[:, pl.ds(first, VOCAB_TILE)] = total
            return carry

        return tile

    yield
    for copy in started:
        copy.wait_recv()
    spreading = line_spread((row, col, cols), lambda d: held.at[d], sems, 0)
    next(spreading)
    for first in range(0, tiles, TILES_AT_ONCE):
        lax.fori_loop(first, min(tiles, first + TILES_AT_ONCE), tile_of(col, base_ref), 0)
        next(spreading, None)
        yield
    for unused in spreading:
        yield
    for k in range(1, cols):
        for first in range(0, tiles, TILES_AT_ONCE):
            lax.fori_loop(
                first, min(tiles, first + TILES_AT_ONCE), tile_of((col + k) % cols, out_ref), 0
            )
            yield
    for copy in started:
        copy.wait_send()


def share_go(place, x_ref, out_ref, sems, row_sems):
    row, col, rows, cols = place
    out_ref[row, col] = x_ref[...]
    yield from line_spread((row, col, cols), lambda d: out_ref.at[row, d], sems, 0)
    copies = [
        push(out_ref.at[row], out_ref.at[row], (row_sems.at[0], row_sems.at[1]), k - 1, ((row + k) % rows, col))
        for k in range(1, rows)
    ]
    yield
    for copy in copies:
        copy.wait()


def gather_kernel(rows, cols, x_ref, table_ref, out_ref, swapped_ref, sems, row_sems, local_sem):
    row, col = lax.axis_index("row"), lax.axis_index("col")
    greet(line_peers(row, col, cols) + [((row + k) % rows, col) for k in range(1, rows)])
    out_ref[col] = x_ref[...]
    spreading = line_spread((row, col, cols), lambda d: out_ref.at[d], sems, 0)
    next(spreading)
    count = swapped_ref.shape[2]

    def part_of(k):
        return table_ref.at[:, pl.ds(pl.multiple_of(k * count, count), count)]

    swapping = swap_go((row, col, rows, cols), part_of, lambda k: swapped_ref.at[k], row_sems, local_sem)
    next(swapping)
    for unused in spreading:
        pass
    for unused in swapping:
        pass


def gather(value, table, collective_id):
    rows, cols = lax.axis_size("row"), lax.axis_size("col")
    dma = pltpu.SemaphoreType.DMA
    vmem, anywhere = pl.BlockSpec(memory_space=pltpu.VMEM), pl.BlockSpec(memory_space=pl.ANY)
    return pl.pallas_call(
        functools.partial(gather_kernel, rows, cols),
        out_shape=[
            jax.ShapeDtypeStruct((cols, *value.shape), value.dtype),
            jax.ShapeDtypeStruct((rows, table.shape[0], table.shape[1] // rows), table.dtype),
        ],
        in_specs=[vmem, anywhere],
        out_specs=[vmem, anywhere],
        scratch_shapes=[dma((2, 2 * (cols - 1))), dma((2, rows - 1)), dma],
        compiler_params=pltpu.CompilerParams(
            collective_id=collective_id, has_side_effects=True, vmem_limit_bytes=VMEM_LIMIT
        ),
    )(value, table)


def send(value, axis, shift):
    count = lax.axis_size(axis)
    return lax.ppermute(value, axis, [(k, (k + shift) % count) for k in range(count)])


def collect(value, axis):
    return [value] + [send(value, axis, k) for k in range(1, lax.axis_size(axis))]


def deliver(pieces, axis, sign):
    return [pieces[0]] + [send(pieces[k], axis, sign * k) for k in range(1, len(pieces))]


def summed(pieces):
    total = pieces[0].astype(jnp.float32)
    for piece in pieces[1:]:
        total = total + piece.astype(jnp.float32)
    return total


def to_absolute(pieces, index):
    count = len(pieces)
    order = [pieces[0]] + [pieces[count - k] for k in range(1, count)]
    return jnp.roll(jnp.stack(order), index, axis=0)


def pick_block(values, index, axis):
    return lax.dynamic_index_in_dim(values, index, axis, keepdims=False)


def rms_norm(values, gain_vec):
    return (
        values
        * lax.rsqrt(jnp.mean(values * values, axis=-1, keepdims=True) + NORM_EPSILON)
        * gain_vec
    )


def rotary(values, positions):
    half_width = values.shape[-1] // 2
    frequency = jnp.power(10000.0, -jnp.arange(half_width, dtype=jnp.float32) / half_width)
    angles = positions[:, None].astype(jnp.float32) * frequency[None, :]
    cosine = jnp.cos(angles)[:, None, :]
    sine_part = jnp.sin(angles)[:, None, :]
    first_half = values[..., :half_width]
    second_half = values[..., half_width:]
    return jnp.concatenate(
        [
            first_half * cosine - second_half * sine_part,
            second_half * cosine + first_half * sine_part,
        ],
        axis=-1,
    )


def swiglu(gate_part, upward):
    return jax.nn.silu(gate_part) * upward


def matmul(left_op, right_op):
    return jnp.dot(left_op, right_op, preferred_element_type=jnp.float32)


def matmul_last(left_op, right_op):
    return lax.dot_general(
        left_op, right_op, (((1,), (1,)), ((), ())), preferred_element_type=jnp.float32
    )


def matmul_first(left_op, right_op):
    return lax.dot_general(
        left_op, right_op, (((0,), (0,)), ((), ())), preferred_element_type=jnp.float32
    )


def norm_back(values, gain_vec, grad_output):
    unused, pull_back = jax.vjp(rms_norm, values, gain_vec)
    return pull_back(grad_output)


def adam_update(weight, gradient_value, moment, square_avg, decay_rate):
    moment_new = MOMENT_BETA * moment + (1.0 - MOMENT_BETA) * gradient_value
    square_new = MOMENT_BETA * square_avg + (1.0 - MOMENT_BETA) * gradient_value * gradient_value
    change = -(
        ADAM_RATE * (moment_new / (jnp.sqrt(square_new) + ADAM_EPSILON) + decay_rate * weight)
    )
    return (change, moment_new, square_new)


def per_device(
    token_ids,
    target_ids,
    loss_slots,
    valid_mask,
    prefix_lens,
    embed_table,
    norm_gains,
    qkv_weight,
    output_weight,
    mlp_weight,
    embed_mean,
    embed_square,
    gain_mean,
    gain_square,
    qkv_mean,
    qkv_square,
    out_mean,
    out_square,
    mlp_mean,
    mlp_square,
    left_bases,
    qkv_bases,
    out_bases,
    feedforward_bases,
):
    row_index = lax.axis_index("row")
    col_index = lax.axis_index("col")
    row_count = lax.axis_size("row")
    col_count = lax.axis_size("col")
    low = jnp.bfloat16
    group_tokens = token_ids.shape[0]
    pick_count = loss_slots.shape[0]
    device_tokens = group_tokens // col_count
    vocab_shard, features = embed_table.shape
    width = features * row_count
    query_width = Q_HEADS * HEAD
    kv_width = KV_HEADS * HEAD
    group_size = Q_HEADS // KV_HEADS
    scaling = HEAD ** (-0.5)
    qkv_cols, out_cols, ff_cols = qkv_weight.shape[1], output_weight.shape[1], mlp_weight.shape[2]
    vocab_part = -(-(vocab_shard + 1) // (128 * row_count)) * 128
    vocab_room = vocab_part * row_count

    ids_all = lax.all_gather(jnp.concatenate([token_ids, target_ids]), "row", axis=0)
    table_first, ids_all = lax.optimization_barrier((embed_table, ids_all))

    qkv_width, ff_width = qkv_cols * col_count, ff_cols * col_count
    mlp_low = mlp_weight.astype(low)
    mlp_full = lax.all_gather(
        jnp.concatenate([mlp_low[0], mlp_low[1], mlp_low[2]], axis=1),
        ("col", "row"),
        axis=0,
        tiled=True,
    ).reshape(col_count, width, 3 * ff_cols)
    bases_low = left_bases.astype(low)
    left_block = jnp.concatenate([bases_low[k] for k in range(5)], axis=1)
    columns = range(col_count)
    gate_full, up_full, down_full = (
        [mlp_full[c, :, k * ff_cols : (k + 1) * ff_cols] for c in columns] for k in range(3)
    )

    def by_columns(values, weights, multiply):
        return jnp.concatenate([multiply(values, weight) for weight in weights], axis=1)

    def over_columns(values, weights):
        count = values.shape[1] // col_count
        terms = [
            matmul_last(values[:, c * count : (c + 1) * count], weight)
            for c, weight in enumerate(weights)
        ]
        return functools.reduce(jnp.add, terms)

    tokens_all = ids_all[:, :group_tokens].reshape(row_count, col_count, device_tokens)
    targets_all = ids_all[:, group_tokens:].reshape(row_count * pick_count)
    local_tokens = jnp.moveaxis(tokens_all, 1, 0) - col_index * vocab_shard
    inside = (local_tokens >= 0) & (local_tokens < vocab_shard)
    local_tokens = jnp.where(inside, local_tokens, vocab_shard)
    table_low_t = table_first.astype(low).T

    def reduce_rows(values):
        return lax.psum_scatter(values, "row", scatter_dimension=0, tiled=True)

    padded = jnp.pad(table_low_t, ((0, 0), (0, vocab_room - vocab_shard)))
    attn_block = jnp.concatenate([qkv_weight.astype(low), output_weight.astype(low)], axis=1)
    found, attn_full = lookup(local_tokens.reshape(-1), padded, attn_block, device_tokens, 6)
    attn_full = attn_full.reshape(col_count, width, qkv_cols + out_cols)
    qkv_full = [attn_full[c, :, :qkv_cols] for c in columns]
    out_full = [attn_full[c, :, qkv_cols:] for c in columns]
    embedded = found.reshape(width, device_tokens).T.astype(jnp.float32)

    normed = rms_norm(embedded, norm_gains[0]).astype(low)
    project = by_columns(normed, qkv_full, matmul).astype(low)
    first_token = col_index * device_tokens
    positions = first_token + jnp.arange(device_tokens, dtype=jnp.int32)
    seq_prefix = jnp.sum(
        jnp.where(jnp.arange(prefix_lens.shape[0], dtype=jnp.int32) == row_index, prefix_lens, 0)
    )

    def rotate_here(values):
        return rotary(values, positions)

    queries_raw = project[:, :query_width].astype(jnp.float32).reshape(device_tokens, Q_HEADS, HEAD)
    keys_raw = (
        project[:, query_width : query_width + kv_width]
        .astype(jnp.float32)
        .reshape(device_tokens, KV_HEADS, HEAD)
    )
    queries = rotate_here(queries_raw).astype(low).reshape(device_tokens, KV_HEADS, group_size, HEAD)
    keys_local = rotate_here(keys_raw).astype(low).reshape(device_tokens, kv_width)
    own_pairs = jnp.concatenate([keys_local, project[:, query_width + kv_width :]], axis=1)
    keys_values, table_part = gather(own_pairs, padded, 8)
    left_block, keys_values = lax.optimization_barrier((left_block, keys_values))
    left_full = lax.all_gather(left_block, "row", axis=0, tiled=True)
    keys_values = keys_values.reshape(LEN, 2 * kv_width)
    table_part = table_part.reshape(width, vocab_part)
    attn_keys = keys_values[:, :kv_width].reshape(LEN, KV_HEADS, HEAD)
    attn_values = keys_values[:, kv_width:].reshape(LEN, KV_HEADS, HEAD)
    key_positions = jnp.arange(LEN, dtype=jnp.int32)
    allowed = (key_positions[None, :] <= positions[:, None]) | (key_positions[None, :] < seq_prefix)

    raw_scores = (
        jnp.einsum("qhgd,khd->hgqk", queries, attn_keys, preferred_element_type=jnp.float32)
        * scaling
    )
    scores = jnp.where(allowed, raw_scores, MASK_VALUE)
    largest = jnp.max(scores, axis=-1, keepdims=True)
    weights = jnp.exp(scores - largest)
    attn_probs = weights / jnp.sum(weights, axis=-1, keepdims=True)
    attended = (
        jnp.einsum(
            "hgqk,khd->qhgd",
            attn_probs.astype(low),
            attn_values,
            preferred_element_type=jnp.float32,
        )
        .astype(low)
        .reshape(device_tokens, query_width)
    )
    hidden_one = embedded + over_columns(attended, out_full)
    middle = rms_norm(hidden_one, norm_gains[1]).astype(low)
    gate_part = by_columns(middle, gate_full, matmul)
    upward = by_columns(middle, up_full, matmul)
    inner_act = swiglu(gate_part, upward).astype(low)
    hidden_two = hidden_one + over_columns(inner_act, down_full)
    final = rms_norm(hidden_two, norm_gains[2]).astype(low)

    pick_hit = (loss_slots[:, None] == positions[None, :]).astype(low)
    final_here = matmul(pick_hit, final).astype(low)
    final_pick = spread(final_here, 0)
    logits = matmul(final_pick, table_part)
    part_line = jnp.arange(vocab_part, dtype=jnp.int32)
    real = part_line < vocab_shard - row_index * vocab_part
    logits = jnp.where(real[None, :], logits, MASK_VALUE)
    local_max = jnp.max(logits, axis=-1)
    local_sum = jnp.sum(jnp.exp(logits - local_max[:, None]), axis=-1)
    part_first = col_index * vocab_shard + row_index * vocab_part
    target_hit = (part_line[None, :] == (targets_all - part_first)[:, None]) & real[None, :]
    local_target = jnp.sum(jnp.where(target_hit, logits, 0.0), axis=-1)
    own_stats = jnp.stack([local_max, local_sum, local_target]).reshape(-1, 128)
    everyone = share(own_stats, 1).reshape(row_count * col_count, 3, row_count * pick_count)
    top = jnp.max(everyone[:, 0], axis=0)
    log_total = top + jnp.log(jnp.sum(everyone[:, 1] * jnp.exp(everyone[:, 0] - top), axis=0))
    target_logit = jnp.sum(everyone[:, 2], axis=0)
    valid_count = jnp.maximum(jnp.sum(valid_mask).astype(jnp.float32), 1.0)
    row_weights = valid_mask.astype(jnp.float32) / valid_count
    loss_value = jnp.sum(row_weights * (log_total - target_logit))
    grad_logits = (
        (jnp.exp(logits - log_total[:, None]) - target_hit.astype(jnp.float32))
        * row_weights[:, None]
    ).astype(low)
    grad_pick = matmul_last(grad_logits, table_part).astype(low)
    grad_seq = fold(grad_pick, 2)
    grad_final = matmul_first(pick_hit, grad_seq)

    table_grad_part = matmul_first(final_pick, grad_logits).astype(low)
    grad_parts = table_grad_part.reshape(row_count, features, vocab_part)

    grad_two, gain_two = norm_back(hidden_two, norm_gains[2], grad_final)
    grad_two_low = grad_two.astype(low)
    ff_blocks = ff_width // ff_cols
    mlp_grad = outer(grad_two_low, left_full, 4, inner_act, ff_cols, 3 * ff_width, 0, None)
    grad_inner = by_columns(grad_two_low, down_full, matmul)
    unused, pull_swiglu = jax.vjp(swiglu, gate_part, upward)
    grad_gate, grad_up = pull_swiglu(grad_inner)
    grad_gate = grad_gate.astype(low)
    grad_up = grad_up.astype(low)
    mlp_grad = outer(middle, left_full, 2, grad_gate, ff_cols, 3 * ff_width, ff_blocks, mlp_grad)
    mlp_grad = outer(middle, left_full, 3, grad_up, ff_cols, 3 * ff_width, 2 * ff_blocks, mlp_grad)
    grad_gate, grad_up, mlp_grad = lax.optimization_barrier((grad_gate, grad_up, mlp_grad))
    mlp_rows = reduce_rows(mlp_grad)
    grad_middle = over_columns(grad_gate, gate_full) + over_columns(grad_up, up_full)
    grad_middle_in, gain_one = norm_back(hidden_one, norm_gains[1], grad_middle)
    grad_one = grad_two + grad_middle_in
    grad_one_low = grad_one.astype(low)
    attn_width = query_width + qkv_width
    attn_grad = outer(
        grad_one_low, left_full, 1, attended, SMALL_BLOCK, attn_width, 0, None
    )
    grad_attended = by_columns(grad_one_low, out_full, matmul).astype(low).reshape(
        device_tokens, KV_HEADS, group_size, HEAD
    )
    grad_probs = jnp.einsum(
        "qhgd,khd->hgqk", grad_attended, attn_values, preferred_element_type=jnp.float32
    )
    inner_sum = jnp.sum(attn_probs * grad_probs, axis=-1, keepdims=True)
    grad_scores = (attn_probs * (grad_probs - inner_sum)).astype(low)
    grad_queries = (
        jnp.einsum("hgqk,khd->qhgd", grad_scores, attn_keys, preferred_element_type=jnp.float32)
        * scaling
    )
    grad_keys = (
        jnp.einsum("hgqk,qhgd->khd", grad_scores, queries, preferred_element_type=jnp.float32)
        * scaling
    )
    grad_values = jnp.einsum(
        "hgqk,qhgd->khd",
        attn_probs.astype(low),
        grad_attended,
        preferred_element_type=jnp.float32,
    )
    grad_pairs = (
        jnp.concatenate([grad_keys.reshape(LEN, kv_width), grad_values.reshape(LEN, kv_width)], axis=1)
        .astype(low)
        .reshape(col_count, device_tokens, 2 * kv_width)
    )
    pair_pieces = [
        pick_block(grad_pairs, (col_index + col_count - k) % col_count, 0) for k in range(col_count)
    ]
    grad_pairs = summed(deliver(pair_pieces, "col", -1))
    unused, pull_query = jax.vjp(rotate_here, queries_raw)
    grad_query_raw = pull_query(grad_queries.reshape(device_tokens, Q_HEADS, HEAD))[0]
    unused, pull_key = jax.vjp(rotate_here, keys_raw)
    grad_key_raw = pull_key(grad_pairs[:, :kv_width].reshape(device_tokens, KV_HEADS, HEAD))[0]
    grad_project = jnp.concatenate(
        [
            grad_query_raw.reshape(device_tokens, query_width),
            grad_key_raw.reshape(device_tokens, kv_width),
            grad_pairs[:, kv_width:],
        ],
        axis=1,
    ).astype(low)
    attn_grad = outer(
        normed, left_full, 0, grad_project, SMALL_BLOCK, attn_width,
        query_width // SMALL_BLOCK, attn_grad,
    )
    grad_normed = over_columns(grad_project, qkv_full)
    grad_embed_in, gain_zero = norm_back(embedded, norm_gains[0], grad_normed)
    grad_embedded = (grad_one + grad_embed_in).astype(low)
    own_gains = jnp.stack([gain_zero, gain_one, gain_two]).reshape(-1, 128)
    by_feature = grad_embedded.T.reshape(row_count, features, device_tokens)
    mlp_mean_later, by_feature, attn_grad = lax.optimization_barrier((mlp_mean, by_feature, attn_grad))
    attn_rows = reduce_rows(attn_grad)
    mlp_new = soap(
        [mlp_rows],
        [feedforward_bases],
        [(mlp_mean_later[j], mlp_square[j], mlp_weight[j], bases_low[2 + j]) for j in range(3)],
        (True, True, True),
        (2, 0, 1),
        (grad_parts,),
        4,
    )
    mlp_new, table_base = mlp_new[:3], mlp_new[3]
    mlp_next, mlp_moment, mlp_scale = (
        jnp.stack([entry[k] for entry in mlp_new]) for k in range(3)
    )

    attn_rows, mlp_next = lax.optimization_barrier((attn_rows, mlp_next))

    def blocks(values):
        return jnp.moveaxis(values.reshape(values.shape[0], col_count, -1), 1, 0)

    out_new, qkv_new, table_grad, all_gains = soap(
        [blocks(attn_rows[:, :query_width]), blocks(attn_rows[:, query_width:])],
        [blocks(out_bases.astype(low)), blocks(qkv_bases.astype(low))],
        [
            (out_mean, out_square, output_weight, bases_low[1]),
            (qkv_mean, qkv_square, qkv_weight, bases_low[0]),
        ],
        (False, True),
        (),
        (local_tokens[:, :, :, None], by_feature, table_base, own_gains),
        5,
    )
    out_update, out_moment, out_scale = out_new
    qkv_next, qkv_moment, qkv_scale = qkv_new
    table_grad = table_grad[:, :vocab_shard]
    gain_grads = jnp.sum(all_gains.reshape(row_count * col_count, 3, width), axis=0)
    embed_change, embed_moment, embed_scale = adam_update(
        embed_table, table_grad.T, embed_mean, embed_square, WEIGHT_DECAY
    )
    embed_next = embed_table + embed_change
    gain_update, gain_moment, gain_scale = adam_update(
        norm_gains, gain_grads, gain_mean, gain_square, 0.0
    )
    return (
        loss_value,
        embed_next,
        embed_moment,
        embed_scale,
        gain_update,
        gain_moment,
        gain_scale,
        qkv_next,
        qkv_moment,
        qkv_scale,
        out_update,
        out_moment,
        out_scale,
        mlp_next,
        mlp_moment,
        mlp_scale,
    )


def solution(mesh):
    placed = (
        P("row"),
        P("row"),
        P("row"),
        P(),
        P(),
        P("col", "row"),
        P(),
        P("row", "col"),
        P("row", "col"),
        P(None, "row", "col"),
        P("col", "row"),
        P("col", "row"),
        P(),
        P(),
        P("row", "col"),
        P("row", "col"),
        P("row", "col"),
        P("row", "col"),
        P(None, "row", "col"),
        P(None, "row", "col"),
        P(None, "row", None),
        P("col", None),
        P("col", None),
        P(None, "col", None),
    )
    return jax.shard_map(
        per_device,
        mesh=mesh,
        in_specs=placed,
        out_specs=(
            P(),
            P("col", "row"),
            P("col", "row"),
            P("col", "row"),
            P(),
            P(),
            P(),
            P("row", "col"),
            P("row", "col"),
            P("row", "col"),
            P("row", "col"),
            P("row", "col"),
            P("row", "col"),
            P(None, "row", "col"),
            P(None, "row", "col"),
            P(None, "row", "col"),
        ),
        check_vma=False,
    )
```

```python
import functools

import jax
import jax.numpy as jnp
from jax import lax
from jax.experimental import pallas as pl
from jax.experimental.pallas import tpu as pltpu
from jax.sharding import PartitionSpec as P

Q_HEADS = 18
KV_HEADS = 6
HEAD = 64
LEN = 1024
PICK = 128


NORM_EPSILON = 1e-05
ADAM_EPSILON = 1e-08
MOMENT_BETA = 0.5
SOAP_RATE = 0.05
ADAM_RATE = 0.01
WEIGHT_DECAY = 0.1
MASK_VALUE = -1e30
MESH = pl.DeviceIdType.MESH
VMEM_LIMIT = 58 * 2**20
VOCAB_TILE = 1024
LOOK_STEP = 32
TILES_AT_ONCE = 3
SKEW = 2
SOAP_VMEM = 62 * 2**20
SMALL_BLOCK = 384


def greet(peers):
    barrier = pltpu.get_barrier_semaphore()
    for peer in peers:
        pl.semaphore_signal(barrier, inc=1, device_id=peer, device_id_type=MESH)
    pl.semaphore_wait(barrier, len(peers))


def push(source, target, sems, slot, peer):
    copy = pltpu.make_async_remote_copy(
        src_ref=source,
        dst_ref=target,
        send_sem=sems[0].at[slot],
        recv_sem=sems[1].at[slot],
        device_id=peer,
        device_id_type=MESH,
    )
    copy.start()
    return copy


def row_peer(row, col, rows, k):
    half = rows // 2
    if k < half:
        return ((row + 2 * k) % rows, col)
    return ((row // 2 * 2 + 2 * (k - half)) % rows + 1 - row % 2, col)


def share_kernel(rows, cols, x_ref, out_ref, col_send, col_recv, row_send, row_recv):
    row, col = lax.axis_index("row"), lax.axis_index("col")
    col_peers = [(row, (col + k) % cols) for k in range(1, cols)]
    row_peers = [((row + k) % rows, col) for k in range(1, rows)]
    greet(col_peers + row_peers)
    out_ref[row, col] = x_ref[...]
    copies = [
        push(out_ref.at[row, col], out_ref.at[row, col], (col_send, col_recv), k, peer)
        for k, peer in enumerate(col_peers)
    ]
    for copy in copies:
        copy.wait()
    copies = [
        push(out_ref.at[row], out_ref.at[row], (row_send, row_recv), k, peer)
        for k, peer in enumerate(row_peers)
    ]
    for copy in copies:
        copy.wait()


def share(value, collective_id):
    rows, cols = lax.axis_size("row"), lax.axis_size("col")
    return pl.pallas_call(
        functools.partial(share_kernel, rows, cols),
        out_shape=jax.ShapeDtypeStruct((rows, cols, *value.shape), value.dtype),
        in_specs=[pl.BlockSpec(memory_space=pltpu.VMEM)],
        out_specs=pl.BlockSpec(memory_space=pltpu.VMEM),
        scratch_shapes=[
            pltpu.SemaphoreType.DMA((cols - 1,)),
            pltpu.SemaphoreType.DMA((cols - 1,)),
            pltpu.SemaphoreType.DMA((rows - 1,)),
            pltpu.SemaphoreType.DMA((rows - 1,)),
        ],
        compiler_params=pltpu.CompilerParams(
            collective_id=collective_id, has_side_effects=True, vmem_limit_bytes=VMEM_LIMIT
        ),
    )(value)


def spread_kernel(
    rows, cols, x_ref, out_ref, landed, part_send, part_recv, col_send, col_recv,
    row_send, row_recv, core_send, core_recv,
):
    row, col = lax.axis_index("row"), lax.axis_index("col")
    half = rows // 2
    other = row // 2 * 2 + 1 - row % 2
    col_peers = [(row, (col + k) % cols) for k in range(1, cols)]
    row_peers = [((row + 2 * k) % rows, col) for k in range(1, half)]
    greet(col_peers + row_peers + [(other, col)])
    copies = [
        push(x_ref.at[(col + k + 1) % cols], landed.at[k], (part_send, part_recv), k, peer)
        for k, peer in enumerate(col_peers)
    ]
    for copy in copies:
        copy.wait()
    total = x_ref[col].astype(jnp.float32)
    for k in range(cols - 1):
        total = total + landed[k].astype(jnp.float32)
    out_ref[row, col] = total.astype(out_ref.dtype)
    copies = [
        push(out_ref.at[row, col], out_ref.at[row, col], (col_send, col_recv), k, peer)
        for k, peer in enumerate(col_peers)
    ]
    for copy in copies:
        copy.wait()
    across = [
        push(out_ref.at[row], out_ref.at[row], (row_send, row_recv), k, peer)
        for k, peer in enumerate(row_peers)
    ]
    between = [push(out_ref.at[row], out_ref.at[row], (core_send, core_recv), 0, (other, col))]
    for k in range(1, half):
        across[k - 1].wait_recv()
        source = (row + rows - 2 * k) % rows
        between.append(
            push(out_ref.at[source], out_ref.at[source], (core_send, core_recv), k, (other, col))
        )
    for copy in across:
        copy.wait_send()
    for copy in between:
        copy.wait()


def spread(value, collective_id):
    rows, cols = lax.axis_size("row"), lax.axis_size("col")
    count, width = value.shape
    part = count // cols
    dma = pltpu.SemaphoreType.DMA
    out = pl.pallas_call(
        functools.partial(spread_kernel, rows, cols),
        out_shape=jax.ShapeDtypeStruct((rows, cols, part, width), value.dtype),
        in_specs=[pl.BlockSpec(memory_space=pltpu.VMEM)],
        out_specs=pl.BlockSpec(memory_space=pltpu.VMEM),
        scratch_shapes=[pltpu.VMEM((cols - 1, part, width), value.dtype)]
        + [dma((cols - 1,))] * 4
        + [dma((rows // 2 - 1,))] * 2
        + [dma((rows // 2,))] * 2,
        compiler_params=pltpu.CompilerParams(
            collective_id=collective_id, has_side_effects=True, vmem_limit_bytes=VMEM_LIMIT
        ),
    )(value.reshape(cols, part, width))
    return out.reshape(rows * count, width)


def fold_kernel(
    rows, cols, x_ref, out_ref, from_core, to_row, from_row, mine, landed, core_send, core_recv,
    row_send, row_recv, part_send, part_recv, col_send, col_recv,
):
    row, col = lax.axis_index("row"), lax.axis_index("col")
    half = rows // 2
    core = row % 2
    other = row // 2 * 2 + 1 - core
    col_peers = [(row, (col + k) % cols) for k in range(1, cols)]
    row_peers = [((row + 2 * k) % rows, col) for k in range(1, half)]
    greet(col_peers + row_peers + [(other, col)])
    between = [
        push(
            x_ref.at[(row + 2 * k) % rows // 2 * 2 + 1 - core],
            from_core.at[k],
            (core_send, core_recv),
            k,
            (other, col),
        )
        for k in [*range(1, half), 0]
    ]
    across = []
    for k in range(1, half):
        between[k - 1].wait_recv()
        to_row[k - 1] = (
            x_ref[(row + 2 * k) % rows].astype(jnp.float32) + from_core[k].astype(jnp.float32)
        ).astype(to_row.dtype)
        across.append(
            push(to_row.at[k - 1], from_row.at[k - 1], (row_send, row_recv), k - 1, row_peers[k - 1])
        )
    between[half - 1].wait_recv()
    total = x_ref[row].astype(jnp.float32) + from_core[0].astype(jnp.float32)
    for k in range(half - 1):
        across[k].wait_recv()
        total = total + from_row[k].astype(jnp.float32)
    mine[...] = total.astype(mine.dtype)
    copies = [
        push(mine.at[(col + k + 1) % cols], landed.at[k], (part_send, part_recv), k, peer)
        for k, peer in enumerate(col_peers)
    ]
    for copy in copies:
        copy.wait()
    part = mine[col].astype(jnp.float32)
    for k in range(cols - 1):
        part = part + landed[k].astype(jnp.float32)
    out_ref[col] = part.astype(out_ref.dtype)
    copies = [
        push(out_ref.at[col], out_ref.at[col], (col_send, col_recv), k, peer)
        for k, peer in enumerate(col_peers)
    ]
    for copy in copies:
        copy.wait()
    for copy in between + across:
        copy.wait_send()


def fold(value, collective_id):
    rows, cols = lax.axis_size("row"), lax.axis_size("col")
    count, width = value.shape[0] // rows, value.shape[1]
    part = count // cols
    half = rows // 2
    dma = pltpu.SemaphoreType.DMA
    block = (cols, part, width)
    out = pl.pallas_call(
        functools.partial(fold_kernel, rows, cols),
        out_shape=jax.ShapeDtypeStruct(block, value.dtype),
        in_specs=[pl.BlockSpec(memory_space=pltpu.VMEM)],
        out_specs=pl.BlockSpec(memory_space=pltpu.VMEM),
        scratch_shapes=[
            pltpu.VMEM((half, *block), value.dtype),
            pltpu.VMEM((half - 1, *block), value.dtype),
            pltpu.VMEM((half - 1, *block), value.dtype),
            pltpu.VMEM(block, value.dtype),
            pltpu.VMEM((cols - 1, part, width), value.dtype),
        ]
        + [dma((half,))] * 2
        + [dma((half - 1,))] * 2
        + [dma((cols - 1,))] * 4,
        compiler_params=pltpu.CompilerParams(
            collective_id=collective_id, has_side_effects=True, vmem_limit_bytes=VMEM_LIMIT
        ),
    )(value.reshape(rows, *block))
    return out.reshape(count, width)


def line_peers(row, col, cols):
    return [(row, (col + 1) % cols), (row, (col + cols - 1) % cols)]


def line_ways(place):
    row, col, cols = place
    return ((0, col), (1, cols - 1 - col))


def line_copy(place, down, source, target, sems, at, step):
    row, col, cols = place
    slot = at + down * (cols - 1) + step
    return pltpu.make_async_remote_copy(
        src_ref=source,
        dst_ref=target,
        send_sem=sems.at[0, slot],
        recv_sem=sems.at[1, slot],
        device_id=(row, (col + (cols - 1 if down else 1)) % cols),
        device_id_type=MESH,
    )


def line_sum(place, term, work, inbox, at, sems, sem_at, result):
    row, col, cols = place

    def block_of(down, step):
        return jnp.clip(step - (cols - 1 - col) if down else cols - 1 - step + col, 0, cols - 1)

    def copy_of(down, step):
        landing = inbox.at[at + down * (cols - 1) + step]
        return line_copy(place, down, work.at[block_of(down, step)], landing, sems, sem_at, step)

    for step in range(cols - 1):
        for down, index in line_ways(place):
            d = block_of(down, step)

            @pl.when(index == 0)
            def _(d=d, down=down, step=step):
                if term is not None:
                    work[d] = term(d)
                copy_of(down, step).start()

            if step > 0:
                @pl.when((index > 0) & (index <= step))
                def _(d=d, down=down, step=step):
                    copy_of(down, step - 1).wait_recv()
                    arrived = inbox[at + down * (cols - 1) + step - 1]
                    own = work[d] if term is None else term(d)
                    work[d] = (own.astype(jnp.float32) + arrived.astype(jnp.float32)).astype(work.dtype)
                    copy_of(down, step).start()

        yield
    own = work[col] if term is None else term(col)
    result[...] = own.astype(result.dtype)
    for down, index in line_ways(place):
        @pl.when(index > 0)
        def _(down=down):
            copy_of(down, cols - 2).wait_recv()
            arrived = inbox[at + down * (cols - 1) + cols - 2]
            result[...] = (result[...].astype(jnp.float32) + arrived.astype(jnp.float32)).astype(result.dtype)

    for step in range(cols - 1):
        for down, index in line_ways(place):
            @pl.when(index <= step)
            def _(down=down, step=step):
                copy_of(down, step).wait_send()


def line_spread(place, block, sems, sem_at):
    row, col, cols = place

    def copy_of(down, step):
        lies = block(jnp.clip(col + step if down else col - step, 0, cols - 1))
        return line_copy(place, down, lies, lies, sems, sem_at, step)

    for step in range(cols):
        if step > 0:
            for down, index in line_ways(place):
                @pl.when(index >= step)
                def _(down=down, step=step):
                    copy_of(down, step - 1).wait_recv()

        if step < cols - 1:
            for down, index in line_ways(place):
                @pl.when((index >= step) & (index < cols - 1))
                def _(down=down, step=step):
                    copy_of(down, step).start()

            yield
    for step in range(cols - 1):
        for down, index in line_ways(place):
            @pl.when((index >= step) & (index < cols - 1))
            def _(down=down, step=step):
                copy_of(down, step).wait_send()


def swap_go(place, part_of, lies_at, sems, local_sem):
    row, col, rows, cols = place
    own = pltpu.make_async_copy(part_of(row), lies_at(row), local_sem)
    own.start()
    copies = [
        push(part_of((row + k) % rows), lies_at(row), (sems.at[0], sems.at[1]), k - 1, ((row + k) % rows, col))
        for k in range(1, rows)
    ]
    yield
    yield
    own.wait()
    for copy in copies:
        copy.wait()


class Matrix:
    def __init__(self, place, grad, basis, refs, adds_weight):
        self.row, self.col, self.rows, self.cols = place
        self.grad, self.basis = grad, basis
        (
            self.mean, self.square, self.weight, self.left,
            self.moment, self.scale, self.next,
            self.work, self.inbox, self.sum, self.total, self.whole, self.sems, self.row_sems, self.core_sems,
        ) = refs
        self.adds_weight = adds_weight

    def go(self):
        line = (self.row, self.col, self.cols)
        links = 2 * (self.cols - 1)
        yield from line_sum(
            line, lambda d: self.grad(d)[...], self.work, self.inbox, 0, self.sems, 0, self.sum
        )
        for d in range(self.cols):
            self.work[d] = jnp.dot(
                self.sum[...], self.basis(d), preferred_element_type=jnp.float32
            ).astype(self.work.dtype)
        yield from line_sum(line, None, self.work, self.inbox, links, self.sems, links, self.total)
        rotated = self.total[...]
        moment = MOMENT_BETA * self.mean[...] + (1.0 - MOMENT_BETA) * rotated
        scale = MOMENT_BETA * self.square[...] + (1.0 - MOMENT_BETA) * rotated * rotated
        self.moment[...] = moment
        self.scale[...] = scale
        steps = self.inbox
        steps[self.col] = (moment / (jnp.sqrt(scale) + ADAM_EPSILON)).astype(steps.dtype)
        yield from line_spread(line, lambda d: steps.at[d], self.sems, 2 * links)
        back = None
        for d in range(self.cols):
            term = lax.dot_general(
                steps[d], self.basis(d), (((1,), (1,)), ((), ())), preferred_element_type=jnp.float32
            )
            back = term if back is None else back + term
        self.whole[self.row] = back.astype(self.whole.dtype)
        half = self.rows // 2
        other = (self.row // 2 * 2 + 1 - self.row % 2, self.col)
        own = self.whole.at[self.row]
        across = [
            push(own, own, (self.row_sems.at[0], self.row_sems.at[1]), k - 1, peer)
            for k, peer in enumerate(same_core(self.row, self.col, self.rows), 1)
        ]
        core_sems = (self.core_sems.at[0], self.core_sems.at[1])
        between = [push(own, own, core_sems, 0, other)]
        yield
        for k in range(1, half):
            across[k - 1].wait_recv()
            block = self.whole.at[(self.row + self.rows - 2 * k) % self.rows]
            between.append(push(block, block, core_sems, k, other))
        yield
        for copy in between:
            copy.wait_recv()
        depth, count = self.weight.shape
        everything = self.whole[...].reshape(self.rows * depth, count)
        update = jnp.dot(self.left[...], everything, preferred_element_type=jnp.float32)
        weight = self.weight[...]
        change = -(SOAP_RATE * (update + WEIGHT_DECAY * weight))
        self.next[...] = weight + change if self.adds_weight else change
        for copy in across + between:
            copy.wait_send()


def same_core(row, col, rows):
    return [((row + 2 * k) % rows, col) for k in range(1, rows // 2)]


def soap_kernel(rows, cols, adds, streamed, *refs):
    row, col = lax.axis_index("row"), lax.axis_index("col")
    place = (row, col, rows, cols)
    greet(line_peers(row, col, cols) + [((row + k) % rows, col) for k in range(1, rows)])
    count = len(adds)

    def take(number):
        nonlocal refs
        first, refs = refs[:number], refs[number:]
        return first

    shared = 1 if streamed else count
    grads, bases, kept, lefts = take(shared), take(shared), take(3 * shared), take(count)
    others_in = take(3)
    made = take(3 * shared)
    others_out = take(3 if streamed else 1)
    scratch = take(8 * count)
    running, loads = [], []
    for m, add in enumerate(adds):
        if streamed:
            grad, basis = grads[0], bases[0]
            own = (*(ref.at[m] for ref in kept), lefts[m], *(ref.at[m] for ref in made))
            held, stage, load_sems = refs[:3]
            width = kept[0].shape[2]

            def grad_of(d, m=m):
                at = pl.multiple_of((streamed.index(m) * cols + d) * width, width)
                return grad.at[:, pl.ds(at, width)]

            def basis_of(d, m=m):
                return held[m, d]

            for e in range(cols):
                for part in range(2):
                    lines = pl.ds(part * (width // 2), width // 2)
                    copy = pltpu.make_async_copy(
                        basis.at[m, lines, pl.ds(e * width, width)], stage.at[part], load_sems.at[part]
                    )
                    loads.append((copy, part, m, e))
        else:
            own = (*kept[3 * m : 3 * m + 3], lefts[m], *made[3 * m : 3 * m + 3])

            def grad_of(d, grad=grads[m]):
                return grad.at[d]

            def basis_of(d, basis=bases[m]):
                return basis[d]

        refs_of = (*own, *scratch[8 * m : 8 * m + 8])
        running.append(Matrix(place, grad_of, basis_of, refs_of, add).go())
    beside = []
    if streamed:
        running = [running[m] for m in streamed]
        loads = [load for m in streamed for load in loads if load[2] == m]
        for copy, *unused in loads[:2]:
            copy.start()
        parts, landed = others_in[1], others_out[1]
        span = parts.shape[2]

        def lies_at(k):
            return landed.at[:, pl.ds(pl.multiple_of(k * span, span), span)]

        beside = [
            swap_go(place, lambda k: parts.at[k], lies_at, *refs[3:5]),
            reach_go(place, others_in[0], others_out[0], *refs[5:7]),
            share_go(place, others_in[2], others_out[2], *refs[7:]),
        ]
    else:
        beside = [scatter_go(place, *others_in, *others_out)]
    for m in running + beside:
        next(m)
    for k, (copy, slot, m, e) in enumerate(loads):
        copy.wait()
        lines = pl.ds(slot * stage.shape[1], stage.shape[1])
        held[m, e, lines] = stage[slot].astype(held.dtype)
        if k + 2 < len(loads):
            loads[k + 2][0].start()
    turn = 0
    while running or beside:
        left = []
        for k, m in running if turn else list(enumerate(running)):
            if turn < SKEW * k or next(m, "done") != "done":
                left.append((k, m))
        running = left
        beside = [m for m in beside if next(m, "done") != "done"]
        turn += 1


def soap(grads, bases, kept, lefts, adds, streamed, others, collective_id):
    rows, cols = lax.axis_size("row"), lax.axis_size("col")
    dma = pltpu.SemaphoreType.DMA
    vmem, anywhere = pl.BlockSpec(memory_space=pltpu.VMEM), pl.BlockSpec(memory_space=pl.ANY)
    low = lefts[0].dtype
    scratch = []
    outs = [jax.ShapeDtypeStruct(array.shape, jnp.float32) for array in kept]
    for m in range(len(adds)):
        block = kept[0].shape[1:] if streamed else kept[3 * m].shape
        scratch += [
            pltpu.VMEM((cols, *block), low),
            pltpu.VMEM((4 * (cols - 1), *block), low),
            pltpu.VMEM(block, low),
            pltpu.VMEM(block, jnp.float32),
            pltpu.VMEM((rows, *block), low),
            dma((2, 6 * (cols - 1))),
            dma((2, rows // 2 - 1)),
            dma((2, rows // 2)),
        ]
    specs = [vmem] * len(grads)
    specs += [anywhere if streamed else vmem] * len(bases)
    specs += [vmem] * (len(kept) + len(lefts))
    if streamed:
        width = kept[0].shape[2]
        grad, parts, own = others
        specs += [vmem, anywhere, vmem]
        outs += [
            jax.ShapeDtypeStruct((cols, *grad.shape), grad.dtype),
            jax.ShapeDtypeStruct((parts.shape[1], parts.shape[0] * parts.shape[2]), parts.dtype),
            jax.ShapeDtypeStruct((rows, cols, *own.shape), own.dtype),
        ]
        out_specs = [vmem] * (len(outs) - 2) + [anywhere, vmem]
        scratch += [
            pltpu.VMEM((len(adds), cols, width, width), low),
            pltpu.VMEM((2, width // 2, width), jnp.float32),
            dma((2,)),
            dma((2, rows - 1)),
            dma,
            *[dma((2, 2 * (cols - 1))), dma((2, rows - 1))] * 2,
        ]
    else:
        specs += [vmem] * 3
        outs += [jax.ShapeDtypeStruct(others[2].shape, jnp.float32)]
        out_specs = [vmem] * len(outs)
    return pl.pallas_call(
        functools.partial(soap_kernel, rows, cols, adds, streamed),
        out_shape=outs,
        in_specs=specs,
        out_specs=out_specs,
        scratch_shapes=scratch,
        compiler_params=pltpu.CompilerParams(
            collective_id=collective_id, has_side_effects=True, vmem_limit_bytes=SOAP_VMEM
        ),
    )(*grads, *bases, *kept, *lefts, *others)


def mask_bias(places_ref, keys, tokens):
    key = lax.broadcasted_iota(jnp.int32, (keys, tokens), 0)
    token = lax.broadcasted_iota(jnp.int32, (keys, tokens), 1) + places_ref[0]
    return jnp.where((key <= token) | (key < places_ref[1]), 0.0, MASK_VALUE)


def matmul_nt(left_op, right_op):
    return lax.dot_general(
        left_op, right_op, (((1,), (1,)), ((), ())), preferred_element_type=jnp.float32
    )


def matmul_tn(left_op, right_op):
    return lax.dot_general(
        left_op, right_op, (((0,), (0,)), ((), ())), preferred_element_type=jnp.float32
    )


def halves_swapped(values):
    lane = lax.broadcasted_iota(jnp.int32, values.shape, 1)
    half = HEAD // 2
    later = pltpu.roll(values, 2 * HEAD - half, 1)
    return jnp.where(lane % HEAD < half, later, pltpu.roll(values, half, 1))


def attend_kernel(
    group, places_ref, raw_ref, key_ref, value_ref, cosine_ref, sine_ref, out_ref, total_ref, query_ref, bias
):
    keys, tokens = bias.shape
    for first in range(0, raw_ref.shape[1], 2 * HEAD):
        raw = raw_ref[:, first : first + 2 * HEAD].astype(jnp.float32)
        turned = raw * cosine_ref[...] + halves_swapped(raw) * sine_ref[...]
        query_ref[:, first : first + 2 * HEAD] = turned.astype(query_ref.dtype)

    @pl.when(pl.program_id(0) == 0)
    def _():
        bias[...] = mask_bias(places_ref, keys, tokens)

    for k in range(key_ref.shape[1] // HEAD):
        key = key_ref[:, k * HEAD : (k + 1) * HEAD]
        value = value_ref[:, k * HEAD : (k + 1) * HEAD]
        for h in range(k * group, (k + 1) * group):
            query = query_ref[:, h * HEAD : (h + 1) * HEAD]
            scores = matmul_nt(key, query) * HEAD**-0.5 + bias[...]
            largest = jnp.max(scores, axis=0, keepdims=True)
            weights = jnp.exp(scores - largest)
            total = jnp.sum(weights, axis=0, keepdims=True)
            probs = (weights * (1.0 / total)).astype(query.dtype)
            out = matmul_tn(value, probs)
            out_ref[:, h * HEAD : (h + 1) * HEAD] = out.T.astype(out_ref.dtype)
            total_ref[0, h : h + 1, :] = largest + jnp.log(total)


def attend_back_kernel(
    group, places_ref, query_ref, key_ref, value_ref, cosine_ref, sine_ref, total_ref, grad_ref,
    query_out, pair_out, bias, turned
):
    keys, tokens = bias.shape

    @pl.when(pl.program_id(0) == 0)
    def _():
        bias[...] = mask_bias(places_ref, keys, tokens)

    for k in range(key_ref.shape[1] // HEAD):
        lanes = slice(k * HEAD, (k + 1) * HEAD)
        key, value = key_ref[:, lanes], value_ref[:, lanes]
        grad_key = grad_value = None
        for h in range(k * group, (k + 1) * group):
            query = query_ref[:, h * HEAD : (h + 1) * HEAD]
            grad = grad_ref[:, h * HEAD : (h + 1) * HEAD]
            scores = matmul_nt(key, query) * HEAD**-0.5 + bias[...]
            probs = jnp.exp(scores - total_ref[0, h : h + 1, :])
            grad_probs = matmul_nt(value, grad)
            inner_sum = jnp.sum(probs * grad_probs, axis=0, keepdims=True)
            grad_scores = (probs * (grad_probs - inner_sum)).astype(query.dtype)
            out = matmul_tn(key, grad_scores) * HEAD**-0.5
            turned[:, h * HEAD : (h + 1) * HEAD] = out.T
            key_term = jnp.dot(grad_scores, query, preferred_element_type=jnp.float32)
            value_term = jnp.dot(
                probs.astype(query.dtype), grad, preferred_element_type=jnp.float32
            )
            grad_key = key_term if grad_key is None else grad_key + key_term
            grad_value = value_term if grad_value is None else grad_value + value_term
        pair_out[0, :, lanes] = (grad_key * HEAD**-0.5).astype(pair_out.dtype)
        pair_out[1, :, lanes] = grad_value.astype(pair_out.dtype)
    for first in range(0, turned.shape[1], 2 * HEAD):
        grad = turned[:, first : first + 2 * HEAD]
        raw = grad * cosine_ref[...] - halves_swapped(grad) * sine_ref[...]
        query_out[:, first : first + 2 * HEAD] = raw.astype(query_out.dtype)


def attention_call(kernel, places, queries, pairs, waves, extra, extra_specs, outs, out_specs, scratch):
    tokens, keys = queries.shape[0], pairs.shape[0]
    steps = KV_HEADS // 2
    group = Q_HEADS // KV_HEADS
    wide = 2 * group * HEAD
    return pl.pallas_call(
        functools.partial(kernel, group),
        grid=(steps,),
        in_specs=[
            pl.BlockSpec(memory_space=pltpu.SMEM),
            pl.BlockSpec((tokens, wide), lambda g: (0, g)),
            pl.BlockSpec((keys, 2 * HEAD), lambda g: (0, g)),
            pl.BlockSpec((keys, 2 * HEAD), lambda g: (0, steps + g)),
            *[pl.BlockSpec((tokens, 2 * HEAD), lambda g: (0, 0))] * 2,
            *extra_specs,
        ],
        out_shape=outs,
        out_specs=out_specs,
        scratch_shapes=[pltpu.VMEM((keys, tokens), jnp.float32), *scratch],
        compiler_params=pltpu.CompilerParams(vmem_limit_bytes=VMEM_LIMIT),
        cost_estimate=pl.CostEstimate(
            flops=8 * Q_HEADS * tokens * keys * HEAD,
            bytes_accessed=8 * keys * Q_HEADS * HEAD,
            transcendentals=Q_HEADS * tokens * keys,
        ),
    )(places, queries, pairs, pairs, *waves, *extra)


def attend(places, raw, pairs, waves):
    tokens, width = raw.shape[0], Q_HEADS * HEAD
    steps = KV_HEADS // 2
    heads = Q_HEADS // steps
    return attention_call(
        attend_kernel, places, raw, pairs, waves, [], [],
        [
            jax.ShapeDtypeStruct((tokens, width), raw.dtype),
            jax.ShapeDtypeStruct((steps, heads, tokens), jnp.float32),
            jax.ShapeDtypeStruct((tokens, width), raw.dtype),
        ],
        [
            pl.BlockSpec((tokens, width // steps), lambda g: (0, g)),
            pl.BlockSpec((1, heads, tokens), lambda g: (g, 0, 0)),
            pl.BlockSpec((tokens, width // steps), lambda g: (0, g)),
        ],
        [],
    )


def attend_back(places, queries, pairs, waves, totals, grad):
    tokens, width = queries.shape
    steps = KV_HEADS // 2
    wide = pl.BlockSpec((tokens, width // steps), lambda g: (0, g))
    keys, pair_width = pairs.shape
    return attention_call(
        attend_back_kernel, places, queries, pairs, waves, [totals, grad],
        [pl.BlockSpec((1, Q_HEADS // steps, tokens), lambda g: (g, 0, 0)), wide],
        [
            jax.ShapeDtypeStruct((tokens, width), queries.dtype),
            jax.ShapeDtypeStruct((2, keys, pair_width // 2), queries.dtype),
        ],
        [wide, pl.BlockSpec((2, keys, 2 * HEAD), lambda g: (0, 0, g))],
        [pltpu.VMEM((tokens, width // steps), jnp.float32)],
    )


def outer_kernel(values_ref, left_ref, other_ref, *refs):
    out_ref, turned = refs[-2:]

    @pl.when(pl.program_id(0) == 0)
    def _():
        turned[...] = jnp.dot(
            values_ref[...], left_ref[...], preferred_element_type=jnp.float32
        ).astype(turned.dtype)

    out_ref[...] = lax.dot_general(
        turned[...], other_ref[...], (((0,), (0,)), ((), ())), preferred_element_type=jnp.float32
    ).astype(out_ref.dtype)


def outer(values, left_full, basis, other, block, total, at, buffer):
    tokens, width = values.shape
    specs = [
        pl.BlockSpec((tokens, width), lambda j: (0, 0)),
        pl.BlockSpec((width, width), lambda j: (0, basis)),
        pl.BlockSpec((tokens, block), lambda j: (0, j)),
    ]
    operands = [values, left_full, other]
    aliases = {}
    if buffer is not None:
        specs.append(pl.BlockSpec(memory_space=pl.ANY))
        operands.append(buffer)
        aliases = {3: 0}
    return pl.pallas_call(
        outer_kernel,
        grid=(other.shape[1] // block,),
        out_shape=jax.ShapeDtypeStruct((width, total), values.dtype),
        in_specs=specs,
        out_specs=pl.BlockSpec((width, block), lambda j: (0, at + j)),
        scratch_shapes=[pltpu.VMEM((tokens, width), values.dtype)],
        input_output_aliases=aliases,
        compiler_params=pltpu.CompilerParams(vmem_limit_bytes=VMEM_LIMIT),
        cost_estimate=pl.CostEstimate(
            flops=2 * tokens * width * (width + other.shape[1]),
            bytes_accessed=2 * width * (width + other.shape[1] + tokens),
            transcendentals=0,
        ),
    )(*operands)


def one_hot_tile(ids, first, count):
    columns = lax.broadcasted_iota(jnp.int32, (ids.shape[0], count), 1)
    return jnp.where(ids - first == columns, 1.0, 0.0).astype(jnp.bfloat16)


def lookup_kernel(
    rows, cols, ids_ref, table_ref, weight_ref, out_ref, whole_ref,
    table, taken, found, inbox, summed_ref, sems, row_sems, local_sem, col_sems, chip_sems, core_sems,
):
    row, col = lax.axis_index("row"), lax.axis_index("col")
    row_peers = [((row + k) % rows, col) for k in range(1, rows)]
    other = (row // 2 * 2 + 1 - row % 2, col)
    line = (row, col, cols)
    greet(line_peers(row, col, cols) + row_peers)
    own = pltpu.make_async_copy(weight_ref, whole_ref.at[col, row], local_sem)
    own.start()
    own.wait()
    spreading = line_spread(line, lambda d: whole_ref.at[d, row], col_sems, 0)
    next(spreading)
    features, tokens = out_ref.shape[1:]
    planes = [(k, min(128, features - 128 * k)) for k in range(table.shape[1])]

    def turn(v, carry):
        first = pl.multiple_of(v * 128, 128)
        entries = table_ref[:, pl.ds(first, 128)].astype(jnp.float32).T
        for k, lanes in planes:
            table[pl.ds(first, 128), k, pl.ds(0, lanes)] = entries[:, 128 * k : 128 * k + lanes]
        return carry

    lax.fori_loop(0, table_ref.shape[1] // 128, turn, 0)

    def look(e):
        source = e * rows

        def block(k, carry):
            start = (source + k) * tokens

            def some(j, carry):
                for u in range(LOOK_STEP):
                    at = j * LOOK_STEP + u
                    taken[at] = table[ids_ref[start + at]]
                return carry

            lax.fori_loop(0, tokens // LOOK_STEP, some, 0)
            for p, lanes in planes:
                found[e, k, pl.ds(128 * p, lanes), :] = taken[:, p, :].T[:lanes].astype(found.dtype)
            return carry

        lax.fori_loop(0, rows, block, 0)

    orders = [sorted(range(cols), key=lambda d, i=i: -abs(d - i)) for i in range(cols)]
    summing = line_sum(line, None, found, inbox, 0, sems, 0, summed_ref)
    for k in range(cols - 1):
        e = jnp.int32(orders[0][k])
        for i in range(1, cols):
            e = jnp.where(col == i, orders[i][k], e)
        look(e)
        next(summing)
        next(spreading, None)
    for unused in spreading:
        pass
    mine = whole_ref.at[:, row]
    chips = [
        push(mine, mine, (chip_sems.at[0], chip_sems.at[1]), k - 1, peer)
        for k, peer in enumerate(same_core(row, col, rows), 1)
    ]
    core = [push(mine, mine, (core_sems.at[0], core_sems.at[1]), 0, other)]
    look(col)
    for unused in summing:
        pass
    out_ref[row] = summed_ref[row]
    copies = [
        push(summed_ref.at[peer[0]], out_ref.at[row], (row_sems.at[0], row_sems.at[1]), k, peer)
        for k, peer in enumerate(row_peers)
    ]
    for k, arrived in enumerate(chips, 1):
        arrived.wait_recv()
        block = whole_ref.at[:, (row + rows - 2 * k) % rows]
        core.append(push(block, block, (core_sems.at[0], core_sems.at[1]), k, other))
    for copy in copies + core:
        copy.wait_recv()
    for copy in copies + core + chips:
        copy.wait_send()


def lookup(ids, table, weight, tokens, collective_id):
    rows, cols = lax.axis_size("row"), lax.axis_size("col")
    features, count = table.shape
    planes = -(-features // 128)
    dma = pltpu.SemaphoreType.DMA
    vmem = pl.BlockSpec(memory_space=pltpu.VMEM)
    block = (rows, features, tokens)
    return pl.pallas_call(
        functools.partial(lookup_kernel, rows, cols),
        out_shape=[
            jax.ShapeDtypeStruct(block, table.dtype),
            jax.ShapeDtypeStruct((cols, rows, *weight.shape), weight.dtype),
        ],
        in_specs=[pl.BlockSpec(memory_space=pltpu.SMEM), vmem, pl.BlockSpec(memory_space=pl.ANY)],
        out_specs=[vmem, pl.BlockSpec(memory_space=pl.ANY)],
        scratch_shapes=[
            pltpu.VMEM((count, planes, 128), jnp.float32),
            pltpu.VMEM((tokens, planes, 128), jnp.float32),
            pltpu.VMEM((cols, *block), table.dtype),
            pltpu.VMEM((2 * (cols - 1), *block), table.dtype),
            pltpu.VMEM(block, table.dtype),
            dma((2, 2 * (cols - 1))),
            dma((2, rows - 1)),
            dma,
            dma((2, 2 * (cols - 1))),
            dma((2, rows // 2 - 1)),
            dma((2, rows // 2)),
        ],
        compiler_params=pltpu.CompilerParams(
            collective_id=collective_id, has_side_effects=True, vmem_limit_bytes=VMEM_LIMIT
        ),
    )(ids, table, weight)


def reach_go(place, grad_ref, held, sems, row_sems):
    row, col, rows, cols = place
    row_peers = [((row + k) % rows, col) for k in range(1, rows)]
    held[col, row] = grad_ref[row]
    started = [
        push(grad_ref.at[peer[0]], held.at[col, row], (row_sems.at[0], row_sems.at[1]), k, peer)
        for k, peer in enumerate(row_peers)
    ]
    yield
    for copy in started:
        copy.wait_recv()
    yield from line_spread((row, col, cols), lambda d: held.at[d], sems, 0)
    for copy in started:
        copy.wait_send()


def scatter_go(place, ids_ref, held_ref, base_ref, out_ref):
    row, col, rows, cols = place
    tiles = out_ref.shape[1] // VOCAB_TILE

    def tile_of(d, source_ref):
        def tile(v, carry):
            first = pl.multiple_of(v * VOCAB_TILE, VOCAB_TILE)
            total = source_ref[:, pl.ds(first, VOCAB_TILE)].astype(jnp.float32)
            for k in range(rows):
                total = total + lax.dot_general(
                    held_ref[d, k],
                    one_hot_tile(ids_ref[d, k], first, VOCAB_TILE),
                    (((1,), (0,)), ((), ())),
                    preferred_element_type=jnp.float32,
                )
            out_ref[:, pl.ds(first, VOCAB_TILE)] = total
            return carry

        return tile

    yield
    for d in range(cols):
        for first in range(0, tiles, TILES_AT_ONCE):
            last = min(tiles, first + TILES_AT_ONCE)
            lax.fori_loop(first, last, tile_of(d, out_ref if d else base_ref), 0)
            yield


def share_go(place, x_ref, out_ref, sems, row_sems):
    row, col, rows, cols = place
    out_ref[row, col] = x_ref[...]
    yield from line_spread((row, col, cols), lambda d: out_ref.at[row, d], sems, 0)
    copies = [
        push(out_ref.at[row], out_ref.at[row], (row_sems.at[0], row_sems.at[1]), k - 1, ((row + k) % rows, col))
        for k in range(1, rows)
    ]
    yield
    for copy in copies:
        copy.wait()


def gather_kernel(rows, cols, x_ref, table_ref, out_ref, swapped_ref, sems, row_sems, local_sem):
    row, col = lax.axis_index("row"), lax.axis_index("col")
    greet(line_peers(row, col, cols) + [((row + k) % rows, col) for k in range(1, rows)])
    out_ref[col] = x_ref[...]
    spreading = line_spread((row, col, cols), lambda d: out_ref.at[d], sems, 0)
    next(spreading)
    count = swapped_ref.shape[2]

    def part_of(k):
        return table_ref.at[:, pl.ds(pl.multiple_of(k * count, count), count)]

    swapping = swap_go((row, col, rows, cols), part_of, lambda k: swapped_ref.at[k], row_sems, local_sem)
    next(swapping)
    for unused in spreading:
        pass
    for unused in swapping:
        pass


def gather(value, table, collective_id):
    rows, cols = lax.axis_size("row"), lax.axis_size("col")
    dma = pltpu.SemaphoreType.DMA
    vmem, anywhere = pl.BlockSpec(memory_space=pltpu.VMEM), pl.BlockSpec(memory_space=pl.ANY)
    return pl.pallas_call(
        functools.partial(gather_kernel, rows, cols),
        out_shape=[
            jax.ShapeDtypeStruct((cols, *value.shape), value.dtype),
            jax.ShapeDtypeStruct((rows, table.shape[0], table.shape[1] // rows), table.dtype),
        ],
        in_specs=[vmem, anywhere],
        out_specs=[vmem, anywhere],
        scratch_shapes=[dma((2, 2 * (cols - 1))), dma((2, rows - 1)), dma],
        compiler_params=pltpu.CompilerParams(
            collective_id=collective_id, has_side_effects=True, vmem_limit_bytes=VMEM_LIMIT
        ),
    )(value, table)


def send(value, axis, shift):
    count = lax.axis_size(axis)
    return lax.ppermute(value, axis, [(k, (k + shift) % count) for k in range(count)])


def collect(value, axis):
    return [value] + [send(value, axis, k) for k in range(1, lax.axis_size(axis))]


def deliver(pieces, axis, sign):
    return [pieces[0]] + [send(pieces[k], axis, sign * k) for k in range(1, len(pieces))]


def summed(pieces):
    total = pieces[0].astype(jnp.float32)
    for piece in pieces[1:]:
        total = total + piece.astype(jnp.float32)
    return total


def to_absolute(pieces, index):
    count = len(pieces)
    order = [pieces[0]] + [pieces[count - k] for k in range(1, count)]
    return jnp.roll(jnp.stack(order), index, axis=0)


def pick_block(values, index, axis):
    return lax.dynamic_index_in_dim(values, index, axis, keepdims=False)


def rms_norm(values, gain_vec):
    return (
        values
        * lax.rsqrt(jnp.mean(values * values, axis=-1, keepdims=True) + NORM_EPSILON)
        * gain_vec
    )


def rotary(values, positions):
    half_width = values.shape[-1] // 2
    frequency = jnp.power(10000.0, -jnp.arange(half_width, dtype=jnp.float32) / half_width)
    angles = positions[:, None].astype(jnp.float32) * frequency[None, :]
    cosine = jnp.cos(angles)[:, None, :]
    sine_part = jnp.sin(angles)[:, None, :]
    first_half = values[..., :half_width]
    second_half = values[..., half_width:]
    return jnp.concatenate(
        [
            first_half * cosine - second_half * sine_part,
            second_half * cosine + first_half * sine_part,
        ],
        axis=-1,
    )


def swiglu(gate_part, upward):
    return jax.nn.silu(gate_part) * upward


def matmul(left_op, right_op):
    return jnp.dot(left_op, right_op, preferred_element_type=jnp.float32)


def matmul_last(left_op, right_op):
    return lax.dot_general(
        left_op, right_op, (((1,), (1,)), ((), ())), preferred_element_type=jnp.float32
    )


def matmul_first(left_op, right_op):
    return lax.dot_general(
        left_op, right_op, (((0,), (0,)), ((), ())), preferred_element_type=jnp.float32
    )


def norm_back(values, gain_vec, grad_output):
    unused, pull_back = jax.vjp(rms_norm, values, gain_vec)
    return pull_back(grad_output)


def adam_update(weight, gradient_value, moment, square_avg, decay_rate):
    moment_new = MOMENT_BETA * moment + (1.0 - MOMENT_BETA) * gradient_value
    square_new = MOMENT_BETA * square_avg + (1.0 - MOMENT_BETA) * gradient_value * gradient_value
    change = -(
        ADAM_RATE * (moment_new / (jnp.sqrt(square_new) + ADAM_EPSILON) + decay_rate * weight)
    )
    return (change, moment_new, square_new)


def per_device(
    token_ids,
    target_ids,
    loss_slots,
    valid_mask,
    prefix_lens,
    embed_table,
    norm_gains,
    qkv_weight,
    output_weight,
    mlp_weight,
    embed_mean,
    embed_square,
    gain_mean,
    gain_square,
    qkv_mean,
    qkv_square,
    out_mean,
    out_square,
    mlp_mean,
    mlp_square,
    left_bases,
    qkv_bases,
    out_bases,
    feedforward_bases,
):
    row_index = lax.axis_index("row")
    col_index = lax.axis_index("col")
    row_count = lax.axis_size("row")
    col_count = lax.axis_size("col")
    low = jnp.bfloat16
    group_tokens = token_ids.shape[0]
    pick_count = loss_slots.shape[0]
    device_tokens = group_tokens // col_count
    vocab_shard, features = embed_table.shape
    width = features * row_count
    query_width = Q_HEADS * HEAD
    kv_width = KV_HEADS * HEAD
    qkv_cols, out_cols, ff_cols = qkv_weight.shape[1], output_weight.shape[1], mlp_weight.shape[2]
    vocab_part = -(-(vocab_shard + 1) // (128 * row_count)) * 128
    vocab_room = vocab_part * row_count

    ids_all = lax.all_gather(jnp.concatenate([token_ids, target_ids]), "row", axis=0)
    table_first, ids_all = lax.optimization_barrier((embed_table, ids_all))

    qkv_width, ff_width = qkv_cols * col_count, ff_cols * col_count
    mlp_low = mlp_weight.astype(low)
    mlp_full = lax.all_gather(
        jnp.concatenate([mlp_low[0], mlp_low[1], mlp_low[2]], axis=1),
        ("col", "row"),
        axis=0,
        tiled=True,
    ).reshape(col_count, width, 3 * ff_cols)
    bases_low = left_bases.astype(low)
    left_block = jnp.concatenate([bases_low[k] for k in range(5)], axis=1)
    columns = range(col_count)
    gate_full, up_full, down_full = (
        [mlp_full[c, :, k * ff_cols : (k + 1) * ff_cols] for c in columns] for k in range(3)
    )

    def by_columns(values, weights, multiply):
        return jnp.concatenate([multiply(values, weight) for weight in weights], axis=1)

    def over_columns(values, weights):
        count = values.shape[1] // col_count
        terms = [
            matmul_last(values[:, c * count : (c + 1) * count], weight)
            for c, weight in enumerate(weights)
        ]
        return functools.reduce(jnp.add, terms)

    tokens_all = ids_all[:, :group_tokens].reshape(row_count, col_count, device_tokens)
    targets_all = ids_all[:, group_tokens:].reshape(row_count * pick_count)
    local_tokens = jnp.moveaxis(tokens_all, 1, 0) - col_index * vocab_shard
    inside = (local_tokens >= 0) & (local_tokens < vocab_shard)
    local_tokens = jnp.where(inside, local_tokens, vocab_shard)
    table_low_t = table_first.astype(low).T

    def reduce_rows(values):
        return lax.psum_scatter(values, "row", scatter_dimension=0, tiled=True)

    padded = jnp.pad(table_low_t, ((0, 0), (0, vocab_room - vocab_shard)))
    attn_block = jnp.concatenate([qkv_weight.astype(low), output_weight.astype(low)], axis=1)
    found, attn_full = lookup(local_tokens.reshape(-1), padded, attn_block, device_tokens, 6)
    attn_full = attn_full.reshape(col_count, width, qkv_cols + out_cols)
    qkv_full = [attn_full[c, :, :qkv_cols] for c in columns]
    out_full = [attn_full[c, :, qkv_cols:] for c in columns]
    embedded = found.reshape(width, device_tokens).T.astype(jnp.float32)

    normed = rms_norm(embedded, norm_gains[0]).astype(low)
    project = by_columns(normed, qkv_full, matmul).astype(low)
    first_token = col_index * device_tokens
    positions = first_token + jnp.arange(device_tokens, dtype=jnp.int32)
    seq_prefix = jnp.sum(
        jnp.where(jnp.arange(prefix_lens.shape[0], dtype=jnp.int32) == row_index, prefix_lens, 0)
    )

    def rotate_here(values):
        return rotary(values, positions)

    keys_raw = (
        project[:, query_width : query_width + kv_width]
        .astype(jnp.float32)
        .reshape(device_tokens, KV_HEADS, HEAD)
    )
    keys_local = rotate_here(keys_raw).astype(low).reshape(device_tokens, kv_width)
    own_pairs = jnp.concatenate([keys_local, project[:, query_width + kv_width :]], axis=1)
    keys_values, table_part = gather(own_pairs, padded, 8)
    left_block, keys_values = lax.optimization_barrier((left_block, keys_values))
    left_full = lax.all_gather(left_block, "row", axis=0, tiled=True)
    keys_values = keys_values.reshape(LEN, 2 * kv_width)
    table_part = table_part.reshape(width, vocab_part)
    places = jnp.stack([first_token, seq_prefix])
    frequency = jnp.power(10000.0, -jnp.arange(HEAD // 2, dtype=jnp.float32) / (HEAD // 2))
    angles = positions[:, None].astype(jnp.float32) * frequency[None, :]
    sine = jnp.sin(angles)
    waves = [
        jnp.tile(jnp.cos(angles), (1, 4)),
        jnp.tile(jnp.concatenate([-sine, sine], axis=1), (1, 2)),
    ]
    attended, totals, queries = attend(places, project, keys_values, waves)
    hidden_one = embedded + over_columns(attended, out_full)
    middle = rms_norm(hidden_one, norm_gains[1]).astype(low)
    gate_part = by_columns(middle, gate_full, matmul)
    upward = by_columns(middle, up_full, matmul)
    inner_act = swiglu(gate_part, upward).astype(low)
    hidden_two = hidden_one + over_columns(inner_act, down_full)
    final = rms_norm(hidden_two, norm_gains[2]).astype(low)

    pick_hit = (loss_slots[:, None] == positions[None, :]).astype(low)
    final_here = matmul(pick_hit, final).astype(low)
    final_pick = spread(final_here, 0)
    logits = matmul(final_pick, table_part)
    part_line = jnp.arange(vocab_part, dtype=jnp.int32)
    real = part_line < vocab_shard - row_index * vocab_part
    logits = jnp.where(real[None, :], logits, MASK_VALUE)
    local_max = jnp.max(logits, axis=-1)
    local_sum = jnp.sum(jnp.exp(logits - local_max[:, None]), axis=-1)
    part_first = col_index * vocab_shard + row_index * vocab_part
    target_hit = (part_line[None, :] == (targets_all - part_first)[:, None]) & real[None, :]
    local_target = jnp.sum(jnp.where(target_hit, logits, 0.0), axis=-1)
    own_stats = jnp.stack([local_max, local_sum, local_target]).reshape(-1, 128)
    everyone = share(own_stats, 1).reshape(row_count * col_count, 3, row_count * pick_count)
    top = jnp.max(everyone[:, 0], axis=0)
    log_total = top + jnp.log(jnp.sum(everyone[:, 1] * jnp.exp(everyone[:, 0] - top), axis=0))
    target_logit = jnp.sum(everyone[:, 2], axis=0)
    valid_count = jnp.maximum(jnp.sum(valid_mask).astype(jnp.float32), 1.0)
    row_weights = valid_mask.astype(jnp.float32) / valid_count
    loss_value = jnp.sum(row_weights * (log_total - target_logit))
    grad_logits = (
        (jnp.exp(logits - log_total[:, None]) - target_hit.astype(jnp.float32))
        * row_weights[:, None]
    ).astype(low)
    grad_pick = matmul_last(grad_logits, table_part).astype(low)
    grad_seq = fold(grad_pick, 2)
    grad_final = matmul_first(pick_hit, grad_seq)

    table_grad_part = matmul_first(final_pick, grad_logits).astype(low)
    grad_parts = table_grad_part.reshape(row_count, features, vocab_part)

    grad_two, gain_two = norm_back(hidden_two, norm_gains[2], grad_final)
    grad_two_low = grad_two.astype(low)
    ff_blocks = ff_width // ff_cols
    mlp_grad = outer(grad_two_low, left_full, 4, inner_act, ff_cols, 3 * ff_width, 0, None)
    grad_inner = by_columns(grad_two_low, down_full, matmul)
    unused, pull_swiglu = jax.vjp(swiglu, gate_part, upward)
    grad_gate, grad_up = pull_swiglu(grad_inner)
    grad_gate = grad_gate.astype(low)
    grad_up = grad_up.astype(low)
    mlp_grad = outer(middle, left_full, 2, grad_gate, ff_cols, 3 * ff_width, ff_blocks, mlp_grad)
    mlp_grad = outer(middle, left_full, 3, grad_up, ff_cols, 3 * ff_width, 2 * ff_blocks, mlp_grad)
    grad_gate, grad_up, mlp_grad = lax.optimization_barrier((grad_gate, grad_up, mlp_grad))
    mlp_rows = reduce_rows(mlp_grad)
    grad_middle = over_columns(grad_gate, gate_full) + over_columns(grad_up, up_full)
    grad_middle_in, gain_one = norm_back(hidden_one, norm_gains[1], grad_middle)
    grad_one = grad_two + grad_middle_in
    grad_one_low = grad_one.astype(low)
    attn_width = query_width + qkv_width
    attn_grad = outer(
        grad_one_low, left_full, 1, attended, SMALL_BLOCK, attn_width, 0, None
    )
    grad_attended = by_columns(grad_one_low, out_full, matmul).astype(low)
    grad_query_raw, grad_pairs = attend_back(
        places, queries, keys_values, waves, totals, grad_attended
    )
    grad_pairs = grad_pairs.reshape(2, col_count, device_tokens, kv_width)
    pair_pieces = [
        pick_block(grad_pairs, (col_index + col_count - k) % col_count, 1) for k in range(col_count)
    ]
    grad_pairs = summed(deliver(pair_pieces, "col", -1))
    unused, pull_key = jax.vjp(rotate_here, keys_raw)
    grad_key_raw = pull_key(grad_pairs[0].reshape(device_tokens, KV_HEADS, HEAD))[0]
    grad_project = jnp.concatenate(
        [
            grad_query_raw,
            grad_key_raw.reshape(device_tokens, kv_width).astype(low),
            grad_pairs[1].astype(low),
        ],
        axis=1,
    )
    attn_grad = outer(
        normed, left_full, 0, grad_project, SMALL_BLOCK, attn_width,
        query_width // SMALL_BLOCK, attn_grad,
    )
    grad_normed = over_columns(grad_project, qkv_full)
    grad_embed_in, gain_zero = norm_back(embedded, norm_gains[0], grad_normed)
    grad_embedded = (grad_one + grad_embed_in).astype(low)
    own_gains = jnp.stack([gain_zero, gain_one, gain_two]).reshape(-1, 128)
    by_feature = grad_embedded.T.reshape(row_count, features, device_tokens)
    mlp_mean_later, by_feature, attn_grad = lax.optimization_barrier((mlp_mean, by_feature, attn_grad))
    attn_rows = reduce_rows(attn_grad)
    mlp_moment, mlp_scale, mlp_next, token_grads, table_base, all_gains = soap(
        [mlp_rows],
        [feedforward_bases],
        [mlp_mean_later, mlp_square, mlp_weight],
        [bases_low[2 + j] for j in range(3)],
        (True, True, True),
        (2, 0, 1),
        (by_feature, grad_parts, own_gains),
        4,
    )
    attn_rows, mlp_next = lax.optimization_barrier((attn_rows, mlp_next))

    def blocks(values):
        return jnp.moveaxis(values.reshape(values.shape[0], col_count, -1), 1, 0)

    out_moment, out_scale, out_update, qkv_moment, qkv_scale, qkv_next, table_grad = soap(
        [blocks(attn_rows[:, :query_width]), blocks(attn_rows[:, query_width:])],
        [blocks(out_bases.astype(low)), blocks(qkv_bases.astype(low))],
        [out_mean, out_square, output_weight, qkv_mean, qkv_square, qkv_weight],
        [bases_low[1], bases_low[0]],
        (False, True),
        (),
        (local_tokens[:, :, :, None], token_grads, table_base),
        5,
    )
    table_grad = table_grad[:, :vocab_shard]
    gain_grads = jnp.sum(all_gains.reshape(row_count * col_count, 3, width), axis=0)
    embed_change, embed_moment, embed_scale = adam_update(
        embed_table, table_grad.T, embed_mean, embed_square, WEIGHT_DECAY
    )
    embed_next = embed_table + embed_change
    gain_update, gain_moment, gain_scale = adam_update(
        norm_gains, gain_grads, gain_mean, gain_square, 0.0
    )
    return (
        loss_value,
        embed_next,
        embed_moment,
        embed_scale,
        gain_update,
        gain_moment,
        gain_scale,
        qkv_next,
        qkv_moment,
        qkv_scale,
        out_update,
        out_moment,
        out_scale,
        mlp_next,
        mlp_moment,
        mlp_scale,
    )


def solution(mesh):
    placed = (
        P("row"),
        P("row"),
        P("row"),
        P(),
        P(),
        P("col", "row"),
        P(),
        P("row", "col"),
        P("row", "col"),
        P(None, "row", "col"),
        P("col", "row"),
        P("col", "row"),
        P(),
        P(),
        P("row", "col"),
        P("row", "col"),
        P("row", "col"),
        P("row", "col"),
        P(None, "row", "col"),
        P(None, "row", "col"),
        P(None, "row", None),
        P("col", None),
        P("col", None),
        P(None, "col", None),
    )
    return jax.shard_map(
        per_device,
        mesh=mesh,
        in_specs=placed,
        out_specs=(
            P(),
            P("col", "row"),
            P("col", "row"),
            P("col", "row"),
            P(),
            P(),
            P(),
            P("row", "col"),
            P("row", "col"),
            P("row", "col"),
            P("row", "col"),
            P("row", "col"),
            P("row", "col"),
            P(None, "row", "col"),
            P(None, "row", "col"),
            P(None, "row", "col"),
        ),
        check_vma=False,
    )
```

```python
import functools

import jax
import jax.numpy as jnp
from jax import lax
from jax.experimental import pallas as pl
from jax.experimental.pallas import tpu as pltpu
from jax.sharding import PartitionSpec as P

Q_HEADS = 18
KV_HEADS = 6
HEAD = 64
LEN = 1024
PICK = 128


NORM_EPSILON = 1e-05
ADAM_EPSILON = 1e-08
MOMENT_BETA = 0.5
SOAP_RATE = 0.05
ADAM_RATE = 0.01
WEIGHT_DECAY = 0.1
MASK_VALUE = -1e30
MESH = pl.DeviceIdType.MESH
VMEM_LIMIT = 58 * 2**20
VOCAB_TILE = 1024
LOOK_STEP = 32
TILES_AT_ONCE = 3
SKEW = 2
SOAP_VMEM = 62 * 2**20
SMALL_BLOCK = 384


def greet(peers):
    barrier = pltpu.get_barrier_semaphore()
    for peer in peers:
        pl.semaphore_signal(barrier, inc=1, device_id=peer, device_id_type=MESH)
    pl.semaphore_wait(barrier, len(peers))


def push(source, target, sems, slot, peer):
    copy = pltpu.make_async_remote_copy(
        src_ref=source,
        dst_ref=target,
        send_sem=sems[0].at[slot],
        recv_sem=sems[1].at[slot],
        device_id=peer,
        device_id_type=MESH,
    )
    copy.start()
    return copy


def row_peer(row, col, rows, k):
    half = rows // 2
    if k < half:
        return ((row + 2 * k) % rows, col)
    return ((row // 2 * 2 + 2 * (k - half)) % rows + 1 - row % 2, col)


def share_kernel(rows, cols, x_ref, out_ref, col_send, col_recv, row_send, row_recv):
    row, col = lax.axis_index("row"), lax.axis_index("col")
    col_peers = [(row, (col + k) % cols) for k in range(1, cols)]
    row_peers = [((row + k) % rows, col) for k in range(1, rows)]
    greet(col_peers + row_peers)
    out_ref[row, col] = x_ref[...]
    copies = [
        push(out_ref.at[row, col], out_ref.at[row, col], (col_send, col_recv), k, peer)
        for k, peer in enumerate(col_peers)
    ]
    for copy in copies:
        copy.wait()
    copies = [
        push(out_ref.at[row], out_ref.at[row], (row_send, row_recv), k, peer)
        for k, peer in enumerate(row_peers)
    ]
    for copy in copies:
        copy.wait()


def share(value, collective_id):
    rows, cols = lax.axis_size("row"), lax.axis_size("col")
    return pl.pallas_call(
        functools.partial(share_kernel, rows, cols),
        out_shape=jax.ShapeDtypeStruct((rows, cols, *value.shape), value.dtype),
        in_specs=[pl.BlockSpec(memory_space=pltpu.VMEM)],
        out_specs=pl.BlockSpec(memory_space=pltpu.VMEM),
        scratch_shapes=[
            pltpu.SemaphoreType.DMA((cols - 1,)),
            pltpu.SemaphoreType.DMA((cols - 1,)),
            pltpu.SemaphoreType.DMA((rows - 1,)),
            pltpu.SemaphoreType.DMA((rows - 1,)),
        ],
        compiler_params=pltpu.CompilerParams(
            collective_id=collective_id, has_side_effects=True, vmem_limit_bytes=VMEM_LIMIT
        ),
    )(value)


def spread_kernel(
    rows, cols, x_ref, out_ref, landed, part_send, part_recv, col_send, col_recv,
    row_send, row_recv, core_send, core_recv,
):
    row, col = lax.axis_index("row"), lax.axis_index("col")
    half = rows // 2
    other = row // 2 * 2 + 1 - row % 2
    col_peers = [(row, (col + k) % cols) for k in range(1, cols)]
    row_peers = [((row + 2 * k) % rows, col) for k in range(1, half)]
    greet(col_peers + row_peers + [(other, col)])
    copies = [
        push(x_ref.at[(col + k + 1) % cols], landed.at[k], (part_send, part_recv), k, peer)
        for k, peer in enumerate(col_peers)
    ]
    for copy in copies:
        copy.wait()
    total = x_ref[col].astype(jnp.float32)
    for k in range(cols - 1):
        total = total + landed[k].astype(jnp.float32)
    out_ref[row, col] = total.astype(out_ref.dtype)
    copies = [
        push(out_ref.at[row, col], out_ref.at[row, col], (col_send, col_recv), k, peer)
        for k, peer in enumerate(col_peers)
    ]
    for copy in copies:
        copy.wait()
    across = [
        push(out_ref.at[row], out_ref.at[row], (row_send, row_recv), k, peer)
        for k, peer in enumerate(row_peers)
    ]
    between = [push(out_ref.at[row], out_ref.at[row], (core_send, core_recv), 0, (other, col))]
    for k in range(1, half):
        across[k - 1].wait_recv()
        source = (row + rows - 2 * k) % rows
        between.append(
            push(out_ref.at[source], out_ref.at[source], (core_send, core_recv), k, (other, col))
        )
    for copy in across:
        copy.wait_send()
    for copy in between:
        copy.wait()


def spread(value, collective_id):
    rows, cols = lax.axis_size("row"), lax.axis_size("col")
    count, width = value.shape
    part = count // cols
    dma = pltpu.SemaphoreType.DMA
    out = pl.pallas_call(
        functools.partial(spread_kernel, rows, cols),
        out_shape=jax.ShapeDtypeStruct((rows, cols, part, width), value.dtype),
        in_specs=[pl.BlockSpec(memory_space=pltpu.VMEM)],
        out_specs=pl.BlockSpec(memory_space=pltpu.VMEM),
        scratch_shapes=[pltpu.VMEM((cols - 1, part, width), value.dtype)]
        + [dma((cols - 1,))] * 4
        + [dma((rows // 2 - 1,))] * 2
        + [dma((rows // 2,))] * 2,
        compiler_params=pltpu.CompilerParams(
            collective_id=collective_id, has_side_effects=True, vmem_limit_bytes=VMEM_LIMIT
        ),
    )(value.reshape(cols, part, width))
    return out.reshape(rows * count, width)


def fold_kernel(
    rows, cols, x_ref, out_ref, from_core, to_row, from_row, mine, landed, core_send, core_recv,
    row_send, row_recv, part_send, part_recv, col_send, col_recv,
):
    row, col = lax.axis_index("row"), lax.axis_index("col")
    half = rows // 2
    core = row % 2
    other = row // 2 * 2 + 1 - core
    col_peers = [(row, (col + k) % cols) for k in range(1, cols)]
    row_peers = [((row + 2 * k) % rows, col) for k in range(1, half)]
    greet(col_peers + row_peers + [(other, col)])
    between = [
        push(
            x_ref.at[(row + 2 * k) % rows // 2 * 2 + 1 - core],
            from_core.at[k],
            (core_send, core_recv),
            k,
            (other, col),
        )
        for k in [*range(1, half), 0]
    ]
    across = []
    for k in range(1, half):
        between[k - 1].wait_recv()
        to_row[k - 1] = (
            x_ref[(row + 2 * k) % rows].astype(jnp.float32) + from_core[k].astype(jnp.float32)
        ).astype(to_row.dtype)
        across.append(
            push(to_row.at[k - 1], from_row.at[k - 1], (row_send, row_recv), k - 1, row_peers[k - 1])
        )
    between[half - 1].wait_recv()
    total = x_ref[row].astype(jnp.float32) + from_core[0].astype(jnp.float32)
    for k in range(half - 1):
        across[k].wait_recv()
        total = total + from_row[k].astype(jnp.float32)
    mine[...] = total.astype(mine.dtype)
    copies = [
        push(mine.at[(col + k + 1) % cols], landed.at[k], (part_send, part_recv), k, peer)
        for k, peer in enumerate(col_peers)
    ]
    for copy in copies:
        copy.wait()
    part = mine[col].astype(jnp.float32)
    for k in range(cols - 1):
        part = part + landed[k].astype(jnp.float32)
    out_ref[col] = part.astype(out_ref.dtype)
    copies = [
        push(out_ref.at[col], out_ref.at[col], (col_send, col_recv), k, peer)
        for k, peer in enumerate(col_peers)
    ]
    for copy in copies:
        copy.wait()
    for copy in between + across:
        copy.wait_send()


def fold(value, collective_id):
    rows, cols = lax.axis_size("row"), lax.axis_size("col")
    count, width = value.shape[0] // rows, value.shape[1]
    part = count // cols
    half = rows // 2
    dma = pltpu.SemaphoreType.DMA
    block = (cols, part, width)
    out = pl.pallas_call(
        functools.partial(fold_kernel, rows, cols),
        out_shape=jax.ShapeDtypeStruct(block, value.dtype),
        in_specs=[pl.BlockSpec(memory_space=pltpu.VMEM)],
        out_specs=pl.BlockSpec(memory_space=pltpu.VMEM),
        scratch_shapes=[
            pltpu.VMEM((half, *block), value.dtype),
            pltpu.VMEM((half - 1, *block), value.dtype),
            pltpu.VMEM((half - 1, *block), value.dtype),
            pltpu.VMEM(block, value.dtype),
            pltpu.VMEM((cols - 1, part, width), value.dtype),
        ]
        + [dma((half,))] * 2
        + [dma((half - 1,))] * 2
        + [dma((cols - 1,))] * 4,
        compiler_params=pltpu.CompilerParams(
            collective_id=collective_id, has_side_effects=True, vmem_limit_bytes=VMEM_LIMIT
        ),
    )(value.reshape(rows, *block))
    return out.reshape(count, width)


def line_peers(row, col, cols):
    return [(row, (col + 1) % cols), (row, (col + cols - 1) % cols)]


def line_ways(place):
    row, col, cols = place
    return ((0, col), (1, cols - 1 - col))


def line_copy(place, down, source, target, sems, at, step):
    row, col, cols = place
    slot = at + down * (cols - 1) + step
    return pltpu.make_async_remote_copy(
        src_ref=source,
        dst_ref=target,
        send_sem=sems.at[0, slot],
        recv_sem=sems.at[1, slot],
        device_id=(row, (col + (cols - 1 if down else 1)) % cols),
        device_id_type=MESH,
    )


def line_sum(place, term, work, inbox, at, sems, sem_at, result):
    row, col, cols = place

    def block_of(down, step):
        return jnp.clip(step - (cols - 1 - col) if down else cols - 1 - step + col, 0, cols - 1)

    def copy_of(down, step):
        landing = inbox.at[at + down * (cols - 1) + step]
        return line_copy(place, down, work.at[block_of(down, step)], landing, sems, sem_at, step)

    for step in range(cols - 1):
        for down, index in line_ways(place):
            d = block_of(down, step)

            @pl.when(index == 0)
            def _(d=d, down=down, step=step):
                if term is not None:
                    work[d] = term(d)
                copy_of(down, step).start()

            if step > 0:
                @pl.when((index > 0) & (index <= step))
                def _(d=d, down=down, step=step):
                    copy_of(down, step - 1).wait_recv()
                    arrived = inbox[at + down * (cols - 1) + step - 1]
                    own = work[d] if term is None else term(d)
                    work[d] = (own.astype(jnp.float32) + arrived.astype(jnp.float32)).astype(work.dtype)
                    copy_of(down, step).start()

        yield
    own = work[col] if term is None else term(col)
    result[...] = own.astype(result.dtype)
    for down, index in line_ways(place):
        @pl.when(index > 0)
        def _(down=down):
            copy_of(down, cols - 2).wait_recv()
            arrived = inbox[at + down * (cols - 1) + cols - 2]
            result[...] = (result[...].astype(jnp.float32) + arrived.astype(jnp.float32)).astype(result.dtype)

    for step in range(cols - 1):
        for down, index in line_ways(place):
            @pl.when(index <= step)
            def _(down=down, step=step):
                copy_of(down, step).wait_send()


def line_spread(place, block, sems, sem_at):
    row, col, cols = place

    def copy_of(down, step):
        lies = block(jnp.clip(col + step if down else col - step, 0, cols - 1))
        return line_copy(place, down, lies, lies, sems, sem_at, step)

    for step in range(cols):
        if step > 0:
            for down, index in line_ways(place):
                @pl.when(index >= step)
                def _(down=down, step=step):
                    copy_of(down, step - 1).wait_recv()

        if step < cols - 1:
            for down, index in line_ways(place):
                @pl.when((index >= step) & (index < cols - 1))
                def _(down=down, step=step):
                    copy_of(down, step).start()

            yield
    for step in range(cols - 1):
        for down, index in line_ways(place):
            @pl.when((index >= step) & (index < cols - 1))
            def _(down=down, step=step):
                copy_of(down, step).wait_send()


def swap_go(place, part_of, lies_at, sems, local_sem):
    row, col, rows, cols = place
    own = pltpu.make_async_copy(part_of(row), lies_at(row), local_sem)
    own.start()
    copies = [
        push(part_of((row + k) % rows), lies_at(row), (sems.at[0], sems.at[1]), k - 1, ((row + k) % rows, col))
        for k in range(1, rows)
    ]
    yield
    yield
    own.wait()
    for copy in copies:
        copy.wait()


class Matrix:
    def __init__(self, place, grad, basis, refs, adds_weight):
        self.row, self.col, self.rows, self.cols = place
        self.grad, self.basis = grad, basis
        (
            self.mean, self.square, self.weight, self.left,
            self.moment, self.scale, self.next,
            self.work, self.inbox, self.sum, self.total, self.whole, self.sems, self.row_sems, self.core_sems,
        ) = refs
        self.adds_weight = adds_weight

    def go(self):
        line = (self.row, self.col, self.cols)
        links = 2 * (self.cols - 1)
        yield from line_sum(
            line, lambda d: self.grad(d)[...], self.work, self.inbox, 0, self.sems, 0, self.sum
        )
        for d in range(self.cols):
            self.work[d] = jnp.dot(
                self.sum[...], self.basis(d), preferred_element_type=jnp.float32
            ).astype(self.work.dtype)
        yield from line_sum(line, None, self.work, self.inbox, links, self.sems, links, self.total)
        rotated = self.total[...]
        moment = MOMENT_BETA * self.mean[...] + (1.0 - MOMENT_BETA) * rotated
        scale = MOMENT_BETA * self.square[...] + (1.0 - MOMENT_BETA) * rotated * rotated
        self.moment[...] = moment
        self.scale[...] = scale
        steps = self.inbox
        steps[self.col] = (moment / (jnp.sqrt(scale) + ADAM_EPSILON)).astype(steps.dtype)
        yield from line_spread(line, lambda d: steps.at[d], self.sems, 2 * links)
        back = None
        for d in range(self.cols):
            term = lax.dot_general(
                steps[d], self.basis(d), (((1,), (1,)), ((), ())), preferred_element_type=jnp.float32
            )
            back = term if back is None else back + term
        self.whole[self.row] = back.astype(self.whole.dtype)
        half = self.rows // 2
        other = (self.row // 2 * 2 + 1 - self.row % 2, self.col)
        own = self.whole.at[self.row]
        across = [
            push(own, own, (self.row_sems.at[0], self.row_sems.at[1]), k - 1, peer)
            for k, peer in enumerate(same_core(self.row, self.col, self.rows), 1)
        ]
        core_sems = (self.core_sems.at[0], self.core_sems.at[1])
        between = [push(own, own, core_sems, 0, other)]
        yield
        for k in range(1, half):
            across[k - 1].wait_recv()
            block = self.whole.at[(self.row + self.rows - 2 * k) % self.rows]
            between.append(push(block, block, core_sems, k, other))
        yield
        for copy in between:
            copy.wait_recv()
        depth, count = self.weight.shape
        everything = self.whole[...].reshape(self.rows * depth, count)
        update = jnp.dot(self.left[...], everything, preferred_element_type=jnp.float32)
        weight = self.weight[...]
        change = -(SOAP_RATE * (update + WEIGHT_DECAY * weight))
        self.next[...] = weight + change if self.adds_weight else change
        for copy in across + between:
            copy.wait_send()


def same_core(row, col, rows):
    return [((row + 2 * k) % rows, col) for k in range(1, rows // 2)]


def soap_kernel(rows, cols, adds, streamed, *refs):
    row, col = lax.axis_index("row"), lax.axis_index("col")
    place = (row, col, rows, cols)
    greet(line_peers(row, col, cols) + [((row + k) % rows, col) for k in range(1, rows)])
    count = len(adds)

    def take(number):
        nonlocal refs
        first, refs = refs[:number], refs[number:]
        return first

    shared = 1 if streamed else count
    grads, bases, kept, lefts = take(shared), take(shared), take(3 * shared), take(count)
    others_in = take(3)
    made = take(3 * shared)
    others_out = take(3 if streamed else 1)
    scratch = take(8 * count)
    running, loads = [], []
    for m, add in enumerate(adds):
        if streamed:
            grad, basis = grads[0], bases[0]
            own = (*(ref.at[m] for ref in kept), lefts[m], *(ref.at[m] for ref in made))
            held, stage, load_sems = refs[:3]
            width = kept[0].shape[2]

            def grad_of(d, m=m):
                at = pl.multiple_of((streamed.index(m) * cols + d) * width, width)
                return grad.at[:, pl.ds(at, width)]

            def basis_of(d, m=m):
                return held[m, d]

            for e in range(cols):
                for part in range(2):
                    lines = pl.ds(part * (width // 2), width // 2)
                    copy = pltpu.make_async_copy(
                        basis.at[m, lines, pl.ds(e * width, width)], stage.at[part], load_sems.at[part]
                    )
                    loads.append((copy, part, m, e))
        else:
            own = (*kept[3 * m : 3 * m + 3], lefts[m], *made[3 * m : 3 * m + 3])

            def grad_of(d, grad=grads[m]):
                return grad.at[d]

            def basis_of(d, basis=bases[m]):
                return basis[d]

        refs_of = (*own, *scratch[8 * m : 8 * m + 8])
        running.append(Matrix(place, grad_of, basis_of, refs_of, add).go())
    beside = []
    if streamed:
        running = [running[m] for m in streamed]
        loads = [load for m in streamed for load in loads if load[2] == m]
        for copy, *unused in loads[:2]:
            copy.start()
        parts, landed = others_in[1], others_out[1]
        span = parts.shape[2]

        def lies_at(k):
            return landed.at[:, pl.ds(pl.multiple_of(k * span, span), span)]

        beside = [
            swap_go(place, lambda k: parts.at[k], lies_at, *refs[3:5]),
            reach_go(place, others_in[0], others_out[0], *refs[5:7]),
            share_go(place, others_in[2], others_out[2], *refs[7:]),
        ]
    else:
        beside = [scatter_go(place, *others_in, *others_out)]
    for m in running + beside:
        next(m)
    for k, (copy, slot, m, e) in enumerate(loads):
        copy.wait()
        lines = pl.ds(slot * stage.shape[1], stage.shape[1])
        held[m, e, lines] = stage[slot].astype(held.dtype)
        if k + 2 < len(loads):
            loads[k + 2][0].start()
    turn = 0
    while running or beside:
        left = []
        for k, m in running if turn else list(enumerate(running)):
            if turn < SKEW * k or next(m, "done") != "done":
                left.append((k, m))
        running = left
        beside = [m for m in beside if next(m, "done") != "done"]
        turn += 1


def soap(grads, bases, kept, lefts, adds, streamed, others, collective_id):
    rows, cols = lax.axis_size("row"), lax.axis_size("col")
    dma = pltpu.SemaphoreType.DMA
    vmem, anywhere = pl.BlockSpec(memory_space=pltpu.VMEM), pl.BlockSpec(memory_space=pl.ANY)
    low = lefts[0].dtype
    scratch = []
    outs = [jax.ShapeDtypeStruct(array.shape, jnp.float32) for array in kept]
    for m in range(len(adds)):
        block = kept[0].shape[1:] if streamed else kept[3 * m].shape
        scratch += [
            pltpu.VMEM((cols, *block), low),
            pltpu.VMEM((4 * (cols - 1), *block), low),
            pltpu.VMEM(block, low),
            pltpu.VMEM(block, jnp.float32),
            pltpu.VMEM((rows, *block), low),
            dma((2, 6 * (cols - 1))),
            dma((2, rows // 2 - 1)),
            dma((2, rows // 2)),
        ]
    specs = [vmem] * len(grads)
    specs += [anywhere if streamed else vmem] * len(bases)
    specs += [vmem] * (len(kept) + len(lefts))
    if streamed:
        width = kept[0].shape[2]
        grad, parts, own = others
        specs += [vmem] * 3
        outs += [
            jax.ShapeDtypeStruct((cols, *grad.shape), grad.dtype),
            jax.ShapeDtypeStruct((parts.shape[1], parts.shape[0] * parts.shape[2]), parts.dtype),
            jax.ShapeDtypeStruct((rows, cols, *own.shape), own.dtype),
        ]
        scratch += [
            pltpu.VMEM((len(adds), cols, width, width), low),
            pltpu.VMEM((2, width // 2, width), jnp.float32),
            dma((2,)),
            dma((2, rows - 1)),
            dma,
            *[dma((2, 2 * (cols - 1))), dma((2, rows - 1))] * 2,
        ]
    else:
        specs += [vmem] * 3
        outs += [jax.ShapeDtypeStruct(others[2].shape, jnp.float32)]
    return pl.pallas_call(
        functools.partial(soap_kernel, rows, cols, adds, streamed),
        out_shape=outs,
        in_specs=specs,
        out_specs=[vmem] * len(outs),
        scratch_shapes=scratch,
        compiler_params=pltpu.CompilerParams(
            collective_id=collective_id, has_side_effects=True, vmem_limit_bytes=SOAP_VMEM
        ),
    )(*grads, *bases, *kept, *lefts, *others)


def mask_bias(places_ref, keys, tokens):
    key = lax.broadcasted_iota(jnp.int32, (keys, tokens), 0)
    token = lax.broadcasted_iota(jnp.int32, (keys, tokens), 1) + places_ref[0]
    return jnp.where((key <= token) | (key < places_ref[1]), 0.0, MASK_VALUE)


def matmul_nt(left_op, right_op):
    return lax.dot_general(
        left_op, right_op, (((1,), (1,)), ((), ())), preferred_element_type=jnp.float32
    )


def matmul_tn(left_op, right_op):
    return lax.dot_general(
        left_op, right_op, (((0,), (0,)), ((), ())), preferred_element_type=jnp.float32
    )


def halves_swapped(values):
    lane = lax.broadcasted_iota(jnp.int32, values.shape, 1)
    half = HEAD // 2
    later = pltpu.roll(values, 2 * HEAD - half, 1)
    return jnp.where(lane % HEAD < half, later, pltpu.roll(values, half, 1))


def attend_kernel(
    group, places_ref, raw_ref, key_ref, value_ref, cosine_ref, sine_ref, out_ref, total_ref, query_ref, bias
):
    keys, tokens = bias.shape
    for first in range(0, raw_ref.shape[1], 2 * HEAD):
        raw = raw_ref[:, first : first + 2 * HEAD].astype(jnp.float32)
        turned = raw * cosine_ref[...] + halves_swapped(raw) * sine_ref[...]
        query_ref[:, first : first + 2 * HEAD] = turned.astype(query_ref.dtype)

    @pl.when(pl.program_id(0) == 0)
    def _():
        bias[...] = mask_bias(places_ref, keys, tokens)

    for k in range(key_ref.shape[1] // HEAD):
        key = key_ref[:, k * HEAD : (k + 1) * HEAD]
        value = value_ref[:, k * HEAD : (k + 1) * HEAD]
        for h in range(k * group, (k + 1) * group):
            query = query_ref[:, h * HEAD : (h + 1) * HEAD]
            scores = matmul_nt(key, query) * HEAD**-0.5 + bias[...]
            largest = jnp.max(scores, axis=0, keepdims=True)
            weights = jnp.exp(scores - largest)
            total = jnp.sum(weights, axis=0, keepdims=True)
            probs = (weights * (1.0 / total)).astype(query.dtype)
            out = matmul_tn(value, probs)
            out_ref[:, h * HEAD : (h + 1) * HEAD] = out.T.astype(out_ref.dtype)
            total_ref[0, h : h + 1, :] = largest + jnp.log(total)


def attend_back_kernel(
    group, places_ref, query_ref, key_ref, value_ref, cosine_ref, sine_ref, total_ref, grad_ref,
    query_out, pair_out, bias, turned
):
    keys, tokens = bias.shape

    @pl.when(pl.program_id(0) == 0)
    def _():
        bias[...] = mask_bias(places_ref, keys, tokens)

    for k in range(key_ref.shape[1] // HEAD):
        lanes = slice(k * HEAD, (k + 1) * HEAD)
        key, value = key_ref[:, lanes], value_ref[:, lanes]
        grad_key = grad_value = None
        for h in range(k * group, (k + 1) * group):
            query = query_ref[:, h * HEAD : (h + 1) * HEAD]
            grad = grad_ref[:, h * HEAD : (h + 1) * HEAD]
            scores = matmul_nt(key, query) * HEAD**-0.5 + bias[...]
            probs = jnp.exp(scores - total_ref[0, h : h + 1, :])
            grad_probs = matmul_nt(value, grad)
            inner_sum = jnp.sum(probs * grad_probs, axis=0, keepdims=True)
            grad_scores = (probs * (grad_probs - inner_sum)).astype(query.dtype)
            out = matmul_tn(key, grad_scores) * HEAD**-0.5
            turned[:, h * HEAD : (h + 1) * HEAD] = out.T
            key_term = jnp.dot(grad_scores, query, preferred_element_type=jnp.float32)
            value_term = jnp.dot(
                probs.astype(query.dtype), grad, preferred_element_type=jnp.float32
            )
            grad_key = key_term if grad_key is None else grad_key + key_term
            grad_value = value_term if grad_value is None else grad_value + value_term
        pair_out[0, :, lanes] = (grad_key * HEAD**-0.5).astype(pair_out.dtype)
        pair_out[1, :, lanes] = grad_value.astype(pair_out.dtype)
    for first in range(0, turned.shape[1], 2 * HEAD):
        grad = turned[:, first : first + 2 * HEAD]
        raw = grad * cosine_ref[...] - halves_swapped(grad) * sine_ref[...]
        query_out[:, first : first + 2 * HEAD] = raw.astype(query_out.dtype)


def attention_call(kernel, places, queries, pairs, waves, extra, extra_specs, outs, out_specs, scratch):
    tokens, keys = queries.shape[0], pairs.shape[0]
    steps = KV_HEADS // 2
    group = Q_HEADS // KV_HEADS
    wide = 2 * group * HEAD
    return pl.pallas_call(
        functools.partial(kernel, group),
        grid=(steps,),
        in_specs=[
            pl.BlockSpec(memory_space=pltpu.SMEM),
            pl.BlockSpec((tokens, wide), lambda g: (0, g)),
            pl.BlockSpec((keys, 2 * HEAD), lambda g: (0, g)),
            pl.BlockSpec((keys, 2 * HEAD), lambda g: (0, steps + g)),
            *[pl.BlockSpec((tokens, 2 * HEAD), lambda g: (0, 0))] * 2,
            *extra_specs,
        ],
        out_shape=outs,
        out_specs=out_specs,
        scratch_shapes=[pltpu.VMEM((keys, tokens), jnp.float32), *scratch],
        compiler_params=pltpu.CompilerParams(vmem_limit_bytes=VMEM_LIMIT),
        cost_estimate=pl.CostEstimate(
            flops=8 * Q_HEADS * tokens * keys * HEAD,
            bytes_accessed=8 * keys * Q_HEADS * HEAD,
            transcendentals=Q_HEADS * tokens * keys,
        ),
    )(places, queries, pairs, pairs, *waves, *extra)


def attend(places, raw, pairs, waves):
    tokens, width = raw.shape[0], Q_HEADS * HEAD
    steps = KV_HEADS // 2
    heads = Q_HEADS // steps
    return attention_call(
        attend_kernel, places, raw, pairs, waves, [], [],
        [
            jax.ShapeDtypeStruct((tokens, width), raw.dtype),
            jax.ShapeDtypeStruct((steps, heads, tokens), jnp.float32),
            jax.ShapeDtypeStruct((tokens, width), raw.dtype),
        ],
        [
            pl.BlockSpec((tokens, width // steps), lambda g: (0, g)),
            pl.BlockSpec((1, heads, tokens), lambda g: (g, 0, 0)),
            pl.BlockSpec((tokens, width // steps), lambda g: (0, g)),
        ],
        [],
    )


def attend_back(places, queries, pairs, waves, totals, grad):
    tokens, width = queries.shape
    steps = KV_HEADS // 2
    wide = pl.BlockSpec((tokens, width // steps), lambda g: (0, g))
    keys, pair_width = pairs.shape
    return attention_call(
        attend_back_kernel, places, queries, pairs, waves, [totals, grad],
        [pl.BlockSpec((1, Q_HEADS // steps, tokens), lambda g: (g, 0, 0)), wide],
        [
            jax.ShapeDtypeStruct((tokens, width), queries.dtype),
            jax.ShapeDtypeStruct((2, keys, pair_width // 2), queries.dtype),
        ],
        [wide, pl.BlockSpec((2, keys, 2 * HEAD), lambda g: (0, 0, g))],
        [pltpu.VMEM((tokens, width // steps), jnp.float32)],
    )


def outer_kernel(values_ref, left_ref, other_ref, *refs):
    out_ref, turned = refs[-2:]

    @pl.when(pl.program_id(0) == 0)
    def _():
        turned[...] = jnp.dot(
            values_ref[...], left_ref[...], preferred_element_type=jnp.float32
        ).T.astype(turned.dtype)

    out_ref[...] = jnp.dot(
        turned[...], other_ref[...], preferred_element_type=jnp.float32
    ).astype(out_ref.dtype)


def outer(values, left_full, basis, other, block, total, at, buffer):
    tokens, width = values.shape
    specs = [
        pl.BlockSpec((tokens, width), lambda j: (0, 0)),
        pl.BlockSpec((width, width), lambda j: (0, basis)),
        pl.BlockSpec((tokens, block), lambda j: (0, j)),
    ]
    operands = [values, left_full, other]
    aliases = {}
    if buffer is not None:
        specs.append(pl.BlockSpec(memory_space=pl.ANY))
        operands.append(buffer)
        aliases = {3: 0}
    return pl.pallas_call(
        outer_kernel,
        grid=(other.shape[1] // block,),
        out_shape=jax.ShapeDtypeStruct((width, total), values.dtype),
        in_specs=specs,
        out_specs=pl.BlockSpec((width, block), lambda j: (0, at + j)),
        scratch_shapes=[pltpu.VMEM((width, tokens), values.dtype)],
        input_output_aliases=aliases,
        compiler_params=pltpu.CompilerParams(vmem_limit_bytes=VMEM_LIMIT),
        cost_estimate=pl.CostEstimate(
            flops=2 * tokens * width * (width + other.shape[1]),
            bytes_accessed=2 * width * (width + other.shape[1] + tokens),
            transcendentals=0,
        ),
    )(*operands)


def one_hot_tile(ids, first, count):
    columns = lax.broadcasted_iota(jnp.int32, (ids.shape[0], count), 1)
    return jnp.where(ids - first == columns, 1.0, 0.0).astype(jnp.bfloat16)


def line_up_kernel(rows, cols, *refs):
    row, col = lax.axis_index("row"), lax.axis_index("col")
    count = (len(refs) - 8) // 3
    blocks, ids_ref, table_ref = refs[:count], refs[count], refs[count + 1]
    wholes, all_ref, swapped_ref = refs[count + 2 : 2 * count + 2], refs[2 * count + 2], refs[2 * count + 3]
    row_sems, local_sems, swap_sems, swap_local = refs[2 * count + 4 : 2 * count + 8]
    greet(line_peers(row, col, cols) + [((row + k) % rows, col) for k in range(1, rows)])
    all_ref[row] = ids_ref[...]
    copies = [
        push(all_ref.at[row], all_ref.at[row], (row_sems.at[0], row_sems.at[1]), k - 1, ((row + k) % rows, col))
        for k in range(1, rows)
    ]
    running = []
    for k, (block, whole) in enumerate(zip(blocks, wholes, strict=True)):
        width = block.shape[1]

        def lies_at(d, whole=whole, width=width):
            return whole.at[:, pl.ds(pl.multiple_of(d * width, width), width)]

        own = pltpu.make_async_copy(block, lies_at(col), local_sems.at[k])
        own.start()
        own.wait()
        running.append(line_spread((row, col, cols), lies_at, refs[2 * count + 8 + k], 0))
    span = swapped_ref.shape[2]

    def part_of(k):
        return table_ref.at[:, pl.ds(pl.multiple_of(k * span, span), span)]

    place = (row, col, rows, cols)
    running.append(swap_go(place, part_of, lambda k: swapped_ref.at[k], swap_sems, swap_local))
    while running:
        running = [m for m in running if next(m, "done") != "done"]
    for copy in copies:
        copy.wait()


def line_up(blocks, ids, table, collective_id):
    rows, cols = lax.axis_size("row"), lax.axis_size("col")
    dma = pltpu.SemaphoreType.DMA
    vmem = pl.BlockSpec(memory_space=pltpu.VMEM)
    return pl.pallas_call(
        functools.partial(line_up_kernel, rows, cols),
        out_shape=[
            jax.ShapeDtypeStruct((block.shape[0], cols * block.shape[1]), block.dtype)
            for block in blocks
        ]
        + [
            jax.ShapeDtypeStruct((rows, *ids.shape), ids.dtype),
            jax.ShapeDtypeStruct((rows, table.shape[0], table.shape[1] // rows), table.dtype),
        ],
        in_specs=[vmem] * (len(blocks) + 2),
        out_specs=[vmem] * (len(blocks) + 2),
        scratch_shapes=[dma((2, rows - 1)), dma((len(blocks),)), dma((2, rows - 1)), dma]
        + [dma((2, 2 * (cols - 1)))] * len(blocks),
        compiler_params=pltpu.CompilerParams(
            collective_id=collective_id, has_side_effects=True, vmem_limit_bytes=VMEM_LIMIT
        ),
    )(*blocks, ids, table)


def lookup_kernel(
    rows, cols, ids_ref, table_ref, out_ref,
    table, taken, found, inbox, summed_ref, sems, row_sems,
):
    row, col = lax.axis_index("row"), lax.axis_index("col")
    row_peers = [((row + k) % rows, col) for k in range(1, rows)]
    line = (row, col, cols)
    greet(line_peers(row, col, cols) + row_peers)
    features, tokens = out_ref.shape[1:]
    planes = [(k, min(128, features - 128 * k)) for k in range(table.shape[1])]

    def turn(v, carry):
        first = pl.multiple_of(v * 128, 128)
        entries = table_ref[:, pl.ds(first, 128)].astype(jnp.float32).T
        for k, lanes in planes:
            table[pl.ds(first, 128), k, pl.ds(0, lanes)] = entries[:, 128 * k : 128 * k + lanes]
        return carry

    lax.fori_loop(0, table_ref.shape[1] // 128, turn, 0)

    def look(e):
        source = e * rows

        def block(k, carry):
            start = (source + k) * tokens

            def some(j, carry):
                for u in range(LOOK_STEP):
                    at = j * LOOK_STEP + u
                    taken[at] = table[ids_ref[start + at]]
                return carry

            lax.fori_loop(0, tokens // LOOK_STEP, some, 0)
            for p, lanes in planes:
                found[e, k, pl.ds(128 * p, lanes), :] = taken[:, p, :].T[:lanes].astype(found.dtype)
            return carry

        lax.fori_loop(0, rows, block, 0)

    orders = [sorted(range(cols), key=lambda d, i=i: -abs(d - i)) for i in range(cols)]
    summing = line_sum(line, None, found, inbox, 0, sems, 0, summed_ref)
    for k in range(cols - 1):
        e = jnp.int32(orders[0][k])
        for i in range(1, cols):
            e = jnp.where(col == i, orders[i][k], e)
        look(e)
        next(summing)
    look(col)
    for unused in summing:
        pass
    out_ref[row] = summed_ref[row]
    copies = [
        push(summed_ref.at[peer[0]], out_ref.at[row], (row_sems.at[0], row_sems.at[1]), k, peer)
        for k, peer in enumerate(row_peers)
    ]
    for copy in copies:
        copy.wait()


def lookup(ids, table, tokens, collective_id):
    rows, cols = lax.axis_size("row"), lax.axis_size("col")
    features, count = table.shape
    planes = -(-features // 128)
    dma = pltpu.SemaphoreType.DMA
    vmem = pl.BlockSpec(memory_space=pltpu.VMEM)
    block = (rows, features, tokens)
    return pl.pallas_call(
        functools.partial(lookup_kernel, rows, cols),
        out_shape=jax.ShapeDtypeStruct(block, table.dtype),
        in_specs=[pl.BlockSpec(memory_space=pltpu.SMEM), vmem],
        out_specs=vmem,
        scratch_shapes=[
            pltpu.VMEM((count, planes, 128), jnp.float32),
            pltpu.VMEM((tokens, planes, 128), jnp.float32),
            pltpu.VMEM((cols, *block), table.dtype),
            pltpu.VMEM((2 * (cols - 1), *block), table.dtype),
            pltpu.VMEM(block, table.dtype),
            dma((2, 2 * (cols - 1))),
            dma((2, rows - 1)),
        ],
        compiler_params=pltpu.CompilerParams(
            collective_id=collective_id, has_side_effects=True, vmem_limit_bytes=VMEM_LIMIT
        ),
    )(ids, table)


def reach_go(place, grad_ref, held, sems, row_sems):
    row, col, rows, cols = place
    row_peers = [((row + k) % rows, col) for k in range(1, rows)]
    held[col, row] = grad_ref[row]
    started = [
        push(grad_ref.at[peer[0]], held.at[col, row], (row_sems.at[0], row_sems.at[1]), k, peer)
        for k, peer in enumerate(row_peers)
    ]
    yield
    for copy in started:
        copy.wait_recv()
    yield from line_spread((row, col, cols), lambda d: held.at[d], sems, 0)
    for copy in started:
        copy.wait_send()


def scatter_go(place, ids_ref, held_ref, base_ref, out_ref):
    row, col, rows, cols = place
    tiles = out_ref.shape[1] // VOCAB_TILE

    def tile_of(d, source_ref):
        def tile(v, carry):
            first = pl.multiple_of(v * VOCAB_TILE, VOCAB_TILE)
            total = source_ref[:, pl.ds(first, VOCAB_TILE)].astype(jnp.float32)
            for k in range(rows):
                total = total + lax.dot_general(
                    held_ref[d, k],
                    one_hot_tile(ids_ref[d, k], first, VOCAB_TILE),
                    (((1,), (0,)), ((), ())),
                    preferred_element_type=jnp.float32,
                )
            out_ref[:, pl.ds(first, VOCAB_TILE)] = total
            return carry

        return tile

    yield
    for d in range(cols):
        for first in range(0, tiles, TILES_AT_ONCE):
            last = min(tiles, first + TILES_AT_ONCE)
            lax.fori_loop(first, last, tile_of(d, out_ref if d else base_ref), 0)
            yield


def share_go(place, x_ref, out_ref, sems, row_sems):
    row, col, rows, cols = place
    out_ref[row, col] = x_ref[...]
    yield from line_spread((row, col, cols), lambda d: out_ref.at[row, d], sems, 0)
    copies = [
        push(out_ref.at[row], out_ref.at[row], (row_sems.at[0], row_sems.at[1]), k - 1, ((row + k) % rows, col))
        for k in range(1, rows)
    ]
    yield
    for copy in copies:
        copy.wait()


def gather_kernel(rows, cols, x_ref, out_ref, sems):
    row, col = lax.axis_index("row"), lax.axis_index("col")
    greet(line_peers(row, col, cols))
    out_ref[col] = x_ref[...]
    for unused in line_spread((row, col, cols), lambda d: out_ref.at[d], sems, 0):
        pass


def gather(value, collective_id):
    rows, cols = lax.axis_size("row"), lax.axis_size("col")
    vmem = pl.BlockSpec(memory_space=pltpu.VMEM)
    return pl.pallas_call(
        functools.partial(gather_kernel, rows, cols),
        out_shape=jax.ShapeDtypeStruct((cols, *value.shape), value.dtype),
        in_specs=[vmem],
        out_specs=vmem,
        scratch_shapes=[pltpu.SemaphoreType.DMA((2, 2 * (cols - 1)))],
        compiler_params=pltpu.CompilerParams(
            collective_id=collective_id, has_side_effects=True, vmem_limit_bytes=VMEM_LIMIT
        ),
    )(value)


def send(value, axis, shift):
    count = lax.axis_size(axis)
    return lax.ppermute(value, axis, [(k, (k + shift) % count) for k in range(count)])


def collect(value, axis):
    return [value] + [send(value, axis, k) for k in range(1, lax.axis_size(axis))]


def deliver(pieces, axis, sign):
    return [pieces[0]] + [send(pieces[k], axis, sign * k) for k in range(1, len(pieces))]


def summed(pieces):
    total = pieces[0].astype(jnp.float32)
    for piece in pieces[1:]:
        total = total + piece.astype(jnp.float32)
    return total


def to_absolute(pieces, index):
    count = len(pieces)
    order = [pieces[0]] + [pieces[count - k] for k in range(1, count)]
    return jnp.roll(jnp.stack(order), index, axis=0)


def pick_block(values, index, axis):
    return lax.dynamic_index_in_dim(values, index, axis, keepdims=False)


def rms_norm(values, gain_vec):
    return (
        values
        * lax.rsqrt(jnp.mean(values * values, axis=-1, keepdims=True) + NORM_EPSILON)
        * gain_vec
    )


def rotary(values, positions):
    half_width = values.shape[-1] // 2
    frequency = jnp.power(10000.0, -jnp.arange(half_width, dtype=jnp.float32) / half_width)
    angles = positions[:, None].astype(jnp.float32) * frequency[None, :]
    cosine = jnp.cos(angles)[:, None, :]
    sine_part = jnp.sin(angles)[:, None, :]
    first_half = values[..., :half_width]
    second_half = values[..., half_width:]
    return jnp.concatenate(
        [
            first_half * cosine - second_half * sine_part,
            second_half * cosine + first_half * sine_part,
        ],
        axis=-1,
    )


def swiglu(gate_part, upward):
    return jax.nn.silu(gate_part) * upward


def matmul(left_op, right_op):
    return jnp.dot(left_op, right_op, preferred_element_type=jnp.float32)


def matmul_last(left_op, right_op):
    return lax.dot_general(
        left_op, right_op, (((1,), (1,)), ((), ())), preferred_element_type=jnp.float32
    )


def matmul_first(left_op, right_op):
    return lax.dot_general(
        left_op, right_op, (((0,), (0,)), ((), ())), preferred_element_type=jnp.float32
    )


def norm_back(values, gain_vec, grad_output):
    unused, pull_back = jax.vjp(rms_norm, values, gain_vec)
    return pull_back(grad_output)


def adam_update(weight, gradient_value, moment, square_avg, decay_rate):
    moment_new = MOMENT_BETA * moment + (1.0 - MOMENT_BETA) * gradient_value
    square_new = MOMENT_BETA * square_avg + (1.0 - MOMENT_BETA) * gradient_value * gradient_value
    change = -(
        ADAM_RATE * (moment_new / (jnp.sqrt(square_new) + ADAM_EPSILON) + decay_rate * weight)
    )
    return (change, moment_new, square_new)


def per_device(
    token_ids,
    target_ids,
    loss_slots,
    valid_mask,
    prefix_lens,
    embed_table,
    norm_gains,
    qkv_weight,
    output_weight,
    mlp_weight,
    embed_mean,
    embed_square,
    gain_mean,
    gain_square,
    qkv_mean,
    qkv_square,
    out_mean,
    out_square,
    mlp_mean,
    mlp_square,
    left_bases,
    qkv_bases,
    out_bases,
    feedforward_bases,
):
    row_index = lax.axis_index("row")
    col_index = lax.axis_index("col")
    row_count = lax.axis_size("row")
    col_count = lax.axis_size("col")
    low = jnp.bfloat16
    group_tokens = token_ids.shape[0]
    pick_count = loss_slots.shape[0]
    device_tokens = group_tokens // col_count
    vocab_shard, features = embed_table.shape
    width = features * row_count
    query_width = Q_HEADS * HEAD
    kv_width = KV_HEADS * HEAD
    qkv_cols, out_cols, ff_cols = qkv_weight.shape[1], output_weight.shape[1], mlp_weight.shape[2]
    vocab_part = -(-(vocab_shard + 1) // (128 * row_count)) * 128
    vocab_room = vocab_part * row_count

    low_weights = [weight.astype(low) for weight in (qkv_weight, output_weight, *mlp_weight)]
    own_ids = jnp.concatenate([token_ids, target_ids]).reshape(-1, 128)
    table_low_t = embed_table.astype(low).T
    padded = jnp.pad(table_low_t, ((0, 0), (0, vocab_room - vocab_shard)))
    attn_line, mlp_line, ids_all, table_part = line_up(
        [jnp.concatenate(low_weights[:2], axis=1), jnp.concatenate(low_weights[2:], axis=1)],
        own_ids,
        padded,
        6,
    )
    ids_all = ids_all.reshape(row_count, group_tokens + pick_count)
    tokens_all = ids_all[:, :group_tokens].reshape(row_count, col_count, device_tokens)
    targets_all = ids_all[:, group_tokens:].reshape(row_count * pick_count)
    local_tokens = jnp.moveaxis(tokens_all, 1, 0) - col_index * vocab_shard
    inside = (local_tokens >= 0) & (local_tokens < vocab_shard)
    local_tokens = jnp.where(inside, local_tokens, vocab_shard)

    qkv_width, ff_width = qkv_cols * col_count, ff_cols * col_count
    attn_full = lax.all_gather(attn_line, "row", axis=0, tiled=True)
    mlp_line, ids_line = lax.optimization_barrier((mlp_line, local_tokens))
    mlp_full = lax.all_gather(mlp_line, "row", axis=0, tiled=True)
    bases_low = left_bases.astype(low)
    left_block = jnp.concatenate([bases_low[k] for k in range(5)], axis=1)

    def column_blocks(values, first, count):
        span = values.shape[1] // col_count
        return [
            values[:, c * span + first : c * span + first + count] for c in range(col_count)
        ]

    qkv_full = column_blocks(attn_full, 0, qkv_cols)
    out_full = column_blocks(attn_full, qkv_cols, out_cols)
    gate_full, up_full, down_full = (
        column_blocks(mlp_full, k * ff_cols, ff_cols) for k in range(3)
    )

    def by_columns(values, weights, multiply):
        return jnp.concatenate([multiply(values, weight) for weight in weights], axis=1)

    def over_columns(values, weights):
        count = values.shape[1] // col_count
        terms = [
            matmul_last(values[:, c * count : (c + 1) * count], weight)
            for c, weight in enumerate(weights)
        ]
        return functools.reduce(jnp.add, terms)


    def reduce_rows(values):
        return lax.psum_scatter(values, "row", scatter_dimension=0, tiled=True)

    found = lookup(local_tokens.reshape(-1), padded, device_tokens, 7)
    embedded = found.reshape(width, device_tokens).T.astype(jnp.float32)

    normed = rms_norm(embedded, norm_gains[0]).astype(low)
    project = by_columns(normed, qkv_full, matmul).astype(low)
    first_token = col_index * device_tokens
    positions = first_token + jnp.arange(device_tokens, dtype=jnp.int32)
    seq_prefix = jnp.sum(
        jnp.where(jnp.arange(prefix_lens.shape[0], dtype=jnp.int32) == row_index, prefix_lens, 0)
    )

    def rotate_here(values):
        return rotary(values, positions)

    keys_raw = (
        project[:, query_width : query_width + kv_width]
        .astype(jnp.float32)
        .reshape(device_tokens, KV_HEADS, HEAD)
    )
    keys_local = rotate_here(keys_raw).astype(low).reshape(device_tokens, kv_width)
    own_pairs = jnp.concatenate([keys_local, project[:, query_width + kv_width :]], axis=1)
    keys_values = gather(own_pairs, 8)
    left_block, keys_values = lax.optimization_barrier((left_block, keys_values))
    left_full = lax.all_gather(left_block, "row", axis=0, tiled=True)
    keys_values = keys_values.reshape(LEN, 2 * kv_width)
    table_part = table_part.reshape(width, vocab_part)
    places = jnp.stack([first_token, seq_prefix])
    frequency = jnp.power(10000.0, -jnp.arange(HEAD // 2, dtype=jnp.float32) / (HEAD // 2))
    angles = positions[:, None].astype(jnp.float32) * frequency[None, :]
    sine = jnp.sin(angles)
    waves = [
        jnp.tile(jnp.cos(angles), (1, 4)),
        jnp.tile(jnp.concatenate([-sine, sine], axis=1), (1, 2)),
    ]
    attended, totals, queries = attend(places, project, keys_values, waves)
    hidden_one = embedded + over_columns(attended, out_full)
    middle = rms_norm(hidden_one, norm_gains[1]).astype(low)
    gate_part = by_columns(middle, gate_full, matmul)
    upward = by_columns(middle, up_full, matmul)
    inner_act = swiglu(gate_part, upward).astype(low)
    hidden_two = hidden_one + over_columns(inner_act, down_full)
    final = rms_norm(hidden_two, norm_gains[2]).astype(low)

    pick_hit = (loss_slots[:, None] == positions[None, :]).astype(low)
    final_here = matmul(pick_hit, final).astype(low)
    final_pick = spread(final_here, 0)
    logits = matmul(final_pick, table_part)
    part_line = jnp.arange(vocab_part, dtype=jnp.int32)
    real = part_line < vocab_shard - row_index * vocab_part
    logits = jnp.where(real[None, :], logits, MASK_VALUE)
    local_max = jnp.max(logits, axis=-1)
    local_sum = jnp.sum(jnp.exp(logits - local_max[:, None]), axis=-1)
    part_first = col_index * vocab_shard + row_index * vocab_part
    target_hit = (part_line[None, :] == (targets_all - part_first)[:, None]) & real[None, :]
    local_target = jnp.sum(jnp.where(target_hit, logits, 0.0), axis=-1)
    own_stats = jnp.stack([local_max, local_sum, local_target]).reshape(-1, 128)
    everyone = share(own_stats, 1).reshape(row_count * col_count, 3, row_count * pick_count)
    top = jnp.max(everyone[:, 0], axis=0)
    log_total = top + jnp.log(jnp.sum(everyone[:, 1] * jnp.exp(everyone[:, 0] - top), axis=0))
    target_logit = jnp.sum(everyone[:, 2], axis=0)
    valid_count = jnp.maximum(jnp.sum(valid_mask).astype(jnp.float32), 1.0)
    row_weights = valid_mask.astype(jnp.float32) / valid_count
    loss_value = jnp.sum(row_weights * (log_total - target_logit))
    grad_logits = (
        (jnp.exp(logits - log_total[:, None]) - target_hit.astype(jnp.float32))
        * row_weights[:, None]
    ).astype(low)
    grad_pick = matmul_last(grad_logits, table_part).astype(low)
    grad_seq = fold(grad_pick, 2)
    grad_final = matmul_first(pick_hit, grad_seq)

    table_grad_part = matmul_first(final_pick, grad_logits).astype(low)
    grad_parts = table_grad_part.reshape(row_count, features, vocab_part)

    grad_two, gain_two = norm_back(hidden_two, norm_gains[2], grad_final)
    grad_two_low = grad_two.astype(low)
    ff_blocks = ff_width // ff_cols
    mlp_grad = outer(grad_two_low, left_full, 4, inner_act, ff_cols, 3 * ff_width, 0, None)
    grad_inner = by_columns(grad_two_low, down_full, matmul)
    unused, pull_swiglu = jax.vjp(swiglu, gate_part, upward)
    grad_gate, grad_up = pull_swiglu(grad_inner)
    grad_gate = grad_gate.astype(low)
    grad_up = grad_up.astype(low)
    mlp_grad = outer(middle, left_full, 2, grad_gate, ff_cols, 3 * ff_width, ff_blocks, mlp_grad)
    mlp_grad = outer(middle, left_full, 3, grad_up, ff_cols, 3 * ff_width, 2 * ff_blocks, mlp_grad)
    grad_gate, grad_up, mlp_grad = lax.optimization_barrier((grad_gate, grad_up, mlp_grad))
    mlp_rows = reduce_rows(mlp_grad)
    grad_middle = over_columns(grad_gate, gate_full) + over_columns(grad_up, up_full)
    grad_middle_in, gain_one = norm_back(hidden_one, norm_gains[1], grad_middle)
    grad_one = grad_two + grad_middle_in
    grad_one_low = grad_one.astype(low)
    attn_width = query_width + qkv_width
    attn_grad = outer(
        grad_one_low, left_full, 1, attended, SMALL_BLOCK, attn_width, 0, None
    )
    grad_attended = by_columns(grad_one_low, out_full, matmul).astype(low)
    grad_query_raw, grad_pairs = attend_back(
        places, queries, keys_values, waves, totals, grad_attended
    )
    grad_pairs = grad_pairs.reshape(2, col_count, device_tokens, kv_width)
    pair_pieces = [
        pick_block(grad_pairs, (col_index + col_count - k) % col_count, 1) for k in range(col_count)
    ]
    grad_pairs = summed(deliver(pair_pieces, "col", -1))
    unused, pull_key = jax.vjp(rotate_here, keys_raw)
    grad_key_raw = pull_key(grad_pairs[0].reshape(device_tokens, KV_HEADS, HEAD))[0]
    grad_project = jnp.concatenate(
        [
            grad_query_raw,
            grad_key_raw.reshape(device_tokens, kv_width).astype(low),
            grad_pairs[1].astype(low),
        ],
        axis=1,
    )
    attn_grad = outer(
        normed, left_full, 0, grad_project, SMALL_BLOCK, attn_width,
        query_width // SMALL_BLOCK, attn_grad,
    )
    grad_normed = over_columns(grad_project, qkv_full)
    grad_embed_in, gain_zero = norm_back(embedded, norm_gains[0], grad_normed)
    grad_embedded = (grad_one + grad_embed_in).astype(low)
    own_gains = jnp.stack([gain_zero, gain_one, gain_two]).reshape(-1, 128)
    by_feature = grad_embedded.T.reshape(row_count, features, device_tokens)
    mlp_mean_later, by_feature, attn_grad = lax.optimization_barrier((mlp_mean, by_feature, attn_grad))
    attn_rows = reduce_rows(attn_grad)
    mlp_moment, mlp_scale, mlp_next, token_grads, table_base, all_gains = soap(
        [mlp_rows],
        [feedforward_bases],
        [mlp_mean_later, mlp_square, mlp_weight],
        [bases_low[2 + j] for j in range(3)],
        (True, True, True),
        (2, 0, 1),
        (by_feature, grad_parts, own_gains),
        4,
    )
    attn_rows, mlp_next = lax.optimization_barrier((attn_rows, mlp_next))

    def blocks(values):
        return jnp.moveaxis(values.reshape(values.shape[0], col_count, -1), 1, 0)

    out_moment, out_scale, out_update, qkv_moment, qkv_scale, qkv_next, table_grad = soap(
        [blocks(attn_rows[:, :query_width]), blocks(attn_rows[:, query_width:])],
        [blocks(out_bases.astype(low)), blocks(qkv_bases.astype(low))],
        [out_mean, out_square, output_weight, qkv_mean, qkv_square, qkv_weight],
        [bases_low[1], bases_low[0]],
        (False, True),
        (),
        (local_tokens[:, :, :, None], token_grads, table_base),
        5,
    )
    table_grad = table_grad[:, :vocab_shard]
    gain_grads = jnp.sum(all_gains.reshape(row_count * col_count, 3, width), axis=0)
    embed_change, embed_moment, embed_scale = adam_update(
        embed_table, table_grad.T, embed_mean, embed_square, WEIGHT_DECAY
    )
    embed_next = embed_table + embed_change
    gain_update, gain_moment, gain_scale = adam_update(
        norm_gains, gain_grads, gain_mean, gain_square, 0.0
    )
    return (
        loss_value,
        embed_next,
        embed_moment,
        embed_scale,
        gain_update,
        gain_moment,
        gain_scale,
        qkv_next,
        qkv_moment,
        qkv_scale,
        out_update,
        out_moment,
        out_scale,
        mlp_next,
        mlp_moment,
        mlp_scale,
    )


def solution(mesh):
    placed = (
        P("row"),
        P("row"),
        P("row"),
        P(),
        P(),
        P("col", "row"),
        P(),
        P("row", "col"),
        P("row", "col"),
        P(None, "row", "col"),
        P("col", "row"),
        P("col", "row"),
        P(),
        P(),
        P("row", "col"),
        P("row", "col"),
        P("row", "col"),
        P("row", "col"),
        P(None, "row", "col"),
        P(None, "row", "col"),
        P(None, "row", None),
        P("col", None),
        P("col", None),
        P(None, "col", None),
    )
    return jax.shard_map(
        per_device,
        mesh=mesh,
        in_specs=placed,
        out_specs=(
            P(),
            P("col", "row"),
            P("col", "row"),
            P("col", "row"),
            P(),
            P(),
            P(),
            P("row", "col"),
            P("row", "col"),
            P("row", "col"),
            P("row", "col"),
            P("row", "col"),
            P("row", "col"),
            P(None, "row", "col"),
            P(None, "row", "col"),
            P(None, "row", "col"),
        ),
        check_vma=False,
    )
```

```python
import functools

import jax
import jax.numpy as jnp
from jax import lax
from jax.experimental import pallas as pl
from jax.experimental.pallas import tpu as pltpu
from jax.sharding import PartitionSpec as P

Q_HEADS = 18
KV_HEADS = 6
HEAD = 64
LEN = 1024
PICK = 128


NORM_EPSILON = 1e-05
ADAM_EPSILON = 1e-08
MOMENT_BETA = 0.5
SOAP_RATE = 0.05
ADAM_RATE = 0.01
WEIGHT_DECAY = 0.1
MASK_VALUE = -1e30
MESH = pl.DeviceIdType.MESH
VMEM_LIMIT = 58 * 2**20
VOCAB_TILE = 1024
LOOK_STEP = 64
TILES_AT_ONCE = 3
SKEW = 2
SOAP_VMEM = 62 * 2**20
SMALL_BLOCK = 384


def greet(peers):
    barrier = pltpu.get_barrier_semaphore()
    for peer in peers:
        pl.semaphore_signal(barrier, inc=1, device_id=peer, device_id_type=MESH)
    pl.semaphore_wait(barrier, len(peers))


def push(source, target, sems, slot, peer):
    copy = pltpu.make_async_remote_copy(
        src_ref=source,
        dst_ref=target,
        send_sem=sems[0].at[slot],
        recv_sem=sems[1].at[slot],
        device_id=peer,
        device_id_type=MESH,
    )
    copy.start()
    return copy


def row_peer(row, col, rows, k):
    half = rows // 2
    if k < half:
        return ((row + 2 * k) % rows, col)
    return ((row // 2 * 2 + 2 * (k - half)) % rows + 1 - row % 2, col)


def share_kernel(rows, cols, x_ref, out_ref, col_send, col_recv, row_send, row_recv):
    row, col = lax.axis_index("row"), lax.axis_index("col")
    col_peers = [(row, (col + k) % cols) for k in range(1, cols)]
    row_peers = [((row + k) % rows, col) for k in range(1, rows)]
    greet(col_peers + row_peers)
    out_ref[row, col] = x_ref[...]
    copies = [
        push(out_ref.at[row, col], out_ref.at[row, col], (col_send, col_recv), k, peer)
        for k, peer in enumerate(col_peers)
    ]
    for copy in copies:
        copy.wait()
    copies = [
        push(out_ref.at[row], out_ref.at[row], (row_send, row_recv), k, peer)
        for k, peer in enumerate(row_peers)
    ]
    for copy in copies:
        copy.wait()


def share(value, collective_id):
    rows, cols = lax.axis_size("row"), lax.axis_size("col")
    return pl.pallas_call(
        functools.partial(share_kernel, rows, cols),
        out_shape=jax.ShapeDtypeStruct((rows, cols, *value.shape), value.dtype),
        in_specs=[pl.BlockSpec(memory_space=pltpu.VMEM)],
        out_specs=pl.BlockSpec(memory_space=pltpu.VMEM),
        scratch_shapes=[
            pltpu.SemaphoreType.DMA((cols - 1,)),
            pltpu.SemaphoreType.DMA((cols - 1,)),
            pltpu.SemaphoreType.DMA((rows - 1,)),
            pltpu.SemaphoreType.DMA((rows - 1,)),
        ],
        compiler_params=pltpu.CompilerParams(
            collective_id=collective_id, has_side_effects=True, vmem_limit_bytes=VMEM_LIMIT
        ),
    )(value)


def spread_kernel(
    rows, cols, x_ref, out_ref, landed, part_send, part_recv, col_send, col_recv,
    row_send, row_recv, core_send, core_recv,
):
    row, col = lax.axis_index("row"), lax.axis_index("col")
    half = rows // 2
    other = row // 2 * 2 + 1 - row % 2
    col_peers = [(row, (col + k) % cols) for k in range(1, cols)]
    row_peers = [((row + 2 * k) % rows, col) for k in range(1, half)]
    greet(col_peers + row_peers + [(other, col)])
    copies = [
        push(x_ref.at[(col + k + 1) % cols], landed.at[k], (part_send, part_recv), k, peer)
        for k, peer in enumerate(col_peers)
    ]
    for copy in copies:
        copy.wait()
    total = x_ref[col].astype(jnp.float32)
    for k in range(cols - 1):
        total = total + landed[k].astype(jnp.float32)
    out_ref[row, col] = total.astype(out_ref.dtype)
    copies = [
        push(out_ref.at[row, col], out_ref.at[row, col], (col_send, col_recv), k, peer)
        for k, peer in enumerate(col_peers)
    ]
    for copy in copies:
        copy.wait()
    across = [
        push(out_ref.at[row], out_ref.at[row], (row_send, row_recv), k, peer)
        for k, peer in enumerate(row_peers)
    ]
    between = [push(out_ref.at[row], out_ref.at[row], (core_send, core_recv), 0, (other, col))]
    for k in range(1, half):
        across[k - 1].wait_recv()
        source = (row + rows - 2 * k) % rows
        between.append(
            push(out_ref.at[source], out_ref.at[source], (core_send, core_recv), k, (other, col))
        )
    for copy in across:
        copy.wait_send()
    for copy in between:
        copy.wait()


def spread(value, collective_id):
    rows, cols = lax.axis_size("row"), lax.axis_size("col")
    count, width = value.shape
    part = count // cols
    dma = pltpu.SemaphoreType.DMA
    out = pl.pallas_call(
        functools.partial(spread_kernel, rows, cols),
        out_shape=jax.ShapeDtypeStruct((rows, cols, part, width), value.dtype),
        in_specs=[pl.BlockSpec(memory_space=pltpu.VMEM)],
        out_specs=pl.BlockSpec(memory_space=pltpu.VMEM),
        scratch_shapes=[pltpu.VMEM((cols - 1, part, width), value.dtype)]
        + [dma((cols - 1,))] * 4
        + [dma((rows // 2 - 1,))] * 2
        + [dma((rows // 2,))] * 2,
        compiler_params=pltpu.CompilerParams(
            collective_id=collective_id, has_side_effects=True, vmem_limit_bytes=VMEM_LIMIT
        ),
    )(value.reshape(cols, part, width))
    return out.reshape(rows * count, width)


def fold_kernel(
    rows, cols, x_ref, out_ref, from_core, to_row, from_row, mine, landed, core_send, core_recv,
    row_send, row_recv, part_send, part_recv, col_send, col_recv,
):
    row, col = lax.axis_index("row"), lax.axis_index("col")
    half = rows // 2
    core = row % 2
    other = row // 2 * 2 + 1 - core
    col_peers = [(row, (col + k) % cols) for k in range(1, cols)]
    row_peers = [((row + 2 * k) % rows, col) for k in range(1, half)]
    greet(col_peers + row_peers + [(other, col)])
    between = [
        push(
            x_ref.at[(row + 2 * k) % rows // 2 * 2 + 1 - core],
            from_core.at[k],
            (core_send, core_recv),
            k,
            (other, col),
        )
        for k in [*range(1, half), 0]
    ]
    across = []
    for k in range(1, half):
        between[k - 1].wait_recv()
        to_row[k - 1] = (
            x_ref[(row + 2 * k) % rows].astype(jnp.float32) + from_core[k].astype(jnp.float32)
        ).astype(to_row.dtype)
        across.append(
            push(to_row.at[k - 1], from_row.at[k - 1], (row_send, row_recv), k - 1, row_peers[k - 1])
        )
    between[half - 1].wait_recv()
    total = x_ref[row].astype(jnp.float32) + from_core[0].astype(jnp.float32)
    for k in range(half - 1):
        across[k].wait_recv()
        total = total + from_row[k].astype(jnp.float32)
    mine[...] = total.astype(mine.dtype)
    copies = [
        push(mine.at[(col + k + 1) % cols], landed.at[k], (part_send, part_recv), k, peer)
        for k, peer in enumerate(col_peers)
    ]
    for copy in copies:
        copy.wait()
    part = mine[col].astype(jnp.float32)
    for k in range(cols - 1):
        part = part + landed[k].astype(jnp.float32)
    out_ref[col] = part.astype(out_ref.dtype)
    copies = [
        push(out_ref.at[col], out_ref.at[col], (col_send, col_recv), k, peer)
        for k, peer in enumerate(col_peers)
    ]
    for copy in copies:
        copy.wait()
    for copy in between + across:
        copy.wait_send()


def fold(value, collective_id):
    rows, cols = lax.axis_size("row"), lax.axis_size("col")
    count, width = value.shape[0] // rows, value.shape[1]
    part = count // cols
    half = rows // 2
    dma = pltpu.SemaphoreType.DMA
    block = (cols, part, width)
    out = pl.pallas_call(
        functools.partial(fold_kernel, rows, cols),
        out_shape=jax.ShapeDtypeStruct(block, value.dtype),
        in_specs=[pl.BlockSpec(memory_space=pltpu.VMEM)],
        out_specs=pl.BlockSpec(memory_space=pltpu.VMEM),
        scratch_shapes=[
            pltpu.VMEM((half, *block), value.dtype),
            pltpu.VMEM((half - 1, *block), value.dtype),
            pltpu.VMEM((half - 1, *block), value.dtype),
            pltpu.VMEM(block, value.dtype),
            pltpu.VMEM((cols - 1, part, width), value.dtype),
        ]
        + [dma((half,))] * 2
        + [dma((half - 1,))] * 2
        + [dma((cols - 1,))] * 4,
        compiler_params=pltpu.CompilerParams(
            collective_id=collective_id, has_side_effects=True, vmem_limit_bytes=VMEM_LIMIT
        ),
    )(value.reshape(rows, *block))
    return out.reshape(count, width)


def line_peers(row, col, cols):
    return [(row, (col + 1) % cols), (row, (col + cols - 1) % cols)]


def line_ways(place):
    row, col, cols = place
    return ((0, col), (1, cols - 1 - col))


def line_copy(place, down, source, target, sems, at, step):
    row, col, cols = place
    slot = at + down * (cols - 1) + step
    return pltpu.make_async_remote_copy(
        src_ref=source,
        dst_ref=target,
        send_sem=sems.at[0, slot],
        recv_sem=sems.at[1, slot],
        device_id=(row, (col + (cols - 1 if down else 1)) % cols),
        device_id_type=MESH,
    )


def line_sum(place, term, work, inbox, at, sems, sem_at, result):
    row, col, cols = place

    def block_of(down, step):
        return jnp.clip(step - (cols - 1 - col) if down else cols - 1 - step + col, 0, cols - 1)

    def copy_of(down, step):
        landing = inbox.at[at + down * (cols - 1) + step]
        return line_copy(place, down, work.at[block_of(down, step)], landing, sems, sem_at, step)

    for step in range(cols - 1):
        for down, index in line_ways(place):
            d = block_of(down, step)

            @pl.when(index == 0)
            def _(d=d, down=down, step=step):
                if term is not None:
                    work[d] = term(d)
                copy_of(down, step).start()

            if step > 0:
                @pl.when((index > 0) & (index <= step))
                def _(d=d, down=down, step=step):
                    copy_of(down, step - 1).wait_recv()
                    arrived = inbox[at + down * (cols - 1) + step - 1]
                    own = work[d] if term is None else term(d)
                    work[d] = (own.astype(jnp.float32) + arrived.astype(jnp.float32)).astype(work.dtype)
                    copy_of(down, step).start()

        yield
    own = work[col] if term is None else term(col)
    result[...] = own.astype(result.dtype)
    for down, index in line_ways(place):
        @pl.when(index > 0)
        def _(down=down):
            copy_of(down, cols - 2).wait_recv()
            arrived = inbox[at + down * (cols - 1) + cols - 2]
            result[...] = (result[...].astype(jnp.float32) + arrived.astype(jnp.float32)).astype(result.dtype)

    for step in range(cols - 1):
        for down, index in line_ways(place):
            @pl.when(index <= step)
            def _(down=down, step=step):
                copy_of(down, step).wait_send()


def line_spread(place, block, sems, sem_at):
    row, col, cols = place

    def copy_of(down, step):
        lies = block(jnp.clip(col + step if down else col - step, 0, cols - 1))
        return line_copy(place, down, lies, lies, sems, sem_at, step)

    for step in range(cols):
        if step > 0:
            for down, index in line_ways(place):
                @pl.when(index >= step)
                def _(down=down, step=step):
                    copy_of(down, step - 1).wait_recv()

        if step < cols - 1:
            for down, index in line_ways(place):
                @pl.when((index >= step) & (index < cols - 1))
                def _(down=down, step=step):
                    copy_of(down, step).start()

            yield
    for step in range(cols - 1):
        for down, index in line_ways(place):
            @pl.when((index >= step) & (index < cols - 1))
            def _(down=down, step=step):
                copy_of(down, step).wait_send()


def swap_go(place, part_of, lies_at, sems, local_sem):
    row, col, rows, cols = place
    own = pltpu.make_async_copy(part_of(row), lies_at(row), local_sem)
    own.start()
    copies = [
        push(part_of((row + k) % rows), lies_at(row), (sems.at[0], sems.at[1]), k - 1, ((row + k) % rows, col))
        for k in range(1, rows)
    ]
    yield
    yield
    own.wait()
    for copy in copies:
        copy.wait()


class Matrix:
    def __init__(self, place, grad, basis, refs, adds_weight):
        self.row, self.col, self.rows, self.cols = place
        self.grad, self.basis = grad, basis
        (
            self.mean, self.square, self.weight, self.left,
            self.moment, self.scale, self.next,
            self.work, self.inbox, self.sum, self.total, self.whole, self.sems, self.row_sems, self.core_sems,
        ) = refs
        self.adds_weight = adds_weight

    def go(self):
        line = (self.row, self.col, self.cols)
        links = 2 * (self.cols - 1)
        yield from line_sum(
            line, lambda d: self.grad(d)[...], self.work, self.inbox, 0, self.sems, 0, self.sum
        )
        for d in range(self.cols):
            self.work[d] = jnp.dot(
                self.sum[...], self.basis(d), preferred_element_type=jnp.float32
            ).astype(self.work.dtype)
        yield from line_sum(line, None, self.work, self.inbox, links, self.sems, links, self.total)
        rotated = self.total[...]
        moment = MOMENT_BETA * self.mean[...] + (1.0 - MOMENT_BETA) * rotated
        scale = MOMENT_BETA * self.square[...] + (1.0 - MOMENT_BETA) * rotated * rotated
        self.moment[...] = moment
        self.scale[...] = scale
        steps = self.inbox
        steps[self.col] = (moment / (jnp.sqrt(scale) + ADAM_EPSILON)).astype(steps.dtype)
        yield from line_spread(line, lambda d: steps.at[d], self.sems, 2 * links)
        back = None
        for d in range(self.cols):
            term = lax.dot_general(
                steps[d], self.basis(d), (((1,), (1,)), ((), ())), preferred_element_type=jnp.float32
            )
            back = term if back is None else back + term
        self.whole[self.row] = back.astype(self.whole.dtype)
        half = self.rows // 2
        other = (self.row // 2 * 2 + 1 - self.row % 2, self.col)
        own = self.whole.at[self.row]
        across = [
            push(own, own, (self.row_sems.at[0], self.row_sems.at[1]), k - 1, peer)
            for k, peer in enumerate(same_core(self.row, self.col, self.rows), 1)
        ]
        core_sems = (self.core_sems.at[0], self.core_sems.at[1])
        between = [push(own, own, core_sems, 0, other)]
        yield
        for k in range(1, half):
            across[k - 1].wait_recv()
            block = self.whole.at[(self.row + self.rows - 2 * k) % self.rows]
            between.append(push(block, block, core_sems, k, other))
        yield
        for copy in between:
            copy.wait_recv()
        depth, count = self.weight.shape
        everything = self.whole[...].reshape(self.rows * depth, count)
        update = jnp.dot(self.left[...], everything, preferred_element_type=jnp.float32)
        weight = self.weight[...]
        change = -(SOAP_RATE * (update + WEIGHT_DECAY * weight))
        self.next[...] = weight + change if self.adds_weight else change
        for copy in across + between:
            copy.wait_send()


def same_core(row, col, rows):
    return [((row + 2 * k) % rows, col) for k in range(1, rows // 2)]


def soap_kernel(rows, cols, adds, streamed, *refs):
    row, col = lax.axis_index("row"), lax.axis_index("col")
    place = (row, col, rows, cols)
    greet(line_peers(row, col, cols) + [((row + k) % rows, col) for k in range(1, rows)])
    count = len(adds)

    def take(number):
        nonlocal refs
        first, refs = refs[:number], refs[number:]
        return first

    shared = 1 if streamed else count
    grads, bases, kept, lefts = take(shared), take(shared), take(3 * shared), take(count)
    others_in = take(3)
    made = take(3 * shared)
    others_out = take(3 if streamed else 1)
    scratch = take(8 * count)
    running, loads = [], []
    for m, add in enumerate(adds):
        if streamed:
            grad, basis = grads[0], bases[0]
            own = (*(ref.at[m] for ref in kept), lefts[m], *(ref.at[m] for ref in made))
            held, stage, load_sems = refs[:3]
            width = kept[0].shape[2]

            def grad_of(d, m=m):
                at = pl.multiple_of((streamed.index(m) * cols + d) * width, width)
                return grad.at[:, pl.ds(at, width)]

            def basis_of(d, m=m):
                return held[m, d]

            for e in range(cols):
                for part in range(2):
                    lines = pl.ds(part * (width // 2), width // 2)
                    copy = pltpu.make_async_copy(
                        basis.at[m, lines, pl.ds(e * width, width)], stage.at[part], load_sems.at[part]
                    )
                    loads.append((copy, part, m, e))
        else:
            own = (*kept[3 * m : 3 * m + 3], lefts[m], *made[3 * m : 3 * m + 3])

            def grad_of(d, grad=grads[m]):
                return grad.at[d]

            def basis_of(d, basis=bases[m]):
                return basis[d]

        refs_of = (*own, *scratch[8 * m : 8 * m + 8])
        running.append(Matrix(place, grad_of, basis_of, refs_of, add).go())
    beside = []
    if streamed:
        running = [running[m] for m in streamed]
        loads = [load for m in streamed for load in loads if load[2] == m]
        for copy, *unused in loads[:2]:
            copy.start()
        parts, landed = others_in[1], others_out[1]
        span = parts.shape[2]

        def lies_at(k):
            return landed.at[:, pl.ds(pl.multiple_of(k * span, span), span)]

        beside = [
            swap_go(place, lambda k: parts.at[k], lies_at, *refs[3:5]),
            reach_go(place, others_in[0], others_out[0], *refs[5:7]),
            share_go(place, others_in[2], others_out[2], *refs[7:]),
        ]
    else:
        beside = [scatter_go(place, *others_in, *others_out)]
    for m in running + beside:
        next(m)
    for k, (copy, slot, m, e) in enumerate(loads):
        copy.wait()
        lines = pl.ds(slot * stage.shape[1], stage.shape[1])
        held[m, e, lines] = stage[slot].astype(held.dtype)
        if k + 2 < len(loads):
            loads[k + 2][0].start()
    turn = 0
    while running or beside:
        left = []
        for k, m in running if turn else list(enumerate(running)):
            if turn < SKEW * k or next(m, "done") != "done":
                left.append((k, m))
        running = left
        beside = [m for m in beside if next(m, "done") != "done"]
        turn += 1


def soap(grads, bases, kept, lefts, adds, streamed, others, collective_id):
    rows, cols = lax.axis_size("row"), lax.axis_size("col")
    dma = pltpu.SemaphoreType.DMA
    vmem, anywhere = pl.BlockSpec(memory_space=pltpu.VMEM), pl.BlockSpec(memory_space=pl.ANY)
    low = lefts[0].dtype
    scratch = []
    outs = [jax.ShapeDtypeStruct(array.shape, jnp.float32) for array in kept]
    for m in range(len(adds)):
        block = kept[0].shape[1:] if streamed else kept[3 * m].shape
        scratch += [
            pltpu.VMEM((cols, *block), low),
            pltpu.VMEM((4 * (cols - 1), *block), low),
            pltpu.VMEM(block, low),
            pltpu.VMEM(block, jnp.float32),
            pltpu.VMEM((rows, *block), low),
            dma((2, 6 * (cols - 1))),
            dma((2, rows // 2 - 1)),
            dma((2, rows // 2)),
        ]
    specs = [vmem] * len(grads)
    specs += [anywhere if streamed else vmem] * len(bases)
    specs += [vmem] * (len(kept) + len(lefts))
    if streamed:
        width = kept[0].shape[2]
        grad, parts, own = others
        specs += [vmem] * 3
        outs += [
            jax.ShapeDtypeStruct((cols, *grad.shape), grad.dtype),
            jax.ShapeDtypeStruct((parts.shape[1], parts.shape[0] * parts.shape[2]), parts.dtype),
            jax.ShapeDtypeStruct((rows, cols, *own.shape), own.dtype),
        ]
        scratch += [
            pltpu.VMEM((len(adds), cols, width, width), low),
            pltpu.VMEM((2, width // 2, width), jnp.float32),
            dma((2,)),
            dma((2, rows - 1)),
            dma,
            *[dma((2, 2 * (cols - 1))), dma((2, rows - 1))] * 2,
        ]
    else:
        specs += [vmem] * 3
        outs += [jax.ShapeDtypeStruct(others[2].shape, jnp.float32)]
    return pl.pallas_call(
        functools.partial(soap_kernel, rows, cols, adds, streamed),
        out_shape=outs,
        in_specs=specs,
        out_specs=[vmem] * len(outs),
        scratch_shapes=scratch,
        compiler_params=pltpu.CompilerParams(
            collective_id=collective_id, has_side_effects=True, vmem_limit_bytes=SOAP_VMEM
        ),
    )(*grads, *bases, *kept, *lefts, *others)


def mask_bias(places_ref, keys, tokens):
    key = lax.broadcasted_iota(jnp.int32, (keys, tokens), 0)
    token = lax.broadcasted_iota(jnp.int32, (keys, tokens), 1) + places_ref[0]
    return jnp.where((key <= token) | (key < places_ref[1]), 0.0, MASK_VALUE)


def matmul_nt(left_op, right_op):
    return lax.dot_general(
        left_op, right_op, (((1,), (1,)), ((), ())), preferred_element_type=jnp.float32
    )


def matmul_tn(left_op, right_op):
    return lax.dot_general(
        left_op, right_op, (((0,), (0,)), ((), ())), preferred_element_type=jnp.float32
    )


def halves_swapped(values):
    lane = lax.broadcasted_iota(jnp.int32, values.shape, 1)
    half = HEAD // 2
    later = pltpu.roll(values, 2 * HEAD - half, 1)
    return jnp.where(lane % HEAD < half, later, pltpu.roll(values, half, 1))


def attend_kernel(
    group, places_ref, raw_ref, key_ref, value_ref, cosine_ref, sine_ref, out_ref, total_ref, query_ref, bias
):
    keys, tokens = bias.shape
    for first in range(0, raw_ref.shape[1], 2 * HEAD):
        raw = raw_ref[:, first : first + 2 * HEAD].astype(jnp.float32)
        turned = raw * cosine_ref[...] + halves_swapped(raw) * sine_ref[...]
        query_ref[:, first : first + 2 * HEAD] = turned.astype(query_ref.dtype)

    @pl.when(pl.program_id(0) == 0)
    def _():
        bias[...] = mask_bias(places_ref, keys, tokens)

    for k in range(key_ref.shape[1] // HEAD):
        key = key_ref[:, k * HEAD : (k + 1) * HEAD]
        value = value_ref[:, k * HEAD : (k + 1) * HEAD]
        for h in range(k * group, (k + 1) * group):
            query = query_ref[:, h * HEAD : (h + 1) * HEAD]
            scores = matmul_nt(key, query) * HEAD**-0.5 + bias[...]
            largest = jnp.max(scores, axis=0, keepdims=True)
            weights = jnp.exp(scores - largest)
            total = jnp.sum(weights, axis=0, keepdims=True)
            probs = (weights * (1.0 / total)).astype(query.dtype)
            out = matmul_tn(value, probs)
            out_ref[:, h * HEAD : (h + 1) * HEAD] = out.T.astype(out_ref.dtype)
            total_ref[0, h : h + 1, :] = largest + jnp.log(total)


def attend_back_kernel(
    group, places_ref, query_ref, key_ref, value_ref, cosine_ref, sine_ref, total_ref, grad_ref,
    query_out, pair_out, bias, turned
):
    keys, tokens = bias.shape

    @pl.when(pl.program_id(0) == 0)
    def _():
        bias[...] = mask_bias(places_ref, keys, tokens)

    for k in range(key_ref.shape[1] // HEAD):
        lanes = slice(k * HEAD, (k + 1) * HEAD)
        key, value = key_ref[:, lanes], value_ref[:, lanes]
        grad_key = grad_value = None
        for h in range(k * group, (k + 1) * group):
            query = query_ref[:, h * HEAD : (h + 1) * HEAD]
            grad = grad_ref[:, h * HEAD : (h + 1) * HEAD]
            scores = matmul_nt(key, query) * HEAD**-0.5 + bias[...]
            probs = jnp.exp(scores - total_ref[0, h : h + 1, :])
            grad_probs = matmul_nt(value, grad)
            inner_sum = jnp.sum(probs * grad_probs, axis=0, keepdims=True)
            grad_scores = (probs * (grad_probs - inner_sum)).astype(query.dtype)
            out = matmul_tn(key, grad_scores) * HEAD**-0.5
            turned[:, h * HEAD : (h + 1) * HEAD] = out.T
            key_term = jnp.dot(grad_scores, query, preferred_element_type=jnp.float32)
            value_term = jnp.dot(
                probs.astype(query.dtype), grad, preferred_element_type=jnp.float32
            )
            grad_key = key_term if grad_key is None else grad_key + key_term
            grad_value = value_term if grad_value is None else grad_value + value_term
        pair_out[0, :, lanes] = (grad_key * HEAD**-0.5).astype(pair_out.dtype)
        pair_out[1, :, lanes] = grad_value.astype(pair_out.dtype)
    for first in range(0, turned.shape[1], 2 * HEAD):
        grad = turned[:, first : first + 2 * HEAD]
        raw = grad * cosine_ref[...] - halves_swapped(grad) * sine_ref[...]
        query_out[:, first : first + 2 * HEAD] = raw.astype(query_out.dtype)


def attention_call(kernel, places, queries, pairs, waves, extra, extra_specs, outs, out_specs, scratch):
    tokens, keys = queries.shape[0], pairs.shape[0]
    steps = KV_HEADS // 2
    group = Q_HEADS // KV_HEADS
    wide = 2 * group * HEAD
    return pl.pallas_call(
        functools.partial(kernel, group),
        grid=(steps,),
        in_specs=[
            pl.BlockSpec(memory_space=pltpu.SMEM),
            pl.BlockSpec((tokens, wide), lambda g: (0, g)),
            pl.BlockSpec((keys, 2 * HEAD), lambda g: (0, g)),
            pl.BlockSpec((keys, 2 * HEAD), lambda g: (0, steps + g)),
            *[pl.BlockSpec((tokens, 2 * HEAD), lambda g: (0, 0))] * 2,
            *extra_specs,
        ],
        out_shape=outs,
        out_specs=out_specs,
        scratch_shapes=[pltpu.VMEM((keys, tokens), jnp.float32), *scratch],
        compiler_params=pltpu.CompilerParams(vmem_limit_bytes=VMEM_LIMIT),
        cost_estimate=pl.CostEstimate(
            flops=8 * Q_HEADS * tokens * keys * HEAD,
            bytes_accessed=8 * keys * Q_HEADS * HEAD,
            transcendentals=Q_HEADS * tokens * keys,
        ),
    )(places, queries, pairs, pairs, *waves, *extra)


def attend(places, raw, pairs, waves):
    tokens, width = raw.shape[0], Q_HEADS * HEAD
    steps = KV_HEADS // 2
    heads = Q_HEADS // steps
    return attention_call(
        attend_kernel, places, raw, pairs, waves, [], [],
        [
            jax.ShapeDtypeStruct((tokens, width), raw.dtype),
            jax.ShapeDtypeStruct((steps, heads, tokens), jnp.float32),
            jax.ShapeDtypeStruct((tokens, width), raw.dtype),
        ],
        [
            pl.BlockSpec((tokens, width // steps), lambda g: (0, g)),
            pl.BlockSpec((1, heads, tokens), lambda g: (g, 0, 0)),
            pl.BlockSpec((tokens, width // steps), lambda g: (0, g)),
        ],
        [],
    )


def attend_back(places, queries, pairs, waves, totals, grad):
    tokens, width = queries.shape
    steps = KV_HEADS // 2
    wide = pl.BlockSpec((tokens, width // steps), lambda g: (0, g))
    keys, pair_width = pairs.shape
    return attention_call(
        attend_back_kernel, places, queries, pairs, waves, [totals, grad],
        [pl.BlockSpec((1, Q_HEADS // steps, tokens), lambda g: (g, 0, 0)), wide],
        [
            jax.ShapeDtypeStruct((tokens, width), queries.dtype),
            jax.ShapeDtypeStruct((2, keys, pair_width // 2), queries.dtype),
        ],
        [wide, pl.BlockSpec((2, keys, 2 * HEAD), lambda g: (0, 0, g))],
        [pltpu.VMEM((tokens, width // steps), jnp.float32)],
    )


def outer_kernel(values_ref, left_ref, other_ref, *refs):
    out_ref, turned = refs[-2:]

    @pl.when(pl.program_id(0) == 0)
    def _():
        turned[...] = jnp.dot(
            values_ref[...], left_ref[...], preferred_element_type=jnp.float32
        ).astype(turned.dtype).T

    out_ref[...] = jnp.dot(
        turned[...], other_ref[...], preferred_element_type=jnp.float32
    ).astype(out_ref.dtype)


def outer(values, left_full, basis, other, block, total, at, buffer):
    tokens, width = values.shape
    specs = [
        pl.BlockSpec((tokens, width), lambda j: (0, 0)),
        pl.BlockSpec((width, width), lambda j: (0, basis)),
        pl.BlockSpec((tokens, block), lambda j: (0, j)),
    ]
    operands = [values, left_full, other]
    aliases = {}
    if buffer is not None:
        specs.append(pl.BlockSpec(memory_space=pl.ANY))
        operands.append(buffer)
        aliases = {3: 0}
    return pl.pallas_call(
        outer_kernel,
        grid=(other.shape[1] // block,),
        out_shape=jax.ShapeDtypeStruct((width, total), values.dtype),
        in_specs=specs,
        out_specs=pl.BlockSpec((width, block), lambda j: (0, at + j)),
        scratch_shapes=[pltpu.VMEM((width, tokens), values.dtype)],
        input_output_aliases=aliases,
        compiler_params=pltpu.CompilerParams(vmem_limit_bytes=VMEM_LIMIT),
        cost_estimate=pl.CostEstimate(
            flops=2 * tokens * width * (width + other.shape[1]),
            bytes_accessed=2 * width * (width + other.shape[1] + tokens),
            transcendentals=0,
        ),
    )(*operands)


def one_hot_tile(ids, first, count):
    columns = lax.broadcasted_iota(jnp.int32, (ids.shape[0], count), 1)
    return jnp.where(ids - first == columns, 1.0, 0.0).astype(jnp.bfloat16)


def line_up_kernel(rows, cols, *refs):
    row, col = lax.axis_index("row"), lax.axis_index("col")
    count = (len(refs) - 8) // 3
    blocks, ids_ref, table_ref = refs[:count], refs[count], refs[count + 1]
    wholes, all_ref, swapped_ref = refs[count + 2 : 2 * count + 2], refs[2 * count + 2], refs[2 * count + 3]
    row_sems, local_sems, swap_sems, swap_local = refs[2 * count + 4 : 2 * count + 8]
    greet(line_peers(row, col, cols) + [((row + k) % rows, col) for k in range(1, rows)])
    all_ref[row] = ids_ref[...]
    copies = [
        push(all_ref.at[row], all_ref.at[row], (row_sems.at[0], row_sems.at[1]), k - 1, ((row + k) % rows, col))
        for k in range(1, rows)
    ]
    running = []
    for k, (block, whole) in enumerate(zip(blocks, wholes, strict=True)):
        width = block.shape[1]

        def lies_at(d, whole=whole, width=width):
            return whole.at[:, pl.ds(pl.multiple_of(d * width, width), width)]

        own = pltpu.make_async_copy(block, lies_at(col), local_sems.at[k])
        own.start()
        own.wait()
        running.append(line_spread((row, col, cols), lies_at, refs[2 * count + 8 + k], 0))
    span = swapped_ref.shape[2]

    def part_of(k):
        return table_ref.at[:, pl.ds(pl.multiple_of(k * span, span), span)]

    place = (row, col, rows, cols)
    running.append(swap_go(place, part_of, lambda k: swapped_ref.at[k], swap_sems, swap_local))
    while running:
        running = [m for m in running if next(m, "done") != "done"]
    for copy in copies:
        copy.wait()


def line_up(blocks, ids, table, collective_id):
    rows, cols = lax.axis_size("row"), lax.axis_size("col")
    dma = pltpu.SemaphoreType.DMA
    vmem = pl.BlockSpec(memory_space=pltpu.VMEM)
    return pl.pallas_call(
        functools.partial(line_up_kernel, rows, cols),
        out_shape=[
            jax.ShapeDtypeStruct((block.shape[0], cols * block.shape[1]), block.dtype)
            for block in blocks
        ]
        + [
            jax.ShapeDtypeStruct((rows, *ids.shape), ids.dtype),
            jax.ShapeDtypeStruct((rows, table.shape[0], table.shape[1] // rows), table.dtype),
        ],
        in_specs=[vmem] * (len(blocks) + 2),
        out_specs=[vmem] * (len(blocks) + 2),
        scratch_shapes=[dma((2, rows - 1)), dma((len(blocks),)), dma((2, rows - 1)), dma]
        + [dma((2, 2 * (cols - 1)))] * len(blocks),
        compiler_params=pltpu.CompilerParams(
            collective_id=collective_id, has_side_effects=True, vmem_limit_bytes=VMEM_LIMIT
        ),
    )(*blocks, ids, table)


def lookup_kernel(
    rows, cols, ids_ref, table_ref, out_ref,
    table, taken, found, inbox, summed_ref, sems, row_sems,
):
    row, col = lax.axis_index("row"), lax.axis_index("col")
    row_peers = [((row + k) % rows, col) for k in range(1, rows)]
    line = (row, col, cols)
    greet(line_peers(row, col, cols) + row_peers)
    features, tokens = out_ref.shape[1:]
    planes = [(k, min(128, features - 128 * k)) for k in range(table.shape[1])]

    def turn(v, carry):
        first = pl.multiple_of(v * 128, 128)
        entries = table_ref[:, pl.ds(first, 128)].astype(jnp.float32).T
        for k, lanes in planes:
            table[pl.ds(first, 128), k, pl.ds(0, lanes)] = entries[:, 128 * k : 128 * k + lanes]
        return carry

    lax.fori_loop(0, table_ref.shape[1] // 128, turn, 0)

    def look(e):
        source = e * rows

        def block(k, carry):
            start = (source + k) * tokens

            def some(j, carry):
                for u in range(LOOK_STEP):
                    at = j * LOOK_STEP + u
                    taken[at] = table[ids_ref[start + at]]
                return carry

            lax.fori_loop(0, tokens // LOOK_STEP, some, 0)
            for p, lanes in planes:
                found[e, k, pl.ds(128 * p, lanes), :] = taken[:, p, :].T[:lanes].astype(found.dtype)
            return carry

        lax.fori_loop(0, rows, block, 0)

    orders = [sorted(range(cols), key=lambda d, i=i: -abs(d - i)) for i in range(cols)]
    summing = line_sum(line, None, found, inbox, 0, sems, 0, summed_ref)
    for k in range(cols - 1):
        e = jnp.int32(orders[0][k])
        for i in range(1, cols):
            e = jnp.where(col == i, orders[i][k], e)
        look(e)
        next(summing)
    look(col)
    for unused in summing:
        pass
    out_ref[row] = summed_ref[row]
    copies = [
        push(summed_ref.at[peer[0]], out_ref.at[row], (row_sems.at[0], row_sems.at[1]), k, peer)
        for k, peer in enumerate(row_peers)
    ]
    for copy in copies:
        copy.wait()


def lookup(ids, table, tokens, collective_id):
    rows, cols = lax.axis_size("row"), lax.axis_size("col")
    features, count = table.shape
    planes = -(-features // 128)
    dma = pltpu.SemaphoreType.DMA
    vmem = pl.BlockSpec(memory_space=pltpu.VMEM)
    block = (rows, features, tokens)
    return pl.pallas_call(
        functools.partial(lookup_kernel, rows, cols),
        out_shape=jax.ShapeDtypeStruct(block, table.dtype),
        in_specs=[pl.BlockSpec(memory_space=pltpu.SMEM), vmem],
        out_specs=vmem,
        scratch_shapes=[
            pltpu.VMEM((count, planes, 128), jnp.float32),
            pltpu.VMEM((tokens, planes, 128), jnp.float32),
            pltpu.VMEM((cols, *block), table.dtype),
            pltpu.VMEM((2 * (cols - 1), *block), table.dtype),
            pltpu.VMEM(block, table.dtype),
            dma((2, 2 * (cols - 1))),
            dma((2, rows - 1)),
        ],
        compiler_params=pltpu.CompilerParams(
            collective_id=collective_id, has_side_effects=True, vmem_limit_bytes=VMEM_LIMIT
        ),
    )(ids, table)


def reach_go(place, grad_ref, held, sems, row_sems):
    row, col, rows, cols = place
    row_peers = [((row + k) % rows, col) for k in range(1, rows)]
    held[col, row] = grad_ref[row]
    started = [
        push(grad_ref.at[peer[0]], held.at[col, row], (row_sems.at[0], row_sems.at[1]), k, peer)
        for k, peer in enumerate(row_peers)
    ]
    yield
    for copy in started:
        copy.wait_recv()
    yield from line_spread((row, col, cols), lambda d: held.at[d], sems, 0)
    for copy in started:
        copy.wait_send()


def scatter_go(place, ids_ref, held_ref, base_ref, out_ref):
    row, col, rows, cols = place
    tiles = out_ref.shape[1] // VOCAB_TILE

    def tile_of(d, source_ref):
        def tile(v, carry):
            first = pl.multiple_of(v * VOCAB_TILE, VOCAB_TILE)
            total = source_ref[:, pl.ds(first, VOCAB_TILE)].astype(jnp.float32)
            for k in range(rows):
                total = total + lax.dot_general(
                    held_ref[d, k],
                    one_hot_tile(ids_ref[d, k], first, VOCAB_TILE),
                    (((1,), (0,)), ((), ())),
                    preferred_element_type=jnp.float32,
                )
            out_ref[:, pl.ds(first, VOCAB_TILE)] = total
            return carry

        return tile

    yield
    for d in range(cols):
        for first in range(0, tiles, TILES_AT_ONCE):
            last = min(tiles, first + TILES_AT_ONCE)
            lax.fori_loop(first, last, tile_of(d, out_ref if d else base_ref), 0)
            yield


def share_go(place, x_ref, out_ref, sems, row_sems):
    row, col, rows, cols = place
    out_ref[row, col] = x_ref[...]
    yield from line_spread((row, col, cols), lambda d: out_ref.at[row, d], sems, 0)
    copies = [
        push(out_ref.at[row], out_ref.at[row], (row_sems.at[0], row_sems.at[1]), k - 1, ((row + k) % rows, col))
        for k in range(1, rows)
    ]
    yield
    for copy in copies:
        copy.wait()


def gather_kernel(rows, cols, x_ref, out_ref, sems):
    row, col = lax.axis_index("row"), lax.axis_index("col")
    greet(line_peers(row, col, cols))
    out_ref[col] = x_ref[...]
    for unused in line_spread((row, col, cols), lambda d: out_ref.at[d], sems, 0):
        pass


def gather(value, collective_id):
    rows, cols = lax.axis_size("row"), lax.axis_size("col")
    vmem = pl.BlockSpec(memory_space=pltpu.VMEM)
    return pl.pallas_call(
        functools.partial(gather_kernel, rows, cols),
        out_shape=jax.ShapeDtypeStruct((cols, *value.shape), value.dtype),
        in_specs=[vmem],
        out_specs=vmem,
        scratch_shapes=[pltpu.SemaphoreType.DMA((2, 2 * (cols - 1)))],
        compiler_params=pltpu.CompilerParams(
            collective_id=collective_id, has_side_effects=True, vmem_limit_bytes=VMEM_LIMIT
        ),
    )(value)


def send(value, axis, shift):
    count = lax.axis_size(axis)
    return lax.ppermute(value, axis, [(k, (k + shift) % count) for k in range(count)])


def collect(value, axis):
    return [value] + [send(value, axis, k) for k in range(1, lax.axis_size(axis))]


def deliver(pieces, axis, sign):
    return [pieces[0]] + [send(pieces[k], axis, sign * k) for k in range(1, len(pieces))]


def summed(pieces):
    total = pieces[0].astype(jnp.float32)
    for piece in pieces[1:]:
        total = total + piece.astype(jnp.float32)
    return total


def to_absolute(pieces, index):
    count = len(pieces)
    order = [pieces[0]] + [pieces[count - k] for k in range(1, count)]
    return jnp.roll(jnp.stack(order), index, axis=0)


def pick_block(values, index, axis):
    return lax.dynamic_index_in_dim(values, index, axis, keepdims=False)


def rms_norm(values, gain_vec):
    return (
        values
        * lax.rsqrt(jnp.mean(values * values, axis=-1, keepdims=True) + NORM_EPSILON)
        * gain_vec
    )


def rotary(values, positions):
    half_width = values.shape[-1] // 2
    frequency = jnp.power(10000.0, -jnp.arange(half_width, dtype=jnp.float32) / half_width)
    angles = positions[:, None].astype(jnp.float32) * frequency[None, :]
    cosine = jnp.cos(angles)[:, None, :]
    sine_part = jnp.sin(angles)[:, None, :]
    first_half = values[..., :half_width]
    second_half = values[..., half_width:]
    return jnp.concatenate(
        [
            first_half * cosine - second_half * sine_part,
            second_half * cosine + first_half * sine_part,
        ],
        axis=-1,
    )


def swiglu(gate_part, upward):
    return jax.nn.silu(gate_part) * upward


def matmul(left_op, right_op):
    return jnp.dot(left_op, right_op, preferred_element_type=jnp.float32)


def matmul_last(left_op, right_op):
    return lax.dot_general(
        left_op, right_op, (((1,), (1,)), ((), ())), preferred_element_type=jnp.float32
    )


def matmul_first(left_op, right_op):
    return lax.dot_general(
        left_op, right_op, (((0,), (0,)), ((), ())), preferred_element_type=jnp.float32
    )


def norm_back(values, gain_vec, grad_output):
    unused, pull_back = jax.vjp(rms_norm, values, gain_vec)
    return pull_back(grad_output)


def adam_update(weight, gradient_value, moment, square_avg, decay_rate):
    moment_new = MOMENT_BETA * moment + (1.0 - MOMENT_BETA) * gradient_value
    square_new = MOMENT_BETA * square_avg + (1.0 - MOMENT_BETA) * gradient_value * gradient_value
    change = -(
        ADAM_RATE * (moment_new / (jnp.sqrt(square_new) + ADAM_EPSILON) + decay_rate * weight)
    )
    return (change, moment_new, square_new)


def per_device(
    token_ids,
    target_ids,
    loss_slots,
    valid_mask,
    prefix_lens,
    embed_table,
    norm_gains,
    qkv_weight,
    output_weight,
    mlp_weight,
    embed_mean,
    embed_square,
    gain_mean,
    gain_square,
    qkv_mean,
    qkv_square,
    out_mean,
    out_square,
    mlp_mean,
    mlp_square,
    left_bases,
    qkv_bases,
    out_bases,
    feedforward_bases,
):
    row_index = lax.axis_index("row")
    col_index = lax.axis_index("col")
    row_count = lax.axis_size("row")
    col_count = lax.axis_size("col")
    low = jnp.bfloat16
    group_tokens = token_ids.shape[0]
    pick_count = loss_slots.shape[0]
    device_tokens = group_tokens // col_count
    vocab_shard, features = embed_table.shape
    width = features * row_count
    query_width = Q_HEADS * HEAD
    kv_width = KV_HEADS * HEAD
    qkv_cols, out_cols, ff_cols = qkv_weight.shape[1], output_weight.shape[1], mlp_weight.shape[2]
    vocab_part = -(-(vocab_shard + 1) // (128 * row_count)) * 128
    vocab_room = vocab_part * row_count

    low_weights = [weight.astype(low) for weight in (qkv_weight, output_weight, *mlp_weight)]
    own_ids = jnp.concatenate([token_ids, target_ids]).reshape(-1, 128)
    table_low_t = embed_table.astype(low).T
    padded = jnp.pad(table_low_t, ((0, 0), (0, vocab_room - vocab_shard)))
    attn_line, mlp_line, ids_all, table_part = line_up(
        [jnp.concatenate(low_weights[:2], axis=1), jnp.concatenate(low_weights[2:], axis=1)],
        own_ids,
        padded,
        6,
    )
    ids_all = ids_all.reshape(row_count, group_tokens + pick_count)
    tokens_all = ids_all[:, :group_tokens].reshape(row_count, col_count, device_tokens)
    targets_all = ids_all[:, group_tokens:].reshape(row_count * pick_count)
    local_tokens = jnp.moveaxis(tokens_all, 1, 0) - col_index * vocab_shard
    inside = (local_tokens >= 0) & (local_tokens < vocab_shard)
    local_tokens = jnp.where(inside, local_tokens, vocab_shard)

    qkv_width, ff_width = qkv_cols * col_count, ff_cols * col_count
    attn_full = lax.all_gather(attn_line, "row", axis=0, tiled=True)
    mlp_line, ids_line = lax.optimization_barrier((mlp_line, local_tokens))
    mlp_full = lax.all_gather(mlp_line, "row", axis=0, tiled=True)
    bases_low = left_bases.astype(low)
    left_block = jnp.concatenate([bases_low[k] for k in range(5)], axis=1)

    def column_blocks(values, first, count):
        span = values.shape[1] // col_count
        return [
            values[:, c * span + first : c * span + first + count] for c in range(col_count)
        ]

    qkv_full = column_blocks(attn_full, 0, qkv_cols)
    out_full = column_blocks(attn_full, qkv_cols, out_cols)
    gate_full, up_full, down_full = (
        column_blocks(mlp_full, k * ff_cols, ff_cols) for k in range(3)
    )

    def by_columns(values, weights, multiply):
        return jnp.concatenate([multiply(values, weight) for weight in weights], axis=1)

    def over_columns(values, weights):
        count = values.shape[1] // col_count
        terms = [
            matmul_last(values[:, c * count : (c + 1) * count], weight)
            for c, weight in enumerate(weights)
        ]
        return functools.reduce(jnp.add, terms)


    def reduce_rows(values):
        return lax.psum_scatter(values, "row", scatter_dimension=0, tiled=True)

    found = lookup(local_tokens.reshape(-1), padded, device_tokens, 7)
    embedded = found.reshape(width, device_tokens).T.astype(jnp.float32)

    normed = rms_norm(embedded, norm_gains[0]).astype(low)
    project = by_columns(normed, qkv_full, matmul).astype(low)
    first_token = col_index * device_tokens
    positions = first_token + jnp.arange(device_tokens, dtype=jnp.int32)
    seq_prefix = jnp.sum(
        jnp.where(jnp.arange(prefix_lens.shape[0], dtype=jnp.int32) == row_index, prefix_lens, 0)
    )

    def rotate_here(values):
        return rotary(values, positions)

    keys_raw = (
        project[:, query_width : query_width + kv_width]
        .astype(jnp.float32)
        .reshape(device_tokens, KV_HEADS, HEAD)
    )
    keys_local = rotate_here(keys_raw).astype(low).reshape(device_tokens, kv_width)
    own_pairs = jnp.concatenate([keys_local, project[:, query_width + kv_width :]], axis=1)
    keys_values = gather(own_pairs, 8)
    left_block, keys_values = lax.optimization_barrier((left_block, keys_values))
    left_full = lax.all_gather(left_block, "row", axis=0, tiled=True)
    keys_values = keys_values.reshape(LEN, 2 * kv_width)
    table_part = table_part.reshape(width, vocab_part)
    places = jnp.stack([first_token, seq_prefix])
    frequency = jnp.power(10000.0, -jnp.arange(HEAD // 2, dtype=jnp.float32) / (HEAD // 2))
    angles = positions[:, None].astype(jnp.float32) * frequency[None, :]
    sine = jnp.sin(angles)
    waves = [
        jnp.tile(jnp.cos(angles), (1, 4)),
        jnp.tile(jnp.concatenate([-sine, sine], axis=1), (1, 2)),
    ]
    attended, totals, queries = attend(places, project, keys_values, waves)
    hidden_one = embedded + over_columns(attended, out_full)
    middle = rms_norm(hidden_one, norm_gains[1]).astype(low)
    gate_part = by_columns(middle, gate_full, matmul)
    upward = by_columns(middle, up_full, matmul)
    inner_act = swiglu(gate_part, upward).astype(low)
    hidden_two = hidden_one + over_columns(inner_act, down_full)
    final = rms_norm(hidden_two, norm_gains[2]).astype(low)

    pick_hit = (loss_slots[:, None] == positions[None, :]).astype(low)
    final_here = matmul(pick_hit, final).astype(low)
    final_pick = spread(final_here, 0)
    logits = matmul(final_pick, table_part)
    part_line = jnp.arange(vocab_part, dtype=jnp.int32)
    real = part_line < vocab_shard - row_index * vocab_part
    logits = jnp.where(real[None, :], logits, MASK_VALUE)
    local_max = jnp.max(logits, axis=-1)
    local_sum = jnp.sum(jnp.exp(logits - local_max[:, None]), axis=-1)
    part_first = col_index * vocab_shard + row_index * vocab_part
    target_hit = (part_line[None, :] == (targets_all - part_first)[:, None]) & real[None, :]
    local_target = jnp.sum(jnp.where(target_hit, logits, 0.0), axis=-1)
    own_stats = jnp.stack([local_max, local_sum, local_target]).reshape(-1, 128)
    everyone = share(own_stats, 1).reshape(row_count * col_count, 3, row_count * pick_count)
    top = jnp.max(everyone[:, 0], axis=0)
    log_total = top + jnp.log(jnp.sum(everyone[:, 1] * jnp.exp(everyone[:, 0] - top), axis=0))
    target_logit = jnp.sum(everyone[:, 2], axis=0)
    valid_count = jnp.maximum(jnp.sum(valid_mask).astype(jnp.float32), 1.0)
    row_weights = valid_mask.astype(jnp.float32) / valid_count
    loss_value = jnp.sum(row_weights * (log_total - target_logit))
    grad_logits = (
        (jnp.exp(logits - log_total[:, None]) - target_hit.astype(jnp.float32))
        * row_weights[:, None]
    ).astype(low)
    grad_pick = matmul_last(grad_logits, table_part).astype(low)
    grad_seq = fold(grad_pick, 2)
    grad_final = matmul_first(pick_hit, grad_seq)

    table_grad_part = matmul_first(final_pick, grad_logits).astype(low)
    grad_parts = table_grad_part.reshape(row_count, features, vocab_part)

    grad_two, gain_two = norm_back(hidden_two, norm_gains[2], grad_final)
    grad_two_low = grad_two.astype(low)
    ff_blocks = ff_width // ff_cols
    mlp_grad = outer(grad_two_low, left_full, 4, inner_act, ff_cols, 3 * ff_width, 0, None)
    grad_inner = by_columns(grad_two_low, down_full, matmul)
    unused, pull_swiglu = jax.vjp(swiglu, gate_part, upward)
    grad_gate, grad_up = pull_swiglu(grad_inner)
    grad_gate = grad_gate.astype(low)
    grad_up = grad_up.astype(low)
    mlp_grad = outer(middle, left_full, 2, grad_gate, ff_cols, 3 * ff_width, ff_blocks, mlp_grad)
    mlp_grad = outer(middle, left_full, 3, grad_up, ff_cols, 3 * ff_width, 2 * ff_blocks, mlp_grad)
    grad_gate, grad_up, mlp_grad = lax.optimization_barrier((grad_gate, grad_up, mlp_grad))
    mlp_rows = reduce_rows(mlp_grad)
    grad_middle = over_columns(grad_gate, gate_full) + over_columns(grad_up, up_full)
    grad_middle_in, gain_one = norm_back(hidden_one, norm_gains[1], grad_middle)
    grad_one = grad_two + grad_middle_in
    grad_one_low = grad_one.astype(low)
    attn_width = query_width + qkv_width
    attn_grad = outer(
        grad_one_low, left_full, 1, attended, SMALL_BLOCK, attn_width, 0, None
    )
    grad_attended = by_columns(grad_one_low, out_full, matmul).astype(low)
    grad_query_raw, grad_pairs = attend_back(
        places, queries, keys_values, waves, totals, grad_attended
    )
    grad_pairs = grad_pairs.reshape(2, col_count, device_tokens, kv_width)
    pair_pieces = [
        pick_block(grad_pairs, (col_index + col_count - k) % col_count, 1) for k in range(col_count)
    ]
    grad_pairs = summed(deliver(pair_pieces, "col", -1))
    unused, pull_key = jax.vjp(rotate_here, keys_raw)
    grad_key_raw = pull_key(grad_pairs[0].reshape(device_tokens, KV_HEADS, HEAD))[0]
    grad_project = jnp.concatenate(
        [
            grad_query_raw,
            grad_key_raw.reshape(device_tokens, kv_width).astype(low),
            grad_pairs[1].astype(low),
        ],
        axis=1,
    )
    attn_grad = outer(
        normed, left_full, 0, grad_project, SMALL_BLOCK, attn_width,
        query_width // SMALL_BLOCK, attn_grad,
    )
    grad_normed = over_columns(grad_project, qkv_full)
    grad_embed_in, gain_zero = norm_back(embedded, norm_gains[0], grad_normed)
    grad_embedded = (grad_one + grad_embed_in).astype(low)
    own_gains = jnp.stack([gain_zero, gain_one, gain_two]).reshape(-1, 128)
    by_feature = grad_embedded.T.reshape(row_count, features, device_tokens)
    mlp_mean_later, by_feature, attn_grad = lax.optimization_barrier((mlp_mean, by_feature, attn_grad))
    attn_rows = reduce_rows(attn_grad)
    mlp_moment, mlp_scale, mlp_next, token_grads, table_base, all_gains = soap(
        [mlp_rows],
        [feedforward_bases],
        [mlp_mean_later, mlp_square, mlp_weight],
        [bases_low[2 + j] for j in range(3)],
        (True, True, True),
        (2, 0, 1),
        (by_feature, grad_parts, own_gains),
        4,
    )
    attn_rows, mlp_next = lax.optimization_barrier((attn_rows, mlp_next))

    def blocks(values):
        return jnp.moveaxis(values.reshape(values.shape[0], col_count, -1), 1, 0)

    out_moment, out_scale, out_update, qkv_moment, qkv_scale, qkv_next, table_grad = soap(
        [blocks(attn_rows[:, :query_width]), blocks(attn_rows[:, query_width:])],
        [blocks(out_bases.astype(low)), blocks(qkv_bases.astype(low))],
        [out_mean, out_square, output_weight, qkv_mean, qkv_square, qkv_weight],
        [bases_low[1], bases_low[0]],
        (False, True),
        (),
        (local_tokens[:, :, :, None], token_grads, table_base),
        5,
    )
    table_grad = table_grad[:, :vocab_shard]
    gain_grads = jnp.sum(all_gains.reshape(row_count * col_count, 3, width), axis=0)
    embed_change, embed_moment, embed_scale = adam_update(
        embed_table, table_grad.T, embed_mean, embed_square, WEIGHT_DECAY
    )
    embed_next = embed_table + embed_change
    gain_update, gain_moment, gain_scale = adam_update(
        norm_gains, gain_grads, gain_mean, gain_square, 0.0
    )
    return (
        loss_value,
        embed_next,
        embed_moment,
        embed_scale,
        gain_update,
        gain_moment,
        gain_scale,
        qkv_next,
        qkv_moment,
        qkv_scale,
        out_update,
        out_moment,
        out_scale,
        mlp_next,
        mlp_moment,
        mlp_scale,
    )


def solution(mesh):
    placed = (
        P("row"),
        P("row"),
        P("row"),
        P(),
        P(),
        P("col", "row"),
        P(),
        P("row", "col"),
        P("row", "col"),
        P(None, "row", "col"),
        P("col", "row"),
        P("col", "row"),
        P(),
        P(),
        P("row", "col"),
        P("row", "col"),
        P("row", "col"),
        P("row", "col"),
        P(None, "row", "col"),
        P(None, "row", "col"),
        P(None, "row", None),
        P("col", None),
        P("col", None),
        P(None, "col", None),
    )
    return jax.shard_map(
        per_device,
        mesh=mesh,
        in_specs=placed,
        out_specs=(
            P(),
            P("col", "row"),
            P("col", "row"),
            P("col", "row"),
            P(),
            P(),
            P(),
            P("row", "col"),
            P("row", "col"),
            P("row", "col"),
            P("row", "col"),
            P("row", "col"),
            P("row", "col"),
            P(None, "row", "col"),
            P(None, "row", "col"),
            P(None, "row", "col"),
        ),
        check_vma=False,
    )
```
